32 devices in a mesh: seq: 16 (over z, y, core), mlp: 2 (over x).
Axes of the slice: x: 2, y: 2, z: 4, core: 2. Of those that a mesh axis runs over, the one named last changes fastest.
Arguments:
- inputs: bfloat16 [2048, 768], P('seq'), may hold values from -6 to 6
- segments: int32 [2048], P('seq'), may hold values from 0 to 4, as said below
- picks: int32 [1, 256], replicated, may hold values from 0 to 2047, as said below
- gains: float32 [2, 2, 768], replicated, may hold values from 0.5 to 1.5
- router: float32 [768], replicated, may hold values from -0.21875 to 0.21875
- qkv: bfloat16 [2, 3, 768, 768], P(None, None, None, 'mlp'), may hold values from -0.21875 to 0.21875
- proj_out: bfloat16 [2, 768, 768], P(None, 'mlp'), may hold values from -3 to 3
- up: bfloat16 [2, 768, 3072], P(None, None, 'mlp'), may hold values from -0.21875 to 0.21875
- down: bfloat16 [2, 3072, 768], P(None, 'mlp'), may hold values from -0.109375 to 0.109375
- cotangent: bfloat16 [2048, 768], P('seq'), may hold values from -6 to 6
Outputs:
- routed_out: bfloat16 [2048, 768], P('seq')
- dense_out: bfloat16 [2048, 768], P('seq')
- input_grad: float32 [2048, 768], P('seq')
- gains_grad: float32 [2, 2, 768], P(None, None, 'seq')
- router_grad: float32 [768], P('seq')
- qkv_grad: float32 [2, 3, 768, 768], P(None, None, 'seq', 'mlp')
- proj_out_grad: float32 [2, 768, 768], P(None, 'mlp', 'seq')
- up_grad: float32 [2, 768, 3072], P(None, 'seq', 'mlp')
- down_grad: float32 [2, 3072, 768], P(None, 'mlp', 'seq')
The draws below stay inside these ranges and needn't reach their ends.
Inputs may be any that keep to these rules, and one draw needn't show every extreme that they name: `picks`: each row lists 256 increasing positions of one routing window. Splitting a window into aligned runs of 128 positions, some run of each row holds exactly 128 of them and none holds more. `segments`: document ids never fall along the sequence; every id is used. One document starts within the first 128 tokens and ends within the last 128.
All inputs are finite; a program needn't handle non-finite values.
Results may differ from the reference program's by a relative error of at most 0.018.
Values may be sent and summed in bfloat16 or wider, within the bound.
A program may use at most 128 MiB of HBM per device.

```python
import jax
import jax.numpy as jnp
from jax import lax

D = 768
H = 12
HD = 64
FF = 3072
G = 2048
K_SEL = 256
MOST = 128
TOK_DEV = 128
TOKENS = 2048
GROUPS = 1


def draw_picks(key, part):
    key = jax.random.fold_in(key, 11)
    pieces = G // TOK_DEV

    def one_group(sub):
        hot_key, spread_key, order_key = jax.random.split(sub, 3)
        hottest = jax.random.randint(hot_key, (), 0, pieces)
        extra = (hottest + 1 + jax.random.randint(spread_key, (K_SEL - MOST,), 0, pieces - 1)) % pieces
        counts = jnp.sum((extra[:, None] == jnp.arange(pieces, dtype=jnp.int32)[None, :]).astype(jnp.int32), axis=0)
        counts = counts + MOST * (jnp.arange(pieces, dtype=jnp.int32) == hottest).astype(jnp.int32)
        orders = jax.vmap(lambda sub_key: jax.random.permutation(sub_key, TOK_DEV))(jax.random.split(order_key, pieces))
        taken = (orders < counts[:, None]).reshape(-1)
        places = jnp.arange(G, dtype=jnp.int32)
        ranked = jnp.sort(jnp.where(taken, places, G + places))
        return ranked[:K_SEL]
    return jax.vmap(one_group)(jax.random.split(key, GROUPS)).astype(jnp.int32)


def draw_segments(key, part):
    key = jax.random.fold_in(key, 7)
    keys = jax.random.split(key, 4)
    quarter = TOK_DEV // 4
    step_len = quarter // 4
    places = jnp.arange(TOKENS, dtype=jnp.int32)
    ids = jnp.zeros((TOKENS,), jnp.int32)
    for index in range(4):
        bound = TOKENS - quarter + index * step_len + jax.random.randint(keys[index], (), 0, step_len)
        ids = ids + (places >= bound).astype(jnp.int32)
    return ids.astype(jnp.int32)


def level_of(key, extent, cuts, low, largest):
    factor_of, own = 1.0, jax.random.fold_in(key, 6)
    for axis_at, parts in cuts:
        steps = jnp.exp(jax.random.uniform(jax.random.fold_in(own, axis_at), (parts,), jnp.float32, low / len(cuts), largest / len(cuts)))
        factor_of = factor_of * jnp.repeat(steps, extent[axis_at] // parts).reshape([-1 if axis == axis_at else 1 for axis in range(len(extent))])
    return factor_of


def gaussian(own_key, shape, scale, most, cuts=(), held_as=jnp.bfloat16):
    values = scale * jax.random.normal(own_key, shape, jnp.float32)
    if cuts:
        values = values * level_of(own_key, shape, cuts, -0.22, 0.18)
    return jnp.clip(values, -most, most).astype(held_as)


def setup_inputs(seed: int = 0) -> dict:
    streams_of = jax.random.split(jax.random.key(seed), 11)
    return {
        "inputs": gaussian(streams_of[0], (TOKENS, D), 1.0, 6.0, ((0, 16),)),
        "segments": draw_segments(jax.random.fold_in(streams_of[10], 71), 0),
        "picks": draw_picks(jax.random.fold_in(streams_of[10], 71), 0),
        "gains": jnp.clip(1.0 + 0.1 * jax.random.normal(streams_of[3], (2, 2, D), jnp.float32), 0.5, 1.5),
        "router": gaussian(streams_of[4], (D,), D ** -0.5, 0.21875, (), jnp.float32),
        "qkv": gaussian(streams_of[5], (2, 3, D, D), D ** -0.5, 0.21875, ((3, 2),)),
        "proj_out": gaussian(streams_of[6], (2, D, D), 4 ** -0.5, 3.0, ((1, 2),)),
        "up": gaussian(streams_of[7], (2, D, FF), D ** -0.5, 0.21875, ((2, 2),)),
        "down": gaussian(streams_of[8], (2, FF, D), FF ** -0.5, 0.109375, ((1, 2),)),
        "cotangent": gaussian(streams_of[9], (TOKENS, D), 1.0, 6.0, ((0, 16),)),
    }


EPS = 1e-05
NEG = -1e+30

@jax.custom_vjp
def low(v):
    return lax.optimization_barrier(v.astype(jnp.bfloat16)).astype(jnp.float32)

@jax.custom_vjp
def low_back(v):
    return v

def low_keep(v):
    return (low(v), None)

def low_pass(kept, grad):
    return (grad,)

def back_keep(v):
    return (v, None)

def back_low(kept, grad):
    return (low(grad),)
low.defvjp(low_keep, low_pass)
low_back.defvjp(back_keep, back_low)

def matmul(left, right):
    return jnp.dot(left, right, precision=lax.Precision.HIGHEST, preferred_element_type=jnp.float32)

def rms_norm(values, gain):
    return values * lax.rsqrt(lax.optimization_barrier(jnp.mean(values * values, axis=-1, keepdims=True)) + EPS) * gain

def attend(query, keys, values, query_pos, key_pos, query_seg, key_seg):
    count = query.shape[0]
    width = min(512, count)
    key_heads = keys.reshape(keys.shape[0], H, HD)
    value_heads = values.reshape(values.shape[0], H, HD)

    def one_block(items):
        rows, rows_pos, rows_seg = items
        scores = jnp.einsum('qhd,khd->hqk', rows.reshape(width, H, HD), key_heads, precision=lax.Precision.HIGHEST) * HD ** (-0.5)
        scores = low_back(scores)
        allowed = (key_seg[None, :] == rows_seg[:, None]) & (key_pos[None, :] <= rows_pos[:, None])
        scores = jnp.where(allowed[None], scores, NEG)
        probs = low(jax.nn.softmax(scores, axis=-1))
        mixed = jnp.einsum('hqk,khd->qhd', probs, value_heads, precision=lax.Precision.HIGHEST)
        return mixed.reshape(width, H * HD)
    blocks = lax.map(jax.checkpoint(one_block), (query.reshape(-1, width, H * HD), query_pos.reshape(-1, width), query_seg.reshape(-1, width)))
    return blocks.reshape(count, H * HD)

def sublayers(rows, gain_pair, weights, projection, up_weight, down_weight, places, documents):
    normed = low(rms_norm(rows, gain_pair[0]))
    query = low(low_back(matmul(normed, weights[0])))
    keys = low(low_back(matmul(normed, weights[1])))
    values = low(low_back(matmul(normed, weights[2])))
    mixed = low(low_back(attend(query, keys, values, places, places, documents, documents)))
    attn = low_back(matmul(mixed, projection))
    hidden = rows + attn
    normed_two = low(rms_norm(hidden, gain_pair[1]))
    active = low(jax.nn.gelu(low_back(matmul(normed_two, up_weight))))
    mlp = low_back(matmul(active, down_weight))
    return (attn, mlp)

def reference(inputs, segments, picks, gains, router, qkv, proj_out, up, down, cotangent):
    tokens = inputs.shape[0]
    stream_pos = jnp.arange(tokens, dtype=jnp.int32)
    groups = picks.shape[0]
    positions = (picks + G * jnp.arange(groups, dtype=jnp.int32)[:, None]).reshape(-1).astype(jnp.int32)
    routed_seg = segments[positions]

    def forward(source, gain_all, router_vec, qkv_all, proj_all, up_all, down_all):
        chosen = source[positions]
        gate = jax.nn.sigmoid(matmul(chosen, router_vec))
        rows = low_back(chosen)
        attn, mlp = sublayers(rows, gain_all[0], qkv_all[0], proj_all[0], up_all[0], down_all[0], positions, routed_seg)
        change = low(low_back(attn + mlp))
        first = source.at[positions].add(gate[:, None] * change)
        attn_two, mlp_two = sublayers(first, gain_all[1], qkv_all[1], proj_all[1], up_all[1], down_all[1], stream_pos, segments)
        second = first + attn_two + mlp_two
        return (first, second)
    primals = (inputs.astype(jnp.float32), gains.astype(jnp.float32), router.astype(jnp.float32), qkv.astype(jnp.float32), proj_out.astype(jnp.float32), up.astype(jnp.float32), down.astype(jnp.float32))
    (first, second), pull = jax.vjp(forward, *primals)
    grads = pull((jnp.zeros_like(first), cotangent.astype(jnp.float32)))
    return (first.astype(jnp.bfloat16), second.astype(jnp.bfloat16), grads[0], grads[1], grads[2], grads[3], grads[4], grads[5], grads[6])
```

```python
from types import SimpleNamespace

import jax
import jax.numpy as jnp
import numpy as np
from jax import lax
from jax.experimental import pallas as pl
from jax.experimental.pallas import tpu as pltpu
from jax.sharding import PartitionSpec as P

HD = 64
G = 2048
EPS = 1e-05
NEG = -1e30
SCALE = HD**-0.5
BF = jnp.bfloat16
F32 = jnp.float32
MESH = pl.DeviceIdType.MESH
DMA = pltpu.SemaphoreType.DMA
GELU_A = 0.044715
GELU_B = float(np.sqrt(2.0 / np.pi))
KINDS = ("down", "up", "proj", "qkv")


def dot(left, right, dims):
    return lax.dot_general(left, right, (dims, ((), ())), preferred_element_type=F32)


def nn(left, right):
    return dot(left, right, ((1,), (0,)))


def nt(left, right):
    return dot(left, right, ((1,), (1,)))


def tn(left, right):
    return dot(left, right, ((0,), (0,)))


def inverse_rms(x):
    return lax.rsqrt(jnp.mean(x * x, axis=-1, keepdims=True) + EPS)


def rms(x, gain):
    return x * inverse_rms(x) * gain


def rms_back(dy, x, gain):
    r = inverse_rms(x)
    gy = gain * dy
    dx = r * gy - x * (r * r * r) * jnp.mean(gy * x, axis=-1, keepdims=True)
    return dx, jnp.sum(dy * x * r, axis=0, keepdims=True)


def gelu_pair(x):
    t = jnp.tanh(GELU_B * (x + GELU_A * x * x * x))
    half = 0.5 * (1.0 + t)
    slope = half + 0.5 * x * (1.0 - t * t) * (GELU_B * (1.0 + 3.0 * GELU_A * x * x))
    return x * half, slope


def column(row):
    wide = jnp.broadcast_to(row.astype(F32), (128, row.shape[1]))
    return jnp.transpose(wide)[:, 0:1]


def chunks(extent):
    width = 384 if extent % 384 == 0 else extent
    return [(at, width) for at in range(0, extent, width)]


def build(S, n, T, D, W, F, R, groups):
    rest = S // 2
    Y = 2 ** ((rest.bit_length() - 1) // 2)
    Z = rest // Y
    ZY = Z * Y
    H = W // HD
    LEVEL = 2 * Y
    CH = LEVEL * T
    GN = R // T
    RH = R // GN
    RB = R // S
    DM = D // n
    DR = D // S
    DRP = -(-DR // 16) * 16
    Q = ZY * DRP
    XW = {"down": F, "up": F, "proj": W, "qkv": 3 * W}

    target = np.full((2, 1, Q), -1, np.int32)
    for core in range(2):
        for yy in range(Y):
            for zz in range(Z):
                for j in range(DR):
                    target[core, 0, (yy * Z + zz) * DRP + j] = ((zz * Y + yy) * 2 + core) * DR + j

    ins = ["inp", "segr", "picks", "gains", "router", "cot", "target", "qkv_h", "proj_h", "up_h", "down_h"]
    outs = {
        "ro_o": ((T, D), BF),
        "do_o": ((T, D), BF),
        "gi_o": ((T, D), F32),
        "sm_o": ((8, 128), F32),
        "rg_o": ((2, D), F32),
        "qkv_o": ((2, 3, DR, W), F32),
        "proj_o": ((2, W, DR), F32),
        "up_o": ((2, DR, F), F32),
        "down_o": ((2, F, DR), F32),
    }
    vm = {
        "wq": ((2, 3, D, W), BF),
        "wp": ((2, W, D), BF),
        "wu": ((2, D, F), BF),
        "wd": ((2, F, D), BF),
        "sega": ((S, 8, T), jnp.int32),
        "segc": ((T, 1), F32),
        "oht": ((T, R), BF),
        "oh": ((R, T), BF),
        "posr": ((GN, 8, RH), F32),
        "posc": ((RH, 1), F32),
        "sgr": ((GN, 8, RH), F32),
        "sgc": ((RH, 1), F32),
        "part": ((S, RB, DM), BF),
        "r1": ((S, RB, DM), BF),
        "full": ((2, n * ZY, RB, DM), BF),
        "rows": ((R, D), BF),
        "nr": ((RH, D), BF),
        "chh": ((RH, D), BF),
        "qr": ((R, W), BF),
        "kr": ((R, W), BF),
        "vr": ((R, W), BF),
        "mr": ((H, RH, 1), F32),
        "lr": ((H, RH, 1), F32),
        "ar": ((H, RH, HD), F32),
        "mixr": ((RH, W), BF),
        "attr": ((RH, D), F32),
        "n2r": ((RH, D), BF),
        "prer": ((RH, F), F32),
        "actr": ((RH, F), BF),
        "xr": ((2, n, RH, D), BF),
        "xd": ((3, n, T, D), BF),
        "chg": ((GN, RH, D), BF),
        "sel": ((T, D), BF),
        "ro": ((T, D), F32),
        "nd": ((T, D), BF),
        "kva": ((S, T, 2 * W), BF),
        "qa": ((S, T, W), BF),
        "da": ((S, T, W), BF),
        "sta": ((S, 16, T), F32),
        "md": ((H, T, 1), F32),
        "ld": ((H, T, 1), F32),
        "ad": ((H, T, HD), F32),
        "mixd": ((T, W), BF),
        "hid": ((T, D), F32),
        "n2d": ((T, D), BF),
        "dact": ((T, F), F32),
        "actd": ((T, F), BF),
        "dpre": ((T, F), BF),
        "dattn": ((T, D), BF),
        "dq": ((H, max(T, RH), HD), F32),
        "dk": ((H, max(T, RH), HD), F32),
        "dv": ((H, max(T, RH), HD), F32),
        "g3": ((T, 3 * W), BF),
        "dro": ((T, D), F32),
        "small": ((8, D), F32),
        "sblk": ((S, 8, 128), F32),
        "srec": ((S, 8, 128), F32),
        "dor": ((GN, RH, W), BF),
        "str": ((GN, 16, RH), F32),
        "dprer": ((RH, F), BF),
        "dattr": ((RH, D), BF),
        "g3r": ((RH, 3 * W), BF),
        "gr": ((GN, 8, D), F32),
        "sele": ((2, D, Q), BF),
    }
    for k in KINDS:
        X = XW[k]
        vm["keep_" + k] = ((Y, Z, DRP, X), F32)
        vm["send_" + k] = ((Y, Z, DRP, X), BF)
        vm["sibr_" + k] = ((Y, Z, DRP, X), BF)
        vm["yrec_" + k] = ((Y - 1, Z, DRP, X), BF)
        vm["zrec_" + k] = ((Z - 1, DRP, X), BF)
        vm["rsend_" + k] = ((GN - 1, DRP, X), BF)
        vm["rkeep_" + k] = ((DRP, X), F32)
        vm["rrec_" + k] = ((GN - 1, DRP, X), BF)
    n_sends = (Z - 1) + (Y - 1) + 1 + (Z - 1) * Y + Z * (Y - 1)
    sems = {
        "w_s": (8,),
        "seg_s": (2,),
        "t_s": (6,),
        "xr_s": (2, n - 1),
        "xr_r": (2, n - 1),
        "xd_s": (3, n - 1),
        "xd_r": (3, n - 1),
        "sw_s": (10, GN - 1),
        "sw_r": (10, GN - 1),
        "kv_s": (n_sends,),
        "kv_r": (S,),
        "q_s": (n_sends,),
        "q_r": (S,),
        "da_s": (n_sends,),
        "da_r": (S,),
        "st_s": (n_sends,),
        "st_r": (S,),
        "sm_s": (2,),
        "gs_s": (4,),
        "gs_r": (4,),
        "gy_s": (4, Y - 1),
        "gy_r": (4, Y - 1),
        "gz_s": (4, Z - 1),
        "gz_r": (4, Z - 1),
    }
    names = ins + list(outs) + list(vm) + list(sems)

    def kernel(*refs):
        r = SimpleNamespace(**dict(zip(names, refs, strict=True)))
        g = r.__dict__
        s = lax.axis_index("seq")
        m = lax.axis_index("mlp")
        c = lax.rem(s, 2)
        chip = s // 2
        y = lax.rem(chip, Y)
        z = chip // Y
        sib = s + 1 - 2 * c
        gi = lax.rem(s, GN)

        def rank(zz, yy, cc):
            return (zz * Y + yy) * 2 + cc

        def remote(src, dst, send, recv, seq, mlp):
            return pltpu.make_async_remote_copy(
                src_ref=src, dst_ref=dst, send_sem=send, recv_sem=recv, device_id=(seq, mlp), device_id_type=MESH
            )

        bar = pltpu.get_barrier_semaphore()

        def greet(i, carry):
            pl.semaphore_signal(bar, inc=1, device_id=(lax.rem(s + i, S), m), device_id_type=MESH)
            return carry

        lax.fori_loop(1, S, greet, 0)
        for j in range(1, n):

            def greet_other(i, carry, j=j):
                pl.semaphore_signal(bar, inc=1, device_id=(i * 2 + c, lax.rem(m + j, n)), device_id_type=MESH)
                return carry

            lax.fori_loop(0, ZY, greet_other, 0)
        loads = [
            pltpu.make_async_copy(src.at[b], dst.at[b], r.w_s.at[4 * b + i])
            for b in range(2)
            for i, (src, dst) in enumerate(
                ((r.qkv_h, r.wq), (r.proj_h, r.wp), (r.up_h, r.wu), (r.down_h, r.wd))
            )
        ]
        for load in loads:
            load.start()

        prow = jnp.concatenate([r.picks[i : i + 1, :] + G * i for i in range(groups)], axis=1)
        here = s * T + lax.broadcasted_iota(jnp.int32, (T, R), 0)
        hot = jnp.where(prow == here, 1.0, 0.0)
        r.oht[...] = hot.astype(BF)
        r.oh[...] = jnp.transpose(hot).astype(BF)
        prow_f = prow.astype(F32)
        for i in range(GN):
            r.posr[i] = jnp.broadcast_to(prow_f[:, i * RH : (i + 1) * RH], (8, RH))
        r.posc[...] = column(r.posr[gi][0:1])
        r.sega[s] = jnp.broadcast_to(r.segr[...], (8, T))
        r.segc[...] = column(r.segr[...])

        def my_columns(x):
            got = x[:, 0:DM]
            for j in range(1, n):
                got = jnp.where(m == j, x[:, j * DM : (j + 1) * DM], got)
            return got

        def scatter_rows(x):
            r.part[...] = nn(r.oh[...], my_columns(x)).astype(BF).reshape(S, RB, DM)

        scatter_rows(r.inp[...])
        pl.semaphore_wait(bar, S - 1 + (n - 1) * ZY)

        def send_segments(i, carry):
            remote(r.sega.at[s], r.sega.at[s], r.seg_s.at[0], r.seg_s.at[1], lax.rem(s + i, S), m).start()
            return carry

        lax.fori_loop(1, S, send_segments, 0)

        def spread_rows():
            sem = [r.t_s.at[j] for j in range(6)]

            def first(k, carry):
                p = lax.rem(s + k, S)
                remote(r.part.at[p], r.r1.at[s], sem[0], sem[1], p, m).start()
                return carry

            lax.fori_loop(1, S, first, 0)
            r.r1[s] = r.part[s]
            some = pl.ds(0, S - 1)
            remote(r.part.at[some], r.r1.at[some], sem[0], sem[1], s, m).wait()
            me = m * ZY + chip
            r.full[c, me] = jnp.sum(r.r1[...].astype(F32), axis=0).astype(BF)

            def second(k, carry):
                p = lax.rem(me + k, n * ZY)
                block = r.full.at[c, me]
                remote(block, block, sem[2], sem[3], lax.rem(p, ZY) * 2 + c, p // ZY).start()
                return carry

            lax.fori_loop(1, n * ZY, second, 0)
            some = r.full.at[c, pl.ds(0, n * ZY - 1)]
            remote(some, some, sem[2], sem[3], s, m).wait()
            swap = remote(r.full.at[c], r.full.at[c], sem[4], sem[5], sib, m)
            swap.start()
            swap.wait()

            def place(k, carry):
                for cc in range(2):
                    rows = pl.ds(pl.multiple_of((k * 2 + cc) * RB, RB), RB)
                    for mm in range(n):
                        r.rows[rows, mm * DM : (mm + 1) * DM] = r.full[cc, mm * ZY + k]
                return carry

            lax.fori_loop(0, ZY, place, 0)

        def mlp_copies(buf, send, recv, i):
            i = i % buf.shape[0]
            return [
                remote(buf.at[i, m], buf.at[i, m], send.at[i, j - 1], recv.at[i, j - 1], s, lax.rem(m + j, n))
                for j in range(1, n)
            ]

        def mlp_start(which, i, value):
            buf = g["x" + which]
            buf[i % buf.shape[0], m] = value.astype(BF)
            for copy in mlp_copies(buf, g["x" + which + "_s"], g["x" + which + "_r"], i):
                copy.start()

        def mlp_total(which, i):
            buf = g["x" + which]
            for copy in mlp_copies(buf, g["x" + which + "_s"], g["x" + which + "_r"], i):
                copy.wait()
            i = i % buf.shape[0]
            total = buf[i, 0].astype(F32)
            for j in range(1, n):
                total = total + buf[i, j].astype(F32)
            return total

        def friend(j):
            return s - gi + lax.rem(gi + j, GN)

        def share(i, *refs):
            return [
                remote(ref.at[gi], ref.at[gi], r.sw_s.at[i + k, j - 1], r.sw_r.at[i + k, j - 1], friend(j), m)
                for k, ref in enumerate(refs)
                for j in range(1, GN)
            ]

        def attend(count, pick, query, key, value, mask, top, total, acc):
            top[...] = jnp.full(top.shape, NEG, F32)
            total[...] = jnp.zeros(total.shape, F32)
            acc[...] = jnp.zeros(acc.shape, F32)

            def step(i, carry):
                ci = pick(i)
                kept = mask(ci)
                for h in range(H):
                    scores = jnp.where(kept, nt(query(h), key(ci, h)) * SCALE, NEG)
                    old = top[h]
                    new = jnp.maximum(old, jnp.max(scores, axis=-1, keepdims=True))
                    shrink = jnp.exp(old - new)
                    weights = jnp.exp(scores - new)
                    total[h] = total[h] * shrink + jnp.sum(weights, axis=-1, keepdims=True)
                    acc[h] = acc[h] * shrink + nn(weights.astype(BF), value(ci, h))
                    top[h] = new
                return carry

            lax.fori_loop(0, count, step, 0)

        def finish(top, total, acc, mixed):
            for h in range(H):
                out = acc[h] / total[h]
                acc[h] = out
                mixed[:, h * HD : (h + 1) * HD] = out.astype(BF)
                top[h] = top[h] + jnp.log(total[h])

        def row_stats(grad, top, total, acc):
            lane = lax.broadcasted_iota(jnp.int32, (acc.shape[1], 128), 1)
            stats = jnp.zeros((acc.shape[1], 128), F32)
            for h in range(H):
                delta = jnp.sum(grad(h).astype(F32) * acc[h], axis=-1, keepdims=True)
                total[h] = delta
                stats = jnp.where(lane == h, top[h], jnp.where(lane == 8 + h, delta, stats))
            return jnp.transpose(stats)[0:16]

        def back_query(count, pick, query, grad, key, value, mask, log_total, delta, out):
            out[...] = jnp.zeros(out.shape, F32)

            def step(i, carry):
                ci = pick(i)
                kept = mask(ci)
                for h in range(H):
                    scores = nt(query(h), key(ci, h)) * SCALE
                    probs = jnp.where(kept, jnp.exp(scores - log_total[h]), 0.0)
                    grad_probs = nt(grad(h), value(ci, h))
                    grad_scores = (probs * (grad_probs - delta[h])).astype(BF)
                    out[h] = out[h] + nn(grad_scores, key(ci, h))
                return carry

            lax.fori_loop(0, count, step, 0)

        def back_keys(count, pick, key, value, query, grad, mask, stat, out_key, out_value):
            out_key[...] = jnp.zeros(out_key.shape, F32)
            out_value[...] = jnp.zeros(out_value.shape, F32)

            def step(i, carry):
                ci = pick(i)
                kept = mask(ci)
                for h in range(H):
                    scores = nt(key(h), query(ci, h)) * SCALE
                    probs = jnp.where(kept, jnp.exp(scores - stat(ci, h)), 0.0)
                    out_value[h] = out_value[h] + nn(probs.astype(BF), grad(ci, h))
                    grad_probs = nt(value(h), grad(ci, h))
                    grad_scores = (probs * (grad_probs - stat(ci, 8 + h))).astype(BF)
                    out_key[h] = out_key[h] + nn(grad_scores, query(ci, h))
                return carry

            lax.fori_loop(0, count, step, 0)

        dq_d, dk_d, dv_d = (ref.at[:, 0:T] for ref in (r.dq, r.dk, r.dv))
        dq_r, dk_r, dv_r = (ref.at[:, 0:RH] for ref in (r.dq, r.dk, r.dv))

        def pack_grads(dq, dk, dv, out):
            for h in range(H):
                out[:, h * HD : (h + 1) * HD] = (dq[h] * SCALE).astype(BF)
                out[:, W + h * HD : W + (h + 1) * HD] = (dk[h] * SCALE).astype(BF)
                out[:, 2 * W + h * HD : 2 * W + (h + 1) * HD] = dv[h].astype(BF)

        def front_back(grads, b):
            return (
                nt(grads[:, 0:W], r.wq[b, 0])
                + nt(grads[:, W : 2 * W], r.wq[b, 1])
                + nt(grads[:, 2 * W : 3 * W], r.wq[b, 2])
            )

        def gather(items):
            sent = []
            at = [0]

            def send(cond, slot, dst, which):
                k = at[0]
                for buf, ss, rs, up in [items[w] for w in which]:

                    def copy(buf=buf, ss=ss, rs=rs):
                        return remote(buf.at[slot], buf.at[slot], ss.at[k], rs.at[slot], dst, m)

                    if cond is None:
                        copy().start()
                    else:
                        pl.when(cond)(lambda copy=copy: copy().start())
                    sent.append((cond, copy))
                at[0] += 1

            def recv(slot, which):
                for buf, ss, rs, up in [items[w] for w in which]:
                    remote(buf.at[slot], buf.at[slot], ss.at[0], rs.at[slot], s, m).wait_recv()

            every = list(range(len(items)))
            ups = [w for w in every if items[w][3]]
            downs = [w for w in every if not items[w][3]]

            def start():
                for dz in range(1, Z):
                    k = at[0]
                    if ups:
                        send(z + dz < Z, s, rank(z + dz, y, c), ups)
                    if downs:
                        at[0] = k
                        send(z - dz >= 0, s, rank(z - dz, y, c), downs)
                    at[0] = k + 1
                for dy in range(1, Y):
                    send(None, s, rank(z, lax.rem(y + dy, Y), c), every)
                send(None, s, sib, every)

            def level():
                for dy in range(1, Y):
                    slot = rank(z, lax.rem(y + dy, Y), c)
                    recv(slot, every)
                    send(None, slot, sib, every)

            def relay(cond, slot, which, wide):
                pl.when(cond)(lambda: recv(slot, which))
                if wide:
                    for dy in range(1, Y):
                        send(cond, slot, rank(z, lax.rem(y + dy, Y), c), which)
                send(cond, slot, sib, which)

            def both(dz, body):
                k = at[0]
                end = k
                for sign, which in ((-1, ups), (1, downs)):
                    if which:
                        at[0] = k
                        zz = z + sign * dz
                        body((zz >= 0) & (zz < Z), zz, which)
                        end = at[0]
                at[0] = end

            def rest():
                for dz in range(1, Z):
                    both(dz, lambda cond, zz, which: relay(cond, rank(zz, y, c), which, True))
                for dz in range(1, Z):
                    for dy in range(1, Y):
                        yy = lax.rem(y + dy, Y)
                        both(dz, lambda cond, zz, which: relay(cond, rank(zz, yy, c), which, False))
                for dy in range(Y):
                    recv(rank(z, lax.rem(y + dy, Y), 1 - c), every)
                for dz in range(1, Z):
                    for dy in range(Y):
                        yy = lax.rem(y + dy, Y)

                        def last(cond, zz, which):
                            pl.when(cond)(lambda: recv(rank(zz, yy, 1 - c), which))

                        both(dz, last)

            def end():
                for cond, copy in sent:
                    if cond is None:
                        copy().wait_send()
                    else:
                        pl.when(cond)(lambda copy=copy: copy().wait_send())

            return SimpleNamespace(start=start, level=level, rest=rest, end=end)

        for par in range(2):
            ids = lax.broadcasted_iota(jnp.int32, (D, Q), 0)
            r.sele[par] = jnp.where(ids == r.target[par], 1.0, 0.0).astype(BF)

        def sum_start(k, lhs, rhs):
            i = KINDS.index(k)
            out = nn(lhs[...], r.sele[1 - c]).astype(BF)
            stay = nn(lhs[...], r.sele[c]).astype(BF)
            for x, w in chunks(XW[k]):
                g["send_" + k][:, :, :, x : x + w] = tn(out, rhs[:, x : x + w]).astype(BF).reshape(Y, Z, DRP, w)
            remote(g["send_" + k], g["sibr_" + k], r.gs_s.at[i], r.gs_r.at[i], sib, m).start()
            for x, w in chunks(XW[k]):
                g["keep_" + k][:, :, :, x : x + w] = tn(stay, rhs[:, x : x + w]).reshape(Y, Z, DRP, w)

        def y_copy(k, i, dy):
            return remote(
                g["sibr_" + k].at[lax.rem(y + dy, Y)],
                g["yrec_" + k].at[dy - 1],
                r.gy_s.at[i, dy - 1],
                r.gy_r.at[i, dy - 1],
                rank(z, lax.rem(y + dy, Y), c),
                m,
            )

        def z_copy(k, i, dz):
            return remote(
                g["yrec_" + k].at[0, lax.rem(z + dz, Z)],
                g["zrec_" + k].at[dz - 1],
                r.gz_s.at[i, dz - 1],
                r.gz_r.at[i, dz - 1],
                rank(lax.rem(z + dz, Z), y, c),
                m,
            )

        def sum_y(k):
            i = KINDS.index(k)
            remote(g["send_" + k], g["sibr_" + k], r.gs_s.at[i], r.gs_r.at[i], sib, m).wait()
            for dy in range(1, Y):
                yy = lax.rem(y + dy, Y)
                g["sibr_" + k][yy] = (g["keep_" + k][yy] + g["sibr_" + k][yy].astype(F32)).astype(BF)
                y_copy(k, i, dy).start()

        def sum_z(k):
            i = KINDS.index(k)
            for dy in range(1, Y):
                y_copy(k, i, dy).wait()

            def total(zz):
                t = g["keep_" + k][y, zz] + g["sibr_" + k][y, zz].astype(F32)
                for dy in range(1, Y):
                    t = t + g["yrec_" + k][dy - 1, zz].astype(F32)
                return t

            for dz in range(1, Z):
                zz = lax.rem(z + dz, Z)
                g["yrec_" + k][0, zz] = total(zz).astype(BF)
                z_copy(k, i, dz).start()
            g["keep_" + k][y, z] = total(z)

        def put(b, k, value):
            if k == "qkv":
                for j in range(3):
                    r.qkv_o[b, j] = value[0:DR, j * W : (j + 1) * W]
            elif k == "up":
                r.up_o[b] = value[0:DR]
            else:
                g[k + "_o"][b] = jnp.transpose(value)[:, 0:DR]

        def sum_end(k):
            i = KINDS.index(k)
            t = g["keep_" + k][y, z]
            for dz in range(1, Z):
                z_copy(k, i, dz).wait()
                t = t + g["zrec_" + k][dz - 1].astype(F32)
            put(1, k, t)

        def routed_copy(k, j):
            i = 6 + KINDS.index(k)
            send, recv = r.sw_s.at[i, j - 1], r.sw_r.at[i, j - 1]
            return remote(g["rsend_" + k].at[j - 1], g["rrec_" + k].at[j - 1], send, recv, friend(j), m)

        def routed_start(k, lhs, rhs):
            col = lax.broadcasted_iota(jnp.int32, (D, DRP), 1)
            row = lax.broadcasted_iota(jnp.int32, (D, DRP), 0)

            def block(who):
                hit = (row - who * DR == col) & (col < DR)
                return nn(lhs, jnp.where(hit, 1.0, 0.0).astype(BF)).astype(BF)

            for j in range(1, GN):
                g["rsend_" + k][j - 1] = tn(block(friend(j)), rhs).astype(BF)
                routed_copy(k, j).start()
            g["rkeep_" + k][...] = tn(block(s), rhs)

        def routed_end(k):
            t = g["rkeep_" + k][...]
            for j in range(1, GN):
                routed_copy(k, j).wait()
                t = t + g["rrec_" + k][j - 1].astype(F32)
            put(0, k, t)

        def head(h):
            return slice(h * HD, (h + 1) * HD)

        spread_rows()
        some = pl.ds(0, S - 1)
        remote(r.sega.at[some], r.sega.at[some], r.seg_s.at[0], r.seg_s.at[1], s, m).wait()
        starts = [
            jnp.sum(
                jnp.sum(jnp.where(r.sega[...] < k, 0.125, 0.0), axis=0), axis=(0, 1), keepdims=True
            )
            for k in range(1, 5)
        ]
        for i in range(GN):
            r.sgr[i] = sum(jnp.where(r.posr[i] >= at, 1.0, 0.0) for at in starts)
        r.sgc[...] = sum(jnp.where(r.posc[...] >= at, 1.0, 0.0) for at in starts)
        half = pl.ds(pl.multiple_of(gi * RH, RH), RH)

        loads[0].wait()
        r.chh[...] = r.rows[half, :]
        r.nr[...] = rms(r.chh[...].astype(F32), r.gains[0, 0:1]).astype(BF)
        for at in range(0, R, 256):
            part = slice(at, at + 256)
            normed = rms(r.rows[part].astype(F32), r.gains[0, 0:1]).astype(BF)
            r.qr[part] = nn(normed, r.wq[0, 0]).astype(BF)
            r.kr[part] = nn(normed, r.wq[0, 1]).astype(BF)
            r.vr[part] = nn(normed, r.wq[0, 2]).astype(BF)

        def part_rows(ref):
            return lambda ci, h: ref[pl.ds(pl.multiple_of(ci * RH, RH), RH), head(h)]

        def half_rows(ref):
            return lambda h: ref[half, head(h)]

        def routed_mask(ci):
            return (r.sgr[ci][0:1] == r.sgc[...]) & (r.posr[ci][0:1] <= r.posc[...])

        def routed_mask_back(ci):
            return (r.sgr[ci][0:1] == r.sgc[...]) & (r.posc[...] <= r.posr[ci][0:1])

        def routed_pick(i):
            return lax.rem(gi + i, GN)

        attend(GN, routed_pick, half_rows(r.qr), part_rows(r.kr), part_rows(r.vr), routed_mask, r.mr, r.lr, r.ar)
        finish(r.mr, r.lr, r.ar, r.mixr)
        loads[1].wait()
        mlp_start("r", 0, nn(r.mixr[...], r.wp[0]))
        loads[2].wait()
        loads[3].wait()
        attn = mlp_total("r", 0)
        r.attr[...] = attn
        normed = rms(r.chh[...].astype(F32) + attn, r.gains[0, 1:2]).astype(BF)
        r.n2r[...] = normed
        for x, w in chunks(F):
            pre = nn(normed, r.wu[0, :, x : x + w])
            r.prer[:, x : x + w] = pre
            r.actr[:, x : x + w] = gelu_pair(pre)[0].astype(BF)
        mlp_start("r", 1, nn(r.actr[...], r.wd[0]))
        mlp = mlp_total("r", 1)
        r.chg[gi] = (r.attr[...] + mlp).astype(BF)
        swaps = share(0, r.chg)
        for copy in swaps:
            copy.start()
        inp = r.inp[...].astype(F32)
        gate = jax.nn.sigmoid(jnp.sum(inp * r.router[...], axis=-1, keepdims=True))
        for load in loads[4:]:
            load.wait()
        for copy in swaps:
            copy.wait()

        sel = nn(r.oht[...], r.chg[...].reshape(R, D))
        r.sel[...] = sel.astype(BF)
        ro = inp + gate * sel
        r.ro[...] = ro
        r.ro_o[...] = ro.astype(BF)
        normed = rms(ro, r.gains[1, 0:1]).astype(BF)
        r.nd[...] = normed
        r.kva[s, :, 0:W] = nn(normed, r.wq[1, 1]).astype(BF)
        r.kva[s, :, W : 2 * W] = nn(normed, r.wq[1, 2]).astype(BF)
        r.qa[s] = nn(normed, r.wq[1, 0]).astype(BF)
        spread = gather([(r.kva, r.kv_s, r.kv_r, True), (r.qa, r.q_s, r.q_r, False)])
        spread.start()
        spread.level()
        spread.rest()

        def level_rows(ref, first=0):
            def get(ci, h):
                return ref[pl.ds(ci * LEVEL, LEVEL), :, head(first + h)].reshape(CH, HD)

            return get

        def level_line(ref, line):
            return lambda ci: jnp.concatenate([ref[ci * LEVEL + j][line : line + 1] for j in range(LEVEL)], axis=1)

        own_pos = lax.broadcasted_iota(jnp.int32, (T, CH), 0) + s * T
        far_pos = lax.broadcasted_iota(jnp.int32, (T, CH), 1)
        seg_line = level_line(r.sega, 0)

        def dense_mask(ci):
            return (seg_line(ci).astype(F32) == r.segc[...]) & (far_pos + ci * CH <= own_pos)

        def dense_mask_back(ci):
            return (seg_line(ci).astype(F32) == r.segc[...]) & (own_pos <= far_pos + ci * CH)

        attend(
            z + 1,
            lambda i: z - i,
            lambda h: r.qa[s, :, head(h)],
            level_rows(r.kva, 0),
            level_rows(r.kva, H),
            dense_mask,
            r.md,
            r.ld,
            r.ad,
        )
        finish(r.md, r.ld, r.ad, r.mixd)
        mlp_start("d", 0, nn(r.mixd[...], r.wp[1]))
        for x, w in chunks(F):
            r.dact[:, x : x + w] = nt(r.cot[...], r.wd[1, x : x + w, :])
        attn = mlp_total("d", 0)
        hid = r.ro[...] + attn
        r.hid[...] = hid
        normed = rms(hid, r.gains[1, 1:2]).astype(BF)
        r.n2d[...] = normed
        for x, w in chunks(F):
            active, slope = gelu_pair(nn(normed, r.wu[1, :, x : x + w]))
            r.actd[:, x : x + w] = active.astype(BF)
            r.dpre[:, x : x + w] = (r.dact[:, x : x + w] * slope).astype(BF)
        mlp_start("d", 1, nt(r.dpre[...], r.wu[1]))
        mlp_start("d", 2, nn(r.actd[...], r.wd[1]))

        sum_start("down", r.cot, r.actd)
        sum_start("up", r.n2d, r.dpre)
        dn, dg = rms_back(mlp_total("d", 1), r.hid[...], r.gains[1, 1:2])
        r.small[1:2] = dg
        dhid = r.cot[...].astype(F32) + dn
        r.dro[...] = dhid
        r.dattn[...] = dhid.astype(BF)
        r.da[s] = nt(r.dattn[...], r.wp[1]).astype(BF)
        r.sta[s] = row_stats(lambda h: r.da[s, :, head(h)], r.md, r.ld, r.ad)
        spread_back = gather([(r.da, r.da_s, r.da_r, False), (r.sta, r.st_s, r.st_r, False)])
        spread_back.start()
        spread_back.level()
        back_query(
            z + 1,
            lambda i: z - i,
            lambda h: r.qa[s, :, head(h)],
            lambda h: r.da[s, :, head(h)],
            level_rows(r.kva, 0),
            level_rows(r.kva, H),
            dense_mask,
            r.md,
            r.ld,
            dq_d,
        )
        spread_back.rest()
        back_keys(
            Z - z,
            lambda i: z + i,
            lambda h: r.kva[s, :, head(h)],
            lambda h: r.kva[s, :, head(H + h)],
            level_rows(r.qa),
            level_rows(r.da),
            dense_mask_back,
            lambda ci, line: level_line(r.sta, line)(ci),
            dk_d,
            dv_d,
        )
        pack_grads(dq_d, dk_d, dv_d, r.g3)
        mlp_start("d", 3, front_back(r.g3, 1))
        sum_start("proj", r.dattn, r.mixd)
        sum_start("qkv", r.nd, r.g3)
        sum_y("down")
        dn, dg = rms_back(mlp_total("d", 3), r.ro[...], r.gains[1, 0:1])
        r.small[0:1] = dg
        dro = r.dro[...] + dn
        r.dro[...] = dro

        sel = r.sel[...].astype(F32)
        inp = r.inp[...].astype(F32)
        gate = jax.nn.sigmoid(jnp.sum(inp * r.router[...], axis=-1, keepdims=True))
        dlogit = jnp.sum(dro * sel, axis=-1, keepdims=True) * gate * (1.0 - gate)
        scatter_rows((gate * dro).astype(BF))
        spread_rows()
        r.small[2:3] = jnp.sum(inp * dlogit, axis=0, keepdims=True)
        r.small[3:8] = jnp.zeros((5, D), F32)
        r.sblk[...] = jnp.zeros((S, 8, 128), F32)
        for p in range(S):
            r.sblk[p, :, 0:DR] = r.small[:, p * DR : (p + 1) * DR]

        def send_small(i, carry):
            p = lax.rem(s + i, S)
            remote(r.sblk.at[p], r.srec.at[s], r.sm_s.at[0], r.sm_s.at[1], p, m).start()
            return carry

        lax.fori_loop(1, S, send_small, 0)
        r.srec[s] = r.sblk[s]

        dmlp = r.rows[half, :]
        r.attr[...] = r.attr[...] + r.chh[...].astype(F32)
        for x, w in chunks(F):
            grad_active = nt(dmlp, r.wd[0, x : x + w, :])
            r.dprer[:, x : x + w] = (grad_active * gelu_pair(r.prer[:, x : x + w])[1]).astype(BF)
        mlp_start("r", 2, nt(r.dprer[...], r.wu[0]))
        routed_start("down", dmlp, r.actr[...])
        routed_start("up", r.n2r[...], r.dprer[...])
        dn, dg2 = rms_back(mlp_total("r", 2), r.attr[...], r.gains[0, 1:2])
        r.attr[...] = dn
        r.dattr[...] = (dmlp.astype(F32) + dn).astype(BF)
        r.dor[gi] = nt(r.dattr[...], r.wp[0]).astype(BF)
        r.str[gi] = row_stats(lambda h: r.dor[gi, :, head(h)], r.mr, r.lr, r.ar)
        swaps = share(1, r.dor, r.str)
        for copy in swaps:
            copy.start()
        routed_start("proj", r.dattr[...], r.mixr[...])
        back_query(
            GN,
            routed_pick,
            half_rows(r.qr),
            lambda h: r.dor[gi, :, head(h)],
            part_rows(r.kr),
            part_rows(r.vr),
            routed_mask,
            r.mr,
            r.lr,
            dq_r,
        )
        for copy in swaps:
            copy.wait()
        back_keys(
            GN,
            routed_pick,
            half_rows(r.kr),
            half_rows(r.vr),
            part_rows(r.qr),
            lambda ci, h: r.dor[ci, :, head(h)],
            routed_mask_back,
            lambda ci, line: r.str[ci][line : line + 1],
            dk_r,
            dv_r,
        )
        pack_grads(dq_r, dk_r, dv_r, r.g3r)
        mlp_start("r", 3, front_back(r.g3r, 0))
        routed_start("qkv", r.nr[...], r.g3r[...])
        sum_y("up")
        sum_y("proj")
        sum_y("qkv")
        sum_z("down")
        dn, dg1 = rms_back(mlp_total("r", 3), r.chh[...].astype(F32), r.gains[0, 0:1])
        r.chg[gi] = (r.attr[...] + dn).astype(BF)
        r.gr[gi] = jnp.concatenate([dg1, dg2, jnp.zeros((6, D), F32)], axis=0)
        swaps = share(3, r.chg, r.gr)
        for copy in swaps:
            copy.start()
        for copy in swaps:
            copy.wait()
        r.rg_o[...] = jnp.sum(r.gr[...], axis=0)[0:2]
        back = nn(r.oht[...], r.chg[...].reshape(R, D))
        inp = r.inp[...].astype(F32)
        gate = jax.nn.sigmoid(jnp.sum(inp * r.router[...], axis=-1, keepdims=True))
        dlogit = jnp.sum(r.dro[...] * r.sel[...].astype(F32), axis=-1, keepdims=True) * gate * (1.0 - gate)
        r.gi_o[...] = r.dro[...] + back + dlogit * r.router[...]

        r.do_o[...] = (r.hid[...] + mlp_total("d", 2)).astype(BF)
        some = pl.ds(0, S - 1)
        remote(r.sblk.at[some], r.srec.at[some], r.sm_s.at[0], r.sm_s.at[1], s, m).wait()
        r.sm_o[...] = jnp.sum(r.srec[...], axis=0)
        for k in ("up", "proj", "qkv"):
            sum_z(k)
        for k in KINDS:
            routed_end(k)
        for k in KINDS:
            sum_end(k)
        spread.end()
        spread_back.end()

    def run(inp, segments, picks, gains, router, qkv, proj, up, down, cot):
        args = (
            inp,
            segments.reshape(1, T),
            picks,
            gains,
            router.reshape(1, D),
            cot,
            jnp.asarray(target),
            qkv,
            proj,
            up,
            down,
        )
        vmem = pl.BlockSpec(memory_space=pltpu.VMEM)
        hbm = pl.BlockSpec(memory_space=pl.ANY)
        res = pl.pallas_call(
            kernel,
            out_shape=[jax.ShapeDtypeStruct(sh, dt) for sh, dt in outs.values()],
            in_specs=[vmem] * 7 + [hbm] * 4,
            out_specs=[vmem] * len(outs),
            scratch_shapes=[pltpu.VMEM(sh, dt) for sh, dt in vm.values()] + [DMA(sh) for sh in sems.values()],
            compiler_params=pltpu.CompilerParams(
                collective_id=0, has_side_effects=True, vmem_limit_bytes=62 * 1024 * 1024
            ),
            name="train_step",
        )(*args)
        ro, do, gi, sm, rg, gq, gp, gu, gd = res
        at = lax.axis_index("seq") * DR
        routed_gains = lax.dynamic_slice_in_dim(rg, at, DR, 1)
        gains_grad = jnp.stack([routed_gains, sm[0:2, 0:DR]])
        return (ro, do, gi, gains_grad, sm[2, 0:DR], gq, gp, gu, gd)

    return run


def solution(mesh):
    S, n = mesh.shape["seq"], mesh.shape["mlp"]

    def body(inp, segments, picks, gains, router, qkv, proj, up, down, cot):
        run = build(
            S, n, inp.shape[0], inp.shape[1], qkv.shape[-1], up.shape[-1], picks.size, picks.shape[0]
        )
        return run(inp, segments, picks, gains, router, qkv, proj, up, down, cot)

    return jax.shard_map(
        body,
        mesh=mesh,
        in_specs=(
            P("seq", None),
            P("seq"),
            P(),
            P(),
            P(),
            P(None, None, None, "mlp"),
            P(None, "mlp", None),
            P(None, None, "mlp"),
            P(None, "mlp", None),
            P("seq", None),
        ),
        out_specs=(
            P("seq", None),
            P("seq", None),
            P("seq", None),
            P(None, None, "seq"),
            P("seq"),
            P(None, None, "seq", "mlp"),
            P(None, "mlp", "seq"),
            P(None, "seq", "mlp"),
            P(None, "mlp", "seq"),
        ),
        check_vma=False,
    )
```

```python
from types import SimpleNamespace

import jax
import jax.numpy as jnp
import numpy as np
from jax import lax
from jax.experimental import pallas as pl
from jax.experimental.pallas import tpu as pltpu
from jax.sharding import PartitionSpec as P

HD = 64
G = 2048
EPS = 1e-05
NEG = -1e30
SCALE = HD**-0.5
BF = jnp.bfloat16
F32 = jnp.float32
MESH = pl.DeviceIdType.MESH
DMA = pltpu.SemaphoreType.DMA
GELU_A = 0.044715
GELU_B = float(np.sqrt(2.0 / np.pi))
WIDE = 1536
KINDS = ("down", "up", "proj", "qkv")


def dot(left, right, dims):
    return lax.dot_general(left, right, (dims, ((), ())), preferred_element_type=F32)


def nn(left, right):
    return dot(left, right, ((1,), (0,)))


def nt(left, right):
    return dot(left, right, ((1,), (1,)))


def tn(left, right):
    return dot(left, right, ((0,), (0,)))


def inverse_rms(x):
    return lax.rsqrt(jnp.mean(x * x, axis=-1, keepdims=True) + EPS)


def rms(x, gain):
    return x * inverse_rms(x) * gain


def rms_back(dy, x, gain):
    r = inverse_rms(x)
    gy = gain * dy
    dx = r * gy - x * (r * r * r) * jnp.mean(gy * x, axis=-1, keepdims=True)
    return dx, jnp.sum(dy * x * r, axis=0, keepdims=True)


def gelu_pair(x):
    t = jnp.tanh(GELU_B * (x + GELU_A * x * x * x))
    half = 0.5 * (1.0 + t)
    slope = half + 0.5 * x * (1.0 - t * t) * (GELU_B * (1.0 + 3.0 * GELU_A * x * x))
    return x * half, slope


def column(row):
    wide = jnp.broadcast_to(row.astype(F32), (128, row.shape[1]))
    return jnp.transpose(wide)[:, 0:1]


def chunks(extent):
    width = 384 if extent % 384 == 0 else extent
    return [(at, width) for at in range(0, extent, width)]


def build(S, n, T, D, W, F, R, groups):
    rest = S // 2
    Y = 2 ** ((rest.bit_length() - 1) // 2)
    Z = rest // Y
    ZY = Z * Y
    H = W // HD
    LEVEL = 2 * Y
    CH = LEVEL * T
    GN = R // T
    RH = R // GN
    RB = R // S
    DM = D // n
    DR = D // S
    DRP = -(-DR // 16) * 16
    Q = ZY * DRP
    XW = {"down": F, "up": F, "proj": W, "qkv": 3 * W}

    target = np.full((2, 1, Q), -1, np.int32)
    for core in range(2):
        for yy in range(Y):
            for zz in range(Z):
                for j in range(DR):
                    target[core, 0, (yy * Z + zz) * DRP + j] = ((zz * Y + yy) * 2 + core) * DR + j

    ins = ["inp", "segr", "picks", "gains", "router", "cot", "target", "qkv_h", "proj_h", "up_h", "down_h"]
    outs = {
        "ro_o": ((T, D), BF),
        "do_o": ((T, D), BF),
        "gi_o": ((T, D), F32),
        "sm_o": ((8, 128), F32),
        "rg_o": ((2, D), F32),
        "qkv_o": ((2, 3, DR, W), F32),
        "proj_o": ((2, DR, W), F32),
        "up_o": ((2, DR, F), F32),
        "down_o": ((2, DR, F), F32),
    }
    vm = {
        "wq": ((2, 3, D, W), BF),
        "wp": ((2, W, D), BF),
        "wu": ((2, D, F), BF),
        "wd": ((2, F, D), BF),
        "sega": ((S, 8, T), jnp.int32),
        "segc": ((T, 1), F32),
        "oht": ((T, R), BF),
        "oh": ((R, T), BF),
        "posr": ((GN // 2, 8, 2 * RH), F32),
        "posc": ((RH, 1), F32),
        "sgr": ((GN // 2, 8, 2 * RH), F32),
        "sgc": ((RH, 1), F32),
        "part": ((S, RB, DM), BF),
        "r1": ((S, RB, DM), BF),
        "full": ((2, n * ZY, RB, DM), BF),
        "rows": ((R, D), BF),
        "nr": ((RH, D), BF),
        "chh": ((RH, D), BF),
        "qr": ((R, W), BF),
        "kr": ((R, W), BF),
        "vr": ((R, W), BF),
        "mr": ((H, RH, 1), F32),
        "lr": ((H, RH, 1), F32),
        "ar": ((H, RH, HD), F32),
        "mixr": ((RH, W), BF),
        "attr": ((RH, D), F32),
        "n2r": ((RH, D), BF),
        "prer": ((RH, F), F32),
        "actr": ((RH, F), BF),
        "xr": ((2, n, RH, D), BF),
        "xd": ((3, n, T, D), BF),
        "chg": ((GN, RH, D), BF),
        "sel": ((T, D), BF),
        "ro": ((T, D), F32),
        "nd": ((T, D), BF),
        "kva": ((S, T, 2 * W), BF),
        "qa": ((S, T, W), BF),
        "da": ((S, T, W), BF),
        "sta": ((S, 16, T), F32),
        "md": ((H, T, 1), F32),
        "ld": ((H, T, 1), F32),
        "ad": ((H, T, HD), F32),
        "mixd": ((T, W), BF),
        "hid": ((T, D), F32),
        "n2d": ((T, D), BF),
        "dact": ((T, F), F32),
        "actd": ((T, F), BF),
        "dpre": ((T, F), BF),
        "dattn": ((T, D), BF),
        "dq": ((H, max(T, RH), HD), F32),
        "dk": ((H, max(T, RH), HD), F32),
        "dv": ((H, max(T, RH), HD), F32),
        "g3": ((T, 3 * W), BF),
        "dro": ((T, D), F32),
        "small": ((8, D), F32),
        "sblk": ((S, 8, 128), F32),
        "srec": ((S, 8, 128), F32),
        "dor": ((GN, RH, W), BF),
        "str": ((GN, 16, RH), F32),
        "dprer": ((RH, F), BF),
        "dattr": ((RH, D), BF),
        "g3r": ((RH, 3 * W), BF),
        "gr": ((GN, 8, D), F32),
        "sele": ((2, D, Q), BF),
    }
    for k in KINDS:
        X = XW[k]
        vm["keep_" + k] = ((Y, Z, DRP, X), F32)
        vm["send_" + k] = ((Y, Z, DRP, X), BF)
        vm["sibr_" + k] = ((Y, Z, DRP, X), BF)
        vm["yrec_" + k] = ((Y - 1, Z, DRP, X), BF)
        vm["zrec_" + k] = ((Z - 1, DRP, X), BF)
        vm["rsend_" + k] = ((GN - 1, DRP, X), BF)
        vm["rkeep_" + k] = ((DRP, X), F32)
        vm["rrec_" + k] = ((GN - 1, DRP, X), BF)
    n_sends = (Z - 1) + (Y - 1) + 1 + (Z - 1) * Y + Z * (Y - 1)
    sems = {
        "w_s": (8,),
        "seg_s": (2,),
        "t_s": (6,),
        "xr_s": (2, n - 1),
        "xr_r": (2, n - 1),
        "xd_s": (3, n - 1),
        "xd_r": (3, n - 1),
        "sw_s": (10, GN - 1),
        "sw_r": (10, GN - 1),
        "kv_s": (n_sends,),
        "kv_r": (S,),
        "q_s": (n_sends,),
        "q_r": (S,),
        "da_s": (n_sends,),
        "da_r": (S,),
        "st_s": (n_sends,),
        "st_r": (S,),
        "sm_s": (2,),
        "gs_s": (4,),
        "gs_r": (4,),
        "gy_s": (4, Y - 1),
        "gy_r": (4, Y - 1),
        "gz_s": (4, Z - 1),
        "gz_r": (4, Z - 1),
    }
    names = ins + list(outs) + list(vm) + list(sems)

    def kernel(*refs):
        r = SimpleNamespace(**dict(zip(names, refs, strict=True)))
        g = r.__dict__
        s = lax.axis_index("seq")
        m = lax.axis_index("mlp")
        c = lax.rem(s, 2)
        chip = s // 2
        y = lax.rem(chip, Y)
        z = chip // Y
        sib = s + 1 - 2 * c
        gi = lax.rem(s, GN)

        def rank(zz, yy, cc):
            return (zz * Y + yy) * 2 + cc

        def remote(src, dst, send, recv, seq, mlp):
            return pltpu.make_async_remote_copy(
                src_ref=src, dst_ref=dst, send_sem=send, recv_sem=recv, device_id=(seq, mlp), device_id_type=MESH
            )

        bar = pltpu.get_barrier_semaphore()

        def greet(i, carry):
            pl.semaphore_signal(bar, inc=1, device_id=(lax.rem(s + i, S), m), device_id_type=MESH)
            return carry

        lax.fori_loop(1, S, greet, 0)
        for j in range(1, n):

            def greet_other(i, carry, j=j):
                pl.semaphore_signal(bar, inc=1, device_id=(i * 2 + c, lax.rem(m + j, n)), device_id_type=MESH)
                return carry

            lax.fori_loop(0, ZY, greet_other, 0)
        loads = [
            pltpu.make_async_copy(src.at[b], dst.at[b], r.w_s.at[4 * b + i])
            for b in range(2)
            for i, (src, dst) in enumerate(
                ((r.qkv_h, r.wq), (r.proj_h, r.wp), (r.up_h, r.wu), (r.down_h, r.wd))
            )
        ]
        prow = jnp.concatenate([r.picks[i : i + 1, :] + G * i for i in range(groups)], axis=1)
        here = s * T + lax.broadcasted_iota(jnp.int32, (T, R), 0)
        hot = jnp.where(prow == here, 1.0, 0.0)
        r.oht[...] = hot.astype(BF)
        r.oh[...] = jnp.transpose(hot).astype(BF)

        def my_columns(x):
            got = x[:, 0:DM]
            for j in range(1, n):
                got = jnp.where(m == j, x[:, j * DM : (j + 1) * DM], got)
            return got

        def scatter_rows(x):
            r.part[...] = nn(r.oh[...], my_columns(x)).astype(BF).reshape(S, RB, DM)

        scatter_rows(r.inp[...])
        def send_segments(i, carry):
            remote(r.sega.at[s], r.sega.at[s], r.seg_s.at[0], r.seg_s.at[1], lax.rem(s + i, S), m).start()
            return carry

        sem = [r.t_s.at[j] for j in range(6)]

        def spread_start():
            def first(k, carry):
                p = lax.rem(s + k, S)
                remote(r.part.at[p], r.r1.at[s], sem[0], sem[1], p, m).start()
                return carry

            lax.fori_loop(1, S, first, 0)
            r.r1[s] = r.part[s]

        def spread_end(after):
            some = pl.ds(0, S - 1)
            remote(r.part.at[some], r.r1.at[some], sem[0], sem[1], s, m).wait()
            me = m * ZY + chip
            r.full[c, me] = jnp.sum(r.r1[...].astype(F32), axis=0).astype(BF)

            def second(k, carry):
                p = lax.rem(me + k, n * ZY)
                block = r.full.at[c, me]
                remote(block, block, sem[2], sem[3], lax.rem(p, ZY) * 2 + c, p // ZY).start()
                return carry

            lax.fori_loop(1, n * ZY, second, 0)
            after()
            some = r.full.at[c, pl.ds(0, n * ZY - 1)]
            remote(some, some, sem[2], sem[3], s, m).wait()
            swap = remote(r.full.at[c], r.full.at[c], sem[4], sem[5], sib, m)
            swap.start()
            swap.wait()

            def place(k, carry):
                for cc in range(2):
                    rows = pl.ds(pl.multiple_of((k * 2 + cc) * RB, RB), RB)
                    for mm in range(n):
                        r.rows[rows, mm * DM : (mm + 1) * DM] = r.full[cc, mm * ZY + k]
                return carry

            lax.fori_loop(0, ZY, place, 0)

        def mlp_copies(buf, send, recv, i):
            i = i % buf.shape[0]
            return [
                remote(buf.at[i, m], buf.at[i, m], send.at[i, j - 1], recv.at[i, j - 1], s, lax.rem(m + j, n))
                for j in range(1, n)
            ]

        def mlp_start(which, i, value):
            buf = g["x" + which]
            buf[i % buf.shape[0], m] = value.astype(BF)
            for copy in mlp_copies(buf, g["x" + which + "_s"], g["x" + which + "_r"], i):
                copy.start()

        def mlp_total(which, i):
            buf = g["x" + which]
            for copy in mlp_copies(buf, g["x" + which + "_s"], g["x" + which + "_r"], i):
                copy.wait()
            i = i % buf.shape[0]
            total = buf[i, 0].astype(F32)
            for j in range(1, n):
                total = total + buf[i, j].astype(F32)
            return total

        def friend(j):
            return s - gi + lax.rem(gi + j, GN)

        def share(i, *refs):
            return [
                remote(ref.at[gi], ref.at[gi], r.sw_s.at[i + k, j - 1], r.sw_r.at[i + k, j - 1], friend(j), m)
                for k, ref in enumerate(refs)
                for j in range(1, GN)
            ]

        def attend_start(top, total, acc):
            top[...] = jnp.full(top.shape, NEG, F32)
            total[...] = jnp.zeros(total.shape, F32)
            acc[...] = jnp.zeros(acc.shape, F32)

        def head_groups(width):
            step = min(H, max(1, WIDE // width))
            return [range(at, min(at + step, H)) for at in range(0, H, step)]

        def attend(ci, query, key, value, mask, top, total, acc):
            kept = mask(ci)
            for group in head_groups(kept.shape[1]):
                scores = {h: nt(query(h), key(ci, h)) for h in group}
                weights = {}
                for h in group:
                    score = jnp.where(kept, scores[h], NEG)
                    old = top[h]
                    new = jnp.maximum(old, jnp.max(score, axis=-1, keepdims=True))
                    shrink = jnp.exp(old - new)
                    weight = jnp.exp(score - new)
                    total[h] = total[h] * shrink + jnp.sum(weight, axis=-1, keepdims=True)
                    acc[h] = acc[h] * shrink
                    top[h] = new
                    weights[h] = weight.astype(BF)
                for h in group:
                    acc[h] = acc[h] + nn(weights[h], value(ci, h))

        def finish(top, total, acc, mixed):
            for h in range(H):
                out = acc[h] / total[h]
                acc[h] = out
                mixed[:, h * HD : (h + 1) * HD] = out.astype(BF)
                top[h] = top[h] + jnp.log(total[h])

        def row_stats(grad, top, total, acc):
            lane = lax.broadcasted_iota(jnp.int32, (acc.shape[1], 128), 1)
            stats = jnp.zeros((acc.shape[1], 128), F32)
            for h in range(H):
                delta = jnp.sum(grad(h).astype(F32) * acc[h], axis=-1, keepdims=True)
                total[h] = delta
                stats = jnp.where(lane == h, top[h], jnp.where(lane == 8 + h, delta, stats))
            return jnp.transpose(stats)[0:16]

        def back_query(ci, query, grad, key, value, mask, log_total, delta, out):
            kept = mask(ci)
            for group in head_groups(kept.shape[1]):
                scores = {h: nt(query(h), key(ci, h)) for h in group}
                grad_probs = {h: nt(grad(h), value(ci, h)) for h in group}
                grad_scores = {}
                for h in group:
                    probs = jnp.where(kept, jnp.exp(scores[h] - log_total[h]), 0.0)
                    grad_scores[h] = (probs * (grad_probs[h] - delta[h])).astype(BF)
                for h in group:
                    out[h] = out[h] + nn(grad_scores[h], key(ci, h))

        def back_keys(ci, key, value, query, grad, mask, stat, out_key, out_value):
            kept = mask(ci)
            for group in head_groups(kept.shape[1]):
                scores = {h: nt(key(h), query(ci, h)) for h in group}
                grad_probs = {h: nt(value(h), grad(ci, h)) for h in group}
                probs, grad_scores = {}, {}
                for h in group:
                    prob = jnp.where(kept, jnp.exp(scores[h] - stat(ci, h)), 0.0)
                    grad_scores[h] = (prob * (grad_probs[h] - stat(ci, 8 + h))).astype(BF)
                    probs[h] = prob.astype(BF)
                for h in group:
                    out_value[h] = out_value[h] + nn(probs[h], grad(ci, h))
                    out_key[h] = out_key[h] + nn(grad_scores[h], query(ci, h))

        dq_d, dk_d, dv_d = (ref.at[:, 0:T] for ref in (r.dq, r.dk, r.dv))
        dq_r, dk_r, dv_r = (ref.at[:, 0:RH] for ref in (r.dq, r.dk, r.dv))

        def pack_grads(dq, dk, dv, out):
            for h in range(H):
                out[:, h * HD : (h + 1) * HD] = (dq[h] * SCALE).astype(BF)
                out[:, W + h * HD : W + (h + 1) * HD] = dk[h].astype(BF)
                out[:, 2 * W + h * HD : 2 * W + (h + 1) * HD] = dv[h].astype(BF)

        def front_back(grads, b):
            return (
                nt(grads[:, 0:W], r.wq[b, 0])
                + nt(grads[:, W : 2 * W], r.wq[b, 1])
                + nt(grads[:, 2 * W : 3 * W], r.wq[b, 2])
            )

        def loop(low, high, body):
            def step(i, carry):
                body(i)
                return carry

            lax.fori_loop(low, high, step, 0)

        def gather(buf, ss, rs, up):
            sign = -1 if up else 1
            last = z if up else Z - 1 - z
            ahead = Z - 1 - z if up else z
            at_y, at_sib, at_level = Z - 1, Z + Y - 2, Z + Y - 1
            at_z = at_level + Y - 1
            at_far = at_z + (Z - 1) * Y

            def copy(slot, dst, k):
                return remote(buf.at[slot], buf.at[slot], ss.at[k], rs.at[slot], dst, m)

            def recv(slot):
                copy(slot, sib, 0).wait_recv()

            def side(dy):
                return lax.rem(y + dy, Y)

            def copies(each):
                loop(1, ahead + 1, lambda dz: each(copy(s, rank(z - sign * dz, y, c), dz - 1)))
                for dy in range(1, Y):
                    each(copy(s, rank(z, side(dy), c), at_y + dy - 1))
                each(copy(s, sib, at_sib))

            def level_copy(dy):
                return copy(rank(z, side(dy), c), sib, at_level + dy - 1)

            def z_copies(dz):
                slot = rank(z + sign * dz, y, c)
                k = at_z + (dz - 1) * Y
                outs = [copy(slot, rank(z, side(dy), c), k + dy - 1) for dy in range(1, Y)]
                return [*outs, copy(slot, sib, k + Y - 1)]

            def far_copy(dz, dy):
                return copy(rank(z + sign * dz, side(dy), c), sib, at_far + (dz - 1) * (Y - 1) + dy - 1)

            def start():
                copies(lambda one: one.start())

            def level():
                for dy in range(1, Y):
                    recv(rank(z, side(dy), c))
                    level_copy(dy).start()

            def level_end():
                for dy in range(Y):
                    recv(rank(z, side(dy), 1 - c))

            def z_step(dz):
                recv(rank(z + sign * dz, y, c))
                for one in z_copies(dz):
                    one.start()

            def y_step(dz):
                for dy in range(1, Y):
                    recv(rank(z + sign * dz, side(dy), c))
                    far_copy(dz, dy).start()

            def sib_step(dz):
                for dy in range(Y):
                    recv(rank(z + sign * dz, side(dy), 1 - c))

            def end():
                copies(lambda one: one.wait_send())
                for dy in range(1, Y):
                    level_copy(dy).wait_send()

                def sent(dz):
                    for one in z_copies(dz):
                        one.wait_send()
                    for dy in range(1, Y):
                        far_copy(dz, dy).wait_send()

                loop(1, last + 1, sent)

            return SimpleNamespace(
                start=start,
                level=level,
                level_end=level_end,
                z_step=z_step,
                y_step=y_step,
                sib_step=sib_step,
                end=end,
                last=last,
            )

        def walk(items, body):
            last = items[0].last

            def all_of(name, *args):
                for item in items:
                    getattr(item, name)(*args)

            pl.when(last > 0)(lambda: all_of("z_step", 1))
            all_of("level_end")
            body(0)

            def step(dz):
                all_of("y_step", dz)
                pl.when(dz < last)(lambda: all_of("z_step", dz + 1))
                all_of("sib_step", dz)
                body(dz)

            loop(1, last + 1, step)

        def sum_start(k, lhs, rhs):
            i = KINDS.index(k)
            out = nn(lhs[...], r.sele[1 - c]).astype(BF)
            stay = nn(lhs[...], r.sele[c]).astype(BF)
            for x, w in chunks(XW[k]):
                g["send_" + k][:, :, :, x : x + w] = tn(out, rhs[:, x : x + w]).astype(BF).reshape(Y, Z, DRP, w)
            remote(g["send_" + k], g["sibr_" + k], r.gs_s.at[i], r.gs_r.at[i], sib, m).start()
            for x, w in chunks(XW[k]):
                g["keep_" + k][:, :, :, x : x + w] = tn(stay, rhs[:, x : x + w]).reshape(Y, Z, DRP, w)

        def y_copy(k, i, dy):
            return remote(
                g["sibr_" + k].at[lax.rem(y + dy, Y)],
                g["yrec_" + k].at[dy - 1],
                r.gy_s.at[i, dy - 1],
                r.gy_r.at[i, dy - 1],
                rank(z, lax.rem(y + dy, Y), c),
                m,
            )

        def z_copy(k, i, dz):
            return remote(
                g["yrec_" + k].at[0, lax.rem(z + dz, Z)],
                g["zrec_" + k].at[dz - 1],
                r.gz_s.at[i, dz - 1],
                r.gz_r.at[i, dz - 1],
                rank(lax.rem(z + dz, Z), y, c),
                m,
            )

        def sum_y(k):
            i = KINDS.index(k)
            remote(g["send_" + k], g["sibr_" + k], r.gs_s.at[i], r.gs_r.at[i], sib, m).wait()
            for dy in range(1, Y):
                yy = lax.rem(y + dy, Y)
                g["sibr_" + k][yy] = (g["keep_" + k][yy] + g["sibr_" + k][yy].astype(F32)).astype(BF)
                y_copy(k, i, dy).start()

        def sum_z(k):
            i = KINDS.index(k)
            for dy in range(1, Y):
                y_copy(k, i, dy).wait()

            def total(zz):
                t = g["keep_" + k][y, zz] + g["sibr_" + k][y, zz].astype(F32)
                for dy in range(1, Y):
                    t = t + g["yrec_" + k][dy - 1, zz].astype(F32)
                return t

            for dz in range(1, Z):
                zz = lax.rem(z + dz, Z)
                g["yrec_" + k][0, zz] = total(zz).astype(BF)
                z_copy(k, i, dz).start()
            g["keep_" + k][y, z] = total(z)

        def put(b, k, value):
            if k == "qkv":
                for j in range(3):
                    r.qkv_o[b, j] = value[0:DR, j * W : (j + 1) * W]
            else:
                g[k + "_o"][b] = value[0:DR]

        def sum_end(k):
            i = KINDS.index(k)
            t = g["keep_" + k][y, z]
            for dz in range(1, Z):
                z_copy(k, i, dz).wait()
                t = t + g["zrec_" + k][dz - 1].astype(F32)
            put(1, k, t)

        def routed_copy(k, j):
            i = 6 + KINDS.index(k)
            send, recv = r.sw_s.at[i, j - 1], r.sw_r.at[i, j - 1]
            return remote(g["rsend_" + k].at[j - 1], g["rrec_" + k].at[j - 1], send, recv, friend(j), m)

        def routed_start(k, lhs, rhs):
            col = lax.broadcasted_iota(jnp.int32, (D, DRP), 1)
            row = lax.broadcasted_iota(jnp.int32, (D, DRP), 0)

            def block(who):
                hit = (row - who * DR == col) & (col < DR)
                return nn(lhs, jnp.where(hit, 1.0, 0.0).astype(BF)).astype(BF)

            for j in range(1, GN):
                g["rsend_" + k][j - 1] = tn(block(friend(j)), rhs).astype(BF)
                routed_copy(k, j).start()
            g["rkeep_" + k][...] = tn(block(s), rhs)

        def routed_end(k):
            t = g["rkeep_" + k][...]
            for j in range(1, GN):
                routed_copy(k, j).wait()
                t = t + g["rrec_" + k][j - 1].astype(F32)
            put(0, k, t)

        def head(h):
            return slice(h * HD, (h + 1) * HD)

        pl.semaphore_wait(bar, S - 1 + (n - 1) * ZY)
        spread_start()
        r.sega[s] = jnp.broadcast_to(r.segr[...], (8, T))
        for load in loads:
            load.start()
        prow_f = prow.astype(F32)
        for i in range(GN // 2):
            r.posr[i] = jnp.broadcast_to(prow_f[:, i * 2 * RH : (i + 1) * 2 * RH], (8, 2 * RH))
        mine = r.posr[gi // 2][0:1]
        r.posc[...] = column(jnp.where(lax.rem(gi, 2) == 0, mine[:, 0:RH], mine[:, RH : 2 * RH]))
        r.segc[...] = column(r.segr[...])
        for par in range(2):
            ids = lax.broadcasted_iota(jnp.int32, (D, Q), 0)
            r.sele[par] = jnp.where(ids == r.target[par], 1.0, 0.0).astype(BF)
        spread_end(lambda: lax.fori_loop(1, S, send_segments, 0))
        some = pl.ds(0, S - 1)
        remote(r.sega.at[some], r.sega.at[some], r.seg_s.at[0], r.seg_s.at[1], s, m).wait()
        starts = [
            jnp.sum(
                jnp.sum(jnp.where(r.sega[...] < k, 0.125, 0.0), axis=0), axis=(0, 1), keepdims=True
            )
            for k in range(1, 5)
        ]
        for i in range(GN // 2):
            r.sgr[i] = sum(jnp.where(r.posr[i] >= at, 1.0, 0.0) for at in starts)
        r.sgc[...] = sum(jnp.where(r.posc[...] >= at, 1.0, 0.0) for at in starts)
        half = pl.ds(pl.multiple_of(gi * RH, RH), RH)

        loads[0].wait()
        r.chh[...] = r.rows[half, :]
        r.nr[...] = rms(r.chh[...].astype(F32), r.gains[0, 0:1]).astype(BF)
        for at in range(0, R, 256):
            part = slice(at, at + 256)
            normed = rms(r.rows[part].astype(F32), r.gains[0, 0:1]).astype(BF)
            r.qr[part] = (nn(normed, r.wq[0, 0]).astype(BF) * SCALE).astype(BF)
            r.kr[part] = nn(normed, r.wq[0, 1]).astype(BF)
            r.vr[part] = nn(normed, r.wq[0, 2]).astype(BF)

        def part_rows(ref):
            return lambda ci, h: ref[pl.ds(pl.multiple_of(ci * 2 * RH, RH), 2 * RH), head(h)]

        def half_rows(ref):
            return lambda h: ref[half, head(h)]

        def routed_mask(ci):
            return (r.sgr[ci][0:1] == r.sgc[...]) & (r.posr[ci][0:1] <= r.posc[...])

        def routed_mask_back(ci):
            return (r.sgr[ci][0:1] == r.sgc[...]) & (r.posc[...] <= r.posr[ci][0:1])

        def routed_pick(i):
            return lax.rem(gi // 2 + i, GN // 2)

        def routed_loop(body):
            if GN == 2:
                body(0)
            else:
                loop(0, GN // 2, lambda i: body(routed_pick(i)))

        attend_start(r.mr, r.lr, r.ar)
        routed_loop(
            lambda ci: attend(
                ci, half_rows(r.qr), part_rows(r.kr), part_rows(r.vr), routed_mask, r.mr, r.lr, r.ar
            )
        )
        finish(r.mr, r.lr, r.ar, r.mixr)
        loads[1].wait()
        mlp_start("r", 0, nn(r.mixr[...], r.wp[0]))
        loads[2].wait()
        loads[3].wait()
        attn = mlp_total("r", 0)
        r.attr[...] = attn
        normed = rms(r.chh[...].astype(F32) + attn, r.gains[0, 1:2]).astype(BF)
        r.n2r[...] = normed
        for x, w in chunks(F):
            pre = nn(normed, r.wu[0, :, x : x + w])
            r.prer[:, x : x + w] = pre
            r.actr[:, x : x + w] = gelu_pair(pre)[0].astype(BF)
        mlp_start("r", 1, nn(r.actr[...], r.wd[0]))
        mlp = mlp_total("r", 1)
        r.chg[gi] = (r.attr[...] + mlp).astype(BF)
        swaps = share(0, r.chg)
        for copy in swaps:
            copy.start()
        inp = r.inp[...].astype(F32)
        gate = jax.nn.sigmoid(jnp.sum(inp * r.router[...].reshape(1, D), axis=-1, keepdims=True))
        for load in loads[4:]:
            load.wait()
        for copy in swaps:
            copy.wait()

        sel = nn(r.oht[...], r.chg[...].reshape(R, D))
        r.sel[...] = sel.astype(BF)
        ro = inp + gate * sel
        r.ro[...] = ro
        r.ro_o[...] = ro.astype(BF)
        normed = rms(ro, r.gains[1, 0:1]).astype(BF)
        r.nd[...] = normed
        r.kva[s, :, 0:W] = nn(normed, r.wq[1, 1]).astype(BF)
        r.kva[s, :, W : 2 * W] = nn(normed, r.wq[1, 2]).astype(BF)
        keys_all = gather(r.kva, r.kv_s, r.kv_r, True)
        keys_all.start()
        r.qa[s] = (nn(normed, r.wq[1, 0]).astype(BF) * SCALE).astype(BF)
        query_all = gather(r.qa, r.q_s, r.q_r, False)
        query_all.start()
        keys_all.level()
        query_all.level()

        def level_rows(ref, first=0):
            def get(ci, h):
                return ref[pl.ds(ci * LEVEL, LEVEL), :, head(first + h)].reshape(CH, HD)

            return get

        def level_line(ref, line):
            return lambda ci: jnp.concatenate([ref[ci * LEVEL + j][line : line + 1] for j in range(LEVEL)], axis=1)

        own_pos = lax.broadcasted_iota(jnp.int32, (T, CH), 0) + s * T
        far_pos = lax.broadcasted_iota(jnp.int32, (T, CH), 1)
        seg_line = level_line(r.sega, 0)

        def dense_mask(ci):
            return (seg_line(ci).astype(F32) == r.segc[...]) & (far_pos + ci * CH <= own_pos)

        def dense_mask_back(ci):
            return (seg_line(ci).astype(F32) == r.segc[...]) & (own_pos <= far_pos + ci * CH)

        attend_start(r.md, r.ld, r.ad)
        walk(
            [keys_all],
            lambda dz: attend(
                z - dz,
                lambda h: r.qa[s, :, head(h)],
                level_rows(r.kva),
                level_rows(r.kva, H),
                dense_mask,
                r.md,
                r.ld,
                r.ad,
            ),
        )
        finish(r.md, r.ld, r.ad, r.mixd)
        mlp_start("d", 0, nn(r.mixd[...], r.wp[1]))
        loop(1, query_all.last + 1, query_all.z_step)
        for x, w in chunks(F):
            r.dact[:, x : x + w] = nt(r.cot[...], r.wd[1, x : x + w, :])
        attn = mlp_total("d", 0)
        hid = r.ro[...] + attn
        r.hid[...] = hid
        normed = rms(hid, r.gains[1, 1:2]).astype(BF)
        r.n2d[...] = normed
        for x, w in chunks(F):
            active, slope = gelu_pair(nn(normed, r.wu[1, :, x : x + w]))
            r.actd[:, x : x + w] = active.astype(BF)
            r.dpre[:, x : x + w] = (r.dact[:, x : x + w] * slope).astype(BF)
        mlp_start("d", 1, nt(r.dpre[...], r.wu[1]))
        mlp_start("d", 2, nn(r.actd[...], r.wd[1]))

        sum_start("down", r.cot, r.actd)
        sum_start("up", r.n2d, r.dpre)
        loop(1, query_all.last + 1, query_all.y_step)
        dn, dg = rms_back(mlp_total("d", 1), r.hid[...], r.gains[1, 1:2])
        r.small[1:2] = dg
        dhid = r.cot[...].astype(F32) + dn
        r.dro[...] = dhid
        r.dattn[...] = dhid.astype(BF)
        r.da[s] = nt(r.dattn[...], r.wp[1]).astype(BF)
        r.sta[s] = row_stats(lambda h: r.da[s, :, head(h)], r.md, r.ld, r.ad)
        grad_all = gather(r.da, r.da_s, r.da_r, False)
        stat_all = gather(r.sta, r.st_s, r.st_r, False)
        for item in (grad_all, stat_all):
            item.start()
        for item in (grad_all, stat_all):
            item.level()
        query_all.level_end()
        loop(1, query_all.last + 1, query_all.sib_step)
        dq_d[...] = jnp.zeros((H, T, HD), F32)
        dk_d[...] = jnp.zeros((H, T, HD), F32)
        dv_d[...] = jnp.zeros((H, T, HD), F32)
        loop(
            0,
            z + 1,
            lambda dz: back_query(
                z - dz,
                lambda h: r.qa[s, :, head(h)],
                lambda h: r.da[s, :, head(h)],
                level_rows(r.kva),
                level_rows(r.kva, H),
                dense_mask,
                r.md,
                r.ld,
                dq_d,
            ),
        )
        sum_y("down")
        walk(
            [grad_all, stat_all],
            lambda dz: back_keys(
                z + dz,
                lambda h: r.kva[s, :, head(h)],
                lambda h: r.kva[s, :, head(H + h)],
                level_rows(r.qa),
                level_rows(r.da),
                dense_mask_back,
                lambda ci, line: level_line(r.sta, line)(ci),
                dk_d,
                dv_d,
            ),
        )
        sum_y("up")
        pack_grads(dq_d, dk_d, dv_d, r.g3)
        mlp_start("d", 3, front_back(r.g3, 1))
        sum_start("qkv", r.nd, r.g3)
        sum_start("proj", r.dattn, r.mixd)
        sum_z("down")
        dn, dg = rms_back(mlp_total("d", 3), r.ro[...], r.gains[1, 0:1])
        r.small[0:1] = dg
        dro = r.dro[...] + dn
        r.dro[...] = dro

        sel = r.sel[...].astype(F32)
        inp = r.inp[...].astype(F32)
        gate = jax.nn.sigmoid(jnp.sum(inp * r.router[...].reshape(1, D), axis=-1, keepdims=True))
        dlogit = jnp.sum(dro * sel, axis=-1, keepdims=True) * gate * (1.0 - gate)
        scatter_rows((gate * dro).astype(BF))
        spread_start()
        spread_end(lambda: None)
        r.small[2:3] = jnp.sum(inp * dlogit, axis=0, keepdims=True)
        r.small[3:8] = jnp.zeros((5, D), F32)
        r.sblk[...] = jnp.zeros((S, 8, 128), F32)
        for p in range(S):
            r.sblk[p, :, 0:DR] = r.small[:, p * DR : (p + 1) * DR]

        def send_small(i, carry):
            p = lax.rem(s + i, S)
            remote(r.sblk.at[p], r.srec.at[s], r.sm_s.at[0], r.sm_s.at[1], p, m).start()
            return carry

        lax.fori_loop(1, S, send_small, 0)
        r.srec[s] = r.sblk[s]
        sum_y("qkv")
        sum_y("proj")

        dmlp = r.rows[half, :]
        r.attr[...] = r.attr[...] + r.chh[...].astype(F32)
        for x, w in chunks(F):
            grad_active = nt(dmlp, r.wd[0, x : x + w, :])
            r.dprer[:, x : x + w] = (grad_active * gelu_pair(r.prer[:, x : x + w])[1]).astype(BF)
        mlp_start("r", 2, nt(r.dprer[...], r.wu[0]))
        routed_start("down", dmlp, r.actr[...])
        routed_start("up", r.n2r[...], r.dprer[...])
        dn, dg2 = rms_back(mlp_total("r", 2), r.attr[...], r.gains[0, 1:2])
        r.attr[...] = dn
        r.dattr[...] = (dmlp.astype(F32) + dn).astype(BF)
        r.dor[gi] = nt(r.dattr[...], r.wp[0]).astype(BF)
        r.str[gi] = row_stats(lambda h: r.dor[gi, :, head(h)], r.mr, r.lr, r.ar)
        swaps = share(1, r.dor, r.str)
        for copy in swaps:
            copy.start()
        routed_start("proj", r.dattr[...], r.mixr[...])
        sum_z("up")
        dq_r[...] = jnp.zeros((H, RH, HD), F32)
        dk_r[...] = jnp.zeros((H, RH, HD), F32)
        dv_r[...] = jnp.zeros((H, RH, HD), F32)
        routed_loop(
            lambda ci: back_query(
                ci,
                half_rows(r.qr),
                lambda h: r.dor[gi, :, head(h)],
                part_rows(r.kr),
                part_rows(r.vr),
                routed_mask,
                r.mr,
                r.lr,
                dq_r,
            )
        )
        for copy in swaps:
            copy.wait()
        routed_loop(
            lambda ci: back_keys(
                ci,
                half_rows(r.kr),
                half_rows(r.vr),
                part_rows(r.qr),
                lambda ci, h: r.dor[pl.ds(ci * 2, 2), :, head(h)].reshape(2 * RH, HD),
                routed_mask_back,
                lambda ci, line: jnp.concatenate([r.str[ci * 2 + j][line : line + 1] for j in range(2)], axis=1),
                dk_r,
                dv_r,
            )
        )
        pack_grads(dq_r, dk_r, dv_r, r.g3r)
        mlp_start("r", 3, front_back(r.g3r, 0))
        routed_start("qkv", r.nr[...], r.g3r[...])
        sum_end("down")
        sum_z("qkv")
        sum_z("proj")
        dn, dg1 = rms_back(mlp_total("r", 3), r.chh[...].astype(F32), r.gains[0, 0:1])
        r.chg[gi] = (r.attr[...] + dn).astype(BF)
        r.gr[gi] = jnp.concatenate([dg1, dg2, jnp.zeros((6, D), F32)], axis=0)
        swaps = share(3, r.chg, r.gr)
        for copy in swaps:
            copy.start()
        for copy in swaps:
            copy.wait()
        r.rg_o[...] = jnp.sum(r.gr[...], axis=0)[0:2]
        back = nn(r.oht[...], r.chg[...].reshape(R, D))
        inp = r.inp[...].astype(F32)
        gate = jax.nn.sigmoid(jnp.sum(inp * r.router[...].reshape(1, D), axis=-1, keepdims=True))
        dlogit = jnp.sum(r.dro[...] * r.sel[...].astype(F32), axis=-1, keepdims=True) * gate * (1.0 - gate)
        r.gi_o[...] = r.dro[...] + back + dlogit * r.router[...].reshape(1, D)

        r.do_o[...] = (r.hid[...] + mlp_total("d", 2)).astype(BF)
        some = pl.ds(0, S - 1)
        remote(r.sblk.at[some], r.srec.at[some], r.sm_s.at[0], r.sm_s.at[1], s, m).wait()
        r.sm_o[...] = jnp.sum(r.srec[...], axis=0)
        for k in KINDS:
            routed_end(k)
        for k in ("up", "qkv", "proj"):
            sum_end(k)
        for item in (keys_all, query_all, grad_all, stat_all):
            item.end()

    def layout(*refs):
        moved = [refs[i] for i in (0, 1, 2, 5, 6, 7, 8)]
        sm, rg = refs[3:5]
        moved_o = [refs[9 + i] for i in (0, 1, 2, 5, 6, 7, 8)]
        gains_o, router_o = refs[12:14]
        held, sems = refs[18:25], refs[25]
        ways = [
            (pltpu.make_async_copy(a, v, sems.at[0, i]), pltpu.make_async_copy(v, b, sems.at[1, i]))
            for i, (a, v, b) in enumerate(zip(moved, held, moved_o))
        ]
        for into, _ in ways:
            into.start()
        s = lax.axis_index("seq")
        routed = rg[:, 0:DR]
        for p in range(1, S):
            routed = jnp.where(s == p, rg[:, p * DR : (p + 1) * DR], routed)
        gains_o[0] = routed
        gains_o[1] = sm[0:2, 0:DR]
        router_o[...] = sm[2:3, 0:DR]
        for into, out in ways:
            into.wait()
            out.start()
        for _, out in ways:
            out.wait()

    def run(inp, segments, picks, gains, router, qkv, proj, up, down, cot):
        args = (
            inp,
            segments.reshape(1, T),
            picks,
            gains,
            router,
            cot,
            jnp.asarray(target),
            qkv,
            proj,
            up,
            down,
        )
        vmem = pl.BlockSpec(memory_space=pltpu.VMEM)
        hbm = pl.BlockSpec(memory_space=pl.ANY)
        res = pl.pallas_call(
            kernel,
            out_shape=[jax.ShapeDtypeStruct(sh, dt) for sh, dt in outs.values()],
            in_specs=[vmem] * 7 + [hbm] * 4,
            out_specs=[vmem] * len(outs),
            scratch_shapes=[pltpu.VMEM(sh, dt) for sh, dt in vm.values()] + [DMA(sh) for sh in sems.values()],
            compiler_params=pltpu.CompilerParams(
                collective_id=0, has_side_effects=True, vmem_limit_bytes=62 * 1024 * 1024
            ),
            name="train_step",
        )(*args)
        shapes = [
            ((T, D), BF),
            ((T, D), BF),
            ((T, D), F32),
            ((2, 2, DR), F32),
            ((1, DR), F32),
            ((2, 3, DR, W), F32),
            ((2, DR, W), F32),
            ((2, DR, F), F32),
            ((2, DR, F), F32),
        ]
        last = pl.pallas_call(
            layout,
            out_shape=[jax.ShapeDtypeStruct(sh, dt) for sh, dt in shapes],
            in_specs=[hbm] * 3 + [vmem] * 2 + [hbm] * 4,
            out_specs=[hbm] * 3 + [vmem] * 2 + [hbm] * 4,
            scratch_shapes=[pltpu.VMEM(*shapes[i]) for i in (0, 1, 2, 5, 6, 7, 8)] + [DMA((2, 7))],
            compiler_params=pltpu.CompilerParams(vmem_limit_bytes=62 * 1024 * 1024),
            name="layout",
        )(*res)
        ro, do, gi, gains_grad, router_grad, gq, gp, gu, gd = last
        gp, gd = jnp.swapaxes(gp, 1, 2), jnp.swapaxes(gd, 1, 2)
        return (ro, do, gi, gains_grad, router_grad.reshape(DR), gq, gp, gu, gd)

    return run


def solution(mesh):
    S, n = mesh.shape["seq"], mesh.shape["mlp"]

    def body(inp, segments, picks, gains, router, qkv, proj, up, down, cot):
        run = build(
            S, n, inp.shape[0], inp.shape[1], qkv.shape[-1], up.shape[-1], picks.size, picks.shape[0]
        )
        return run(inp, segments, picks, gains, router, qkv, proj, up, down, cot)

    return jax.shard_map(
        body,
        mesh=mesh,
        in_specs=(
            P("seq", None),
            P("seq"),
            P(),
            P(),
            P(),
            P(None, None, None, "mlp"),
            P(None, "mlp", None),
            P(None, None, "mlp"),
            P(None, "mlp", None),
            P("seq", None),
        ),
        out_specs=(
            P("seq", None),
            P("seq", None),
            P("seq", None),
            P(None, None, "seq"),
            P("seq"),
            P(None, None, "seq", "mlp"),
            P(None, "mlp", "seq"),
            P(None, "seq", "mlp"),
            P(None, "mlp", "seq"),
        ),
        check_vma=False,
    )
```

```python
from types import SimpleNamespace

import jax
import jax.numpy as jnp
import numpy as np
from jax import lax
from jax.experimental import pallas as pl
from jax.experimental.pallas import tpu as pltpu
from jax.sharding import PartitionSpec as P

HD = 64
G = 2048
EPS = 1e-05
NEG = -1e30
SCALE = HD**-0.5
BF = jnp.bfloat16
F32 = jnp.float32
MESH = pl.DeviceIdType.MESH
DMA = pltpu.SemaphoreType.DMA
GELU_A = 0.044715
GELU_B = float(np.sqrt(2.0 / np.pi))
WIDE = 1536
KINDS = ("down", "up", "proj", "qkv")


def dot(left, right, dims):
    return lax.dot_general(left, right, (dims, ((), ())), preferred_element_type=F32)


def nn(left, right):
    return dot(left, right, ((1,), (0,)))


def nt(left, right):
    return dot(left, right, ((1,), (1,)))


def tn(left, right):
    return dot(left, right, ((0,), (0,)))


def inverse_rms(x):
    return lax.rsqrt(jnp.mean(x * x, axis=-1, keepdims=True) + EPS)


def rms(x, gain):
    return x * inverse_rms(x) * gain


def rms_back(dy, x, gain):
    r = inverse_rms(x)
    gy = gain * dy
    dx = r * gy - x * (r * r * r) * jnp.mean(gy * x, axis=-1, keepdims=True)
    return dx, jnp.sum(dy * x * r, axis=0, keepdims=True)


def gelu_pair(x):
    t = jnp.tanh(GELU_B * (x + GELU_A * x * x * x))
    half = 0.5 * (1.0 + t)
    slope = half + 0.5 * x * (1.0 - t * t) * (GELU_B * (1.0 + 3.0 * GELU_A * x * x))
    return x * half, slope


def column(row):
    wide = jnp.broadcast_to(row.astype(F32), (128, row.shape[1]))
    return jnp.transpose(wide)[:, 0:1]


def chunks(extent):
    width = 384 if extent % 384 == 0 else extent
    return [(at, width) for at in range(0, extent, width)]


def build(S, n, T, D, W, F, R, groups):
    rest = S // 2
    Y = 2 ** ((rest.bit_length() - 1) // 2)
    Z = rest // Y
    ZY = Z * Y
    H = W // HD
    LEVEL = 2 * Y
    CH = LEVEL * T
    GN = R // T
    RH = R // GN
    RB = R // S
    DM = D // n
    DR = D // S
    DRP = -(-DR // 16) * 16
    ZD = Z * DRP
    QY = 2 * ZD
    XW = {"down": F, "up": F, "proj": W, "qkv": 3 * W}

    target = np.full((Y, 1, QY), -1, np.int32)
    for yy in range(Y):
        for core in range(2):
            for zz in range(Z):
                for j in range(DR):
                    target[yy, 0, (core * Z + zz) * DRP + j] = ((zz * Y + yy) * 2 + core) * DR + j

    ins = ["inp", "segr", "picks", "gains", "router", "cot", "target", "qkv_h", "proj_h", "up_h", "down_h"]
    outs = {
        "ro_o": ((T, D), BF),
        "do_o": ((T, D), BF),
        "gi_o": ((T, D), F32),
        "sm_o": ((8, 128), F32),
        "rg_o": ((2, D), F32),
        "qkv_o": ((2, 3, DR, W), F32),
        "proj_o": ((2, DR, W), F32),
        "up_o": ((2, DR, F), F32),
        "down_o": ((2, DR, F), F32),
    }
    vm = {
        "wq": ((2, 3, D, W), BF),
        "wp": ((2, W, D), BF),
        "wu": ((2, D, F), BF),
        "wd": ((2, F, D), BF),
        "sega": ((S, 8, T), jnp.int32),
        "segc": ((T, 1), F32),
        "oht": ((T, R), BF),
        "oh": ((R, T), BF),
        "posr": ((GN // 2, 8, 2 * RH), F32),
        "posc": ((RH, 1), F32),
        "sgr": ((GN // 2, 8, 2 * RH), F32),
        "sgc": ((RH, 1), F32),
        "part": ((S, RB, DM), BF),
        "r1": ((S, RB, DM), BF),
        "full": ((2, n * ZY, RB, DM), BF),
        "rows": ((R, D), BF),
        "nr": ((RH, D), BF),
        "chh": ((RH, D), BF),
        "qr": ((R, W), BF),
        "kr": ((R, W), BF),
        "vr": ((R, W), BF),
        "mr": ((H, RH, 1), F32),
        "lr": ((H, RH, 1), F32),
        "ar": ((H, RH, HD), F32),
        "mixr": ((RH, W), BF),
        "attr": ((RH, D), F32),
        "n2r": ((RH, D), BF),
        "prer": ((RH, F), F32),
        "actr": ((RH, F), BF),
        "xr": ((2, n, RH, D), BF),
        "xd": ((3, n, T, D), BF),
        "chg": ((GN, RH, D), BF),
        "sel": ((T, D), BF),
        "ro": ((T, D), F32),
        "nd": ((T, D), BF),
        "kva": ((S, T, 2 * W), BF),
        "qa": ((S, T, W), BF),
        "da": ((S, T, W), BF),
        "sta": ((S, 16, T), F32),
        "md": ((H, T, 1), F32),
        "ld": ((H, T, 1), F32),
        "ad": ((H, T, HD), F32),
        "hid": ((T, D), F32),
        "n2d": ((T, D), BF),
        "dact": ((T, F), F32),
        "dattn": ((T, D), BF),
        "dq": ((H, max(T, RH), HD), F32),
        "dk": ((H, max(T, RH), HD), F32),
        "dv": ((H, max(T, RH), HD), F32),
        "dro": ((T, D), F32),
        "small": ((8, D), F32),
        "sblk": ((S, 8, 128), F32),
        "srec": ((S, 8, 128), F32),
        "dor": ((GN, RH, W), BF),
        "str": ((GN, 16, RH), F32),
        "dprer": ((RH, F), BF),
        "dattr": ((RH, D), BF),
        "g3r": ((RH, 3 * W), BF),
        "gr": ((GN, 8, D), F32),
        "sele": ((Y, D, QY), BF),
    }
    for k in KINDS:
        X = XW[k]
        vm["left_" + k] = ((LEVEL, T, QY), BF)
        vm["away_" + k] = ((Y - 1, T, QY), BF)
        vm["right_" + k] = ((LEVEL, T, X), BF)
        vm["zsend_" + k] = ((Z, DRP, X), BF)
        vm["zown_" + k] = ((DRP, X), F32)
        vm["zrec_" + k] = ((Z - 1, DRP, X), BF)
        vm["rsend_" + k] = ((GN - 1, DRP, X), BF)
        vm["rkeep_" + k] = ((DRP, X), F32)
        vm["rrec_" + k] = ((GN - 1, DRP, X), BF)
    n_sends = (Z - 1) + (Y - 1) + 1 + (Z - 1) * Y + Z * (Y - 1)
    sems = {
        "w_s": (8,),
        "seg_s": (2,),
        "t_s": (6,),
        "xr_s": (2, n - 1),
        "xr_r": (2, n - 1),
        "xd_s": (3, n - 1),
        "xd_r": (3, n - 1),
        "sw_s": (10, GN - 1),
        "sw_r": (10, GN - 1),
        "kv_s": (n_sends,),
        "kv_r": (S,),
        "q_s": (n_sends,),
        "q_r": (S,),
        "da_s": (n_sends,),
        "da_r": (S,),
        "st_s": (n_sends,),
        "st_r": (S,),
        "sm_s": (2,),
        "gl_s": (4, 2, 2 * Y - 1),
        "gl_r": (4, 2, LEVEL),
        "gz_s": (4, Z - 1),
        "gz_r": (4, Z - 1),
    }
    names = ins + list(outs) + list(vm) + list(sems)

    def kernel(*refs):
        r = SimpleNamespace(**dict(zip(names, refs, strict=True)))
        g = r.__dict__
        s = lax.axis_index("seq")
        m = lax.axis_index("mlp")
        c = lax.rem(s, 2)
        chip = s // 2
        y = lax.rem(chip, Y)
        z = chip // Y
        sib = s + 1 - 2 * c
        gi = lax.rem(s, GN)

        def rank(zz, yy, cc):
            return (zz * Y + yy) * 2 + cc

        def remote(src, dst, send, recv, seq, mlp):
            return pltpu.make_async_remote_copy(
                src_ref=src, dst_ref=dst, send_sem=send, recv_sem=recv, device_id=(seq, mlp), device_id_type=MESH
            )

        bar = pltpu.get_barrier_semaphore()

        def greet(i, carry):
            pl.semaphore_signal(bar, inc=1, device_id=(lax.rem(s + i, S), m), device_id_type=MESH)
            return carry

        lax.fori_loop(1, S, greet, 0)
        for j in range(1, n):

            def greet_other(i, carry, j=j):
                pl.semaphore_signal(bar, inc=1, device_id=(i * 2 + c, lax.rem(m + j, n)), device_id_type=MESH)
                return carry

            lax.fori_loop(0, ZY, greet_other, 0)
        loads = [
            pltpu.make_async_copy(src.at[b], dst.at[b], r.w_s.at[4 * b + i])
            for b in range(2)
            for i, (src, dst) in enumerate(
                ((r.qkv_h, r.wq), (r.proj_h, r.wp), (r.up_h, r.wu), (r.down_h, r.wd))
            )
        ]
        prow = jnp.concatenate([r.picks[i : i + 1, :] + G * i for i in range(groups)], axis=1)
        here = s * T + lax.broadcasted_iota(jnp.int32, (T, R), 0)
        hot = jnp.where(prow == here, 1.0, 0.0)
        r.oht[...] = hot.astype(BF)
        r.oh[...] = jnp.transpose(hot).astype(BF)

        def my_columns(x):
            got = x[:, 0:DM]
            for j in range(1, n):
                got = jnp.where(m == j, x[:, j * DM : (j + 1) * DM], got)
            return got

        def scatter_rows(x):
            r.part[...] = nn(r.oh[...], my_columns(x)).astype(BF).reshape(S, RB, DM)

        scatter_rows(r.inp[...])
        def send_segments(i, carry):
            remote(r.sega.at[s], r.sega.at[s], r.seg_s.at[0], r.seg_s.at[1], lax.rem(s + i, S), m).start()
            return carry

        sem = [r.t_s.at[j] for j in range(6)]

        def spread_start():
            def first(k, carry):
                p = lax.rem(s + k, S)
                remote(r.part.at[p], r.r1.at[s], sem[0], sem[1], p, m).start()
                return carry

            lax.fori_loop(1, S, first, 0)
            r.r1[s] = r.part[s]

        def spread_end(after):
            some = pl.ds(0, S - 1)
            remote(r.part.at[some], r.r1.at[some], sem[0], sem[1], s, m).wait()
            me = m * ZY + chip
            r.full[c, me] = jnp.sum(r.r1[...].astype(F32), axis=0).astype(BF)

            def second(k, carry):
                p = lax.rem(me + k, n * ZY)
                block = r.full.at[c, me]
                remote(block, block, sem[2], sem[3], lax.rem(p, ZY) * 2 + c, p // ZY).start()
                return carry

            lax.fori_loop(1, n * ZY, second, 0)
            after()
            some = r.full.at[c, pl.ds(0, n * ZY - 1)]
            remote(some, some, sem[2], sem[3], s, m).wait()
            swap = remote(r.full.at[c], r.full.at[c], sem[4], sem[5], sib, m)
            swap.start()
            swap.wait()

            def place(k, carry):
                for cc in range(2):
                    rows = pl.ds(pl.multiple_of((k * 2 + cc) * RB, RB), RB)
                    for mm in range(n):
                        r.rows[rows, mm * DM : (mm + 1) * DM] = r.full[cc, mm * ZY + k]
                return carry

            lax.fori_loop(0, ZY, place, 0)

        def mlp_copies(buf, send, recv, i):
            i = i % buf.shape[0]
            return [
                remote(buf.at[i, m], buf.at[i, m], send.at[i, j - 1], recv.at[i, j - 1], s, lax.rem(m + j, n))
                for j in range(1, n)
            ]

        def mlp_start(which, i, value):
            buf = g["x" + which]
            buf[i % buf.shape[0], m] = value.astype(BF)
            for copy in mlp_copies(buf, g["x" + which + "_s"], g["x" + which + "_r"], i):
                copy.start()

        def mlp_total(which, i):
            buf = g["x" + which]
            for copy in mlp_copies(buf, g["x" + which + "_s"], g["x" + which + "_r"], i):
                copy.wait()
            i = i % buf.shape[0]
            total = buf[i, 0].astype(F32)
            for j in range(1, n):
                total = total + buf[i, j].astype(F32)
            return total

        def friend(j):
            return s - gi + lax.rem(gi + j, GN)

        def share(i, *refs):
            return [
                remote(ref.at[gi], ref.at[gi], r.sw_s.at[i + k, j - 1], r.sw_r.at[i + k, j - 1], friend(j), m)
                for k, ref in enumerate(refs)
                for j in range(1, GN)
            ]

        def attend_start(top, total, acc):
            top[...] = jnp.full(top.shape, NEG, F32)
            total[...] = jnp.zeros(total.shape, F32)
            acc[...] = jnp.zeros(acc.shape, F32)

        def head_groups(width):
            step = min(H, max(1, WIDE // width))
            return [range(at, min(at + step, H)) for at in range(0, H, step)]

        def attend(ci, query, key, value, mask, top, total, acc):
            kept = mask(ci)
            for group in head_groups(kept.shape[1]):
                scores = {h: nt(query(h), key(ci, h)) for h in group}
                weights = {}
                for h in group:
                    score = jnp.where(kept, scores[h], NEG)
                    old = top[h]
                    new = jnp.maximum(old, jnp.max(score, axis=-1, keepdims=True))
                    shrink = jnp.exp(old - new)
                    weight = jnp.exp(score - new)
                    total[h] = total[h] * shrink + jnp.sum(weight, axis=-1, keepdims=True)
                    acc[h] = acc[h] * shrink
                    top[h] = new
                    weights[h] = weight.astype(BF)
                for h in group:
                    acc[h] = acc[h] + nn(weights[h], value(ci, h))

        def finish(top, total, acc, mixed):
            for h in range(H):
                out = acc[h] / total[h]
                acc[h] = out
                mixed[:, h * HD : (h + 1) * HD] = out.astype(BF)
                top[h] = top[h] + jnp.log(total[h])

        def row_stats(grad, top, total, acc):
            lane = lax.broadcasted_iota(jnp.int32, (acc.shape[1], 128), 1)
            stats = jnp.zeros((acc.shape[1], 128), F32)
            for h in range(H):
                delta = jnp.sum(grad(h).astype(F32) * acc[h], axis=-1, keepdims=True)
                total[h] = delta
                stats = jnp.where(lane == h, top[h], jnp.where(lane == 8 + h, delta, stats))
            return jnp.transpose(stats)[0:16]

        def back_query(ci, query, grad, key, value, mask, log_total, delta, out):
            kept = mask(ci)
            for group in head_groups(kept.shape[1]):
                scores = {h: nt(query(h), key(ci, h)) for h in group}
                grad_probs = {h: nt(grad(h), value(ci, h)) for h in group}
                grad_scores = {}
                for h in group:
                    probs = jnp.where(kept, jnp.exp(scores[h] - log_total[h]), 0.0)
                    grad_scores[h] = (probs * (grad_probs[h] - delta[h])).astype(BF)
                for h in group:
                    out[h] = out[h] + nn(grad_scores[h], key(ci, h))

        def back_keys(ci, key, value, query, grad, mask, stat, out_key, out_value):
            kept = mask(ci)
            for group in head_groups(kept.shape[1]):
                scores = {h: nt(key(h), query(ci, h)) for h in group}
                grad_probs = {h: nt(value(h), grad(ci, h)) for h in group}
                probs, grad_scores = {}, {}
                for h in group:
                    prob = jnp.where(kept, jnp.exp(scores[h] - stat(ci, h)), 0.0)
                    grad_scores[h] = (prob * (grad_probs[h] - stat(ci, 8 + h))).astype(BF)
                    probs[h] = prob.astype(BF)
                for h in group:
                    out_value[h] = out_value[h] + nn(probs[h], grad(ci, h))
                    out_key[h] = out_key[h] + nn(grad_scores[h], query(ci, h))

        dq_d, dk_d, dv_d = (ref.at[:, 0:T] for ref in (r.dq, r.dk, r.dv))
        dq_r, dk_r, dv_r = (ref.at[:, 0:RH] for ref in (r.dq, r.dk, r.dv))

        def pack_grads(dq, dk, dv, out):
            for h in range(H):
                out[:, h * HD : (h + 1) * HD] = (dq[h] * SCALE).astype(BF)
                out[:, W + h * HD : W + (h + 1) * HD] = dk[h].astype(BF)
                out[:, 2 * W + h * HD : 2 * W + (h + 1) * HD] = dv[h].astype(BF)

        def front_back(grads, b):
            return (
                nt(grads[:, 0:W], r.wq[b, 0])
                + nt(grads[:, W : 2 * W], r.wq[b, 1])
                + nt(grads[:, 2 * W : 3 * W], r.wq[b, 2])
            )

        def loop(low, high, body):
            def step(i, carry):
                body(i)
                return carry

            lax.fori_loop(low, high, step, 0)

        def gather(buf, ss, rs, up):
            sign = -1 if up else 1
            last = z if up else Z - 1 - z
            ahead = Z - 1 - z if up else z
            at_y, at_sib, at_level = Z - 1, Z + Y - 2, Z + Y - 1
            at_z = at_level + Y - 1
            at_far = at_z + (Z - 1) * Y

            def copy(slot, dst, k):
                return remote(buf.at[slot], buf.at[slot], ss.at[k], rs.at[slot], dst, m)

            def recv(slot):
                copy(slot, sib, 0).wait_recv()

            def side(dy):
                return lax.rem(y + dy, Y)

            def copies(each):
                loop(1, ahead + 1, lambda dz: each(copy(s, rank(z - sign * dz, y, c), dz - 1)))
                for dy in range(1, Y):
                    each(copy(s, rank(z, side(dy), c), at_y + dy - 1))
                each(copy(s, sib, at_sib))

            def level_copy(dy):
                return copy(rank(z, side(dy), c), sib, at_level + dy - 1)

            def z_copies(dz):
                slot = rank(z + sign * dz, y, c)
                k = at_z + (dz - 1) * Y
                outs = [copy(slot, rank(z, side(dy), c), k + dy - 1) for dy in range(1, Y)]
                return [*outs, copy(slot, sib, k + Y - 1)]

            def far_copy(dz, dy):
                return copy(rank(z + sign * dz, side(dy), c), sib, at_far + (dz - 1) * (Y - 1) + dy - 1)

            def start():
                copies(lambda one: one.start())

            def level():
                for dy in range(1, Y):
                    recv(rank(z, side(dy), c))
                    level_copy(dy).start()

            def level_end():
                for dy in range(Y):
                    recv(rank(z, side(dy), 1 - c))

            def z_step(dz):
                recv(rank(z + sign * dz, y, c))
                for one in z_copies(dz):
                    one.start()

            def y_step(dz):
                for dy in range(1, Y):
                    recv(rank(z + sign * dz, side(dy), c))
                    far_copy(dz, dy).start()

            def sib_step(dz):
                for dy in range(Y):
                    recv(rank(z + sign * dz, side(dy), 1 - c))

            def end():
                copies(lambda one: one.wait_send())
                for dy in range(1, Y):
                    level_copy(dy).wait_send()

                def sent(dz):
                    for one in z_copies(dz):
                        one.wait_send()
                    for dy in range(1, Y):
                        far_copy(dz, dy).wait_send()

                loop(1, last + 1, sent)

            return SimpleNamespace(
                start=start,
                level=level,
                level_end=level_end,
                z_step=z_step,
                y_step=y_step,
                sib_step=sib_step,
                end=end,
                last=last,
            )

        def walk(items, body):
            last = items[0].last

            def all_of(name, *args):
                for item in items:
                    getattr(item, name)(*args)

            pl.when(last > 0)(lambda: all_of("z_step", 1))
            all_of("level_end")
            body(0)

            def step(dz):
                all_of("y_step", dz)
                pl.when(dz < last)(lambda: all_of("z_step", dz + 1))
                all_of("sib_step", dz)
                body(dz)

            loop(1, last + 1, step)

        lev = lax.rem(s, LEVEL)

        def level_slot(dy, cc):
            return lax.rem(y + dy, Y) * 2 + cc

        def level_copy(k, side, j, src, slot, dst):
            i = KINDS.index(k)
            buf = g[("left_", "right_")[side] + k]
            return remote(src, buf.at[slot], r.gl_s.at[i, side, j], r.gl_r.at[i, side, slot], dst, m)

        def own_copies(k, side):
            mine = g[("left_", "right_")[side] + k].at[lev]
            out = [level_copy(k, side, 0, mine, lev, sib)]
            for dy in range(1, Y):
                src = g["away_" + k].at[dy - 1] if side == 0 else mine
                out.append(level_copy(k, side, dy, src, lev, rank(z, lax.rem(y + dy, Y), c)))
            return out

        def far_copies(k):
            return [
                level_copy(k, side, Y + dy - 1, g[("left_", "right_")[side] + k].at[level_slot(dy, c)], level_slot(dy, c), sib)
                for side in range(2)
                for dy in range(1, Y)
            ]

        def level_wait(k, slot):
            for side in range(2):
                buf = g[("left_", "right_")[side] + k]
                level_copy(k, side, 0, buf.at[slot], slot, sib).wait_recv()

        def sum_left(k, lhs):
            g["left_" + k][lev] = nn(lhs[...], r.sele[y]).astype(BF)
            for dy in range(1, Y):
                g["away_" + k][dy - 1] = nn(lhs[...], r.sele[lax.rem(y + dy, Y)]).astype(BF)
            for copy in own_copies(k, 0):
                copy.start()

        def sum_right(k):
            for copy in own_copies(k, 1):
                copy.start()

        def sum_far(k):
            for dy in range(1, Y):
                level_wait(k, level_slot(dy, c))
            for copy in far_copies(k):
                copy.start()

        def z_copy(k, dz):
            i = KINDS.index(k)
            return remote(
                g["zsend_" + k].at[lax.rem(z + dz, Z)],
                g["zrec_" + k].at[dz - 1],
                r.gz_s.at[i, dz - 1],
                r.gz_r.at[i, dz - 1],
                rank(lax.rem(z + dz, Z), y, c),
                m,
            )

        def sum_z(k):
            for dy in range(Y):
                level_wait(k, level_slot(dy, 1 - c))
            left = g["left_" + k][...].reshape(LEVEL * T, QY)
            left = jnp.where(c == 0, left[:, 0:ZD], left[:, ZD:QY])
            for x, w in chunks(XW[k]):
                total = tn(left, g["right_" + k][:, :, x : x + w].reshape(LEVEL * T, w)).reshape(Z, DRP, w)
                g["zsend_" + k][:, :, x : x + w] = total.astype(BF)
                own = total[0]
                for zz in range(1, Z):
                    own = jnp.where(z == zz, total[zz], own)
                g["zown_" + k][:, x : x + w] = own
            for dz in range(1, Z):
                z_copy(k, dz).start()

        def put(b, k, value):
            if k == "qkv":
                for j in range(3):
                    r.qkv_o[b, j] = value[0:DR, j * W : (j + 1) * W]
            else:
                g[k + "_o"][b] = value[0:DR]

        def sum_end(k):
            t = g["zown_" + k][...]
            for dz in range(1, Z):
                z_copy(k, dz).wait()
                t = t + g["zrec_" + k][dz - 1].astype(F32)
            put(1, k, t)

        def sum_sent(k):
            for side in range(2):
                for copy in own_copies(k, side):
                    copy.wait_send()
            for copy in far_copies(k):
                copy.wait_send()

        def routed_copy(k, j):
            i = 6 + KINDS.index(k)
            send, recv = r.sw_s.at[i, j - 1], r.sw_r.at[i, j - 1]
            return remote(g["rsend_" + k].at[j - 1], g["rrec_" + k].at[j - 1], send, recv, friend(j), m)

        def routed_start(k, lhs, rhs):
            col = lax.broadcasted_iota(jnp.int32, (D, DRP), 1)
            row = lax.broadcasted_iota(jnp.int32, (D, DRP), 0)

            def block(who):
                hit = (row - who * DR == col) & (col < DR)
                return nn(lhs, jnp.where(hit, 1.0, 0.0).astype(BF)).astype(BF)

            for j in range(1, GN):
                g["rsend_" + k][j - 1] = tn(block(friend(j)), rhs).astype(BF)
                routed_copy(k, j).start()
            g["rkeep_" + k][...] = tn(block(s), rhs)

        def routed_end(k):
            t = g["rkeep_" + k][...]
            for j in range(1, GN):
                routed_copy(k, j).wait()
                t = t + g["rrec_" + k][j - 1].astype(F32)
            put(0, k, t)

        def head(h):
            return slice(h * HD, (h + 1) * HD)

        pl.semaphore_wait(bar, S - 1 + (n - 1) * ZY)
        spread_start()
        r.sega[s] = jnp.broadcast_to(r.segr[...], (8, T))
        for load in loads:
            load.start()
        prow_f = prow.astype(F32)
        for i in range(GN // 2):
            r.posr[i] = jnp.broadcast_to(prow_f[:, i * 2 * RH : (i + 1) * 2 * RH], (8, 2 * RH))
        mine = r.posr[gi // 2][0:1]
        r.posc[...] = column(jnp.where(lax.rem(gi, 2) == 0, mine[:, 0:RH], mine[:, RH : 2 * RH]))
        r.segc[...] = column(r.segr[...])
        for yy in range(Y):
            ids = lax.broadcasted_iota(jnp.int32, (D, QY), 0)
            r.sele[yy] = jnp.where(ids == r.target[yy], 1.0, 0.0).astype(BF)
        spread_end(lambda: lax.fori_loop(1, S, send_segments, 0))
        some = pl.ds(0, S - 1)
        remote(r.sega.at[some], r.sega.at[some], r.seg_s.at[0], r.seg_s.at[1], s, m).wait()
        starts = [
            jnp.sum(
                jnp.sum(jnp.where(r.sega[...] < k, 0.125, 0.0), axis=0), axis=(0, 1), keepdims=True
            )
            for k in range(1, 5)
        ]
        for i in range(GN // 2):
            r.sgr[i] = sum(jnp.where(r.posr[i] >= at, 1.0, 0.0) for at in starts)
        r.sgc[...] = sum(jnp.where(r.posc[...] >= at, 1.0, 0.0) for at in starts)
        half = pl.ds(pl.multiple_of(gi * RH, RH), RH)

        loads[0].wait()
        r.chh[...] = r.rows[half, :]
        r.nr[...] = rms(r.chh[...].astype(F32), r.gains[0, 0:1]).astype(BF)
        for at in range(0, R, 256):
            part = slice(at, at + 256)
            normed = rms(r.rows[part].astype(F32), r.gains[0, 0:1]).astype(BF)
            r.qr[part] = (nn(normed, r.wq[0, 0]).astype(BF) * SCALE).astype(BF)
            r.kr[part] = nn(normed, r.wq[0, 1]).astype(BF)
            r.vr[part] = nn(normed, r.wq[0, 2]).astype(BF)

        def part_rows(ref):
            return lambda ci, h: ref[pl.ds(pl.multiple_of(ci * 2 * RH, RH), 2 * RH), head(h)]

        def half_rows(ref):
            return lambda h: ref[half, head(h)]

        def routed_mask(ci):
            return (r.sgr[ci][0:1] == r.sgc[...]) & (r.posr[ci][0:1] <= r.posc[...])

        def routed_mask_back(ci):
            return (r.sgr[ci][0:1] == r.sgc[...]) & (r.posc[...] <= r.posr[ci][0:1])

        def routed_pick(i):
            return lax.rem(gi // 2 + i, GN // 2)

        def routed_loop(body):
            if GN == 2:
                body(0)
            else:
                loop(0, GN // 2, lambda i: body(routed_pick(i)))

        attend_start(r.mr, r.lr, r.ar)
        routed_loop(
            lambda ci: attend(
                ci, half_rows(r.qr), part_rows(r.kr), part_rows(r.vr), routed_mask, r.mr, r.lr, r.ar
            )
        )
        finish(r.mr, r.lr, r.ar, r.mixr)
        loads[1].wait()
        mlp_start("r", 0, nn(r.mixr[...], r.wp[0]))
        sum_left("down", r.cot)
        loads[2].wait()
        loads[3].wait()
        attn = mlp_total("r", 0)
        r.attr[...] = attn
        normed = rms(r.chh[...].astype(F32) + attn, r.gains[0, 1:2]).astype(BF)
        r.n2r[...] = normed
        for x, w in chunks(F):
            pre = nn(normed, r.wu[0, :, x : x + w])
            r.prer[:, x : x + w] = pre
            r.actr[:, x : x + w] = gelu_pair(pre)[0].astype(BF)
        mlp_start("r", 1, nn(r.actr[...], r.wd[0]))
        mlp = mlp_total("r", 1)
        r.chg[gi] = (r.attr[...] + mlp).astype(BF)
        swaps = share(0, r.chg)
        for copy in swaps:
            copy.start()
        inp = r.inp[...].astype(F32)
        gate = jax.nn.sigmoid(jnp.sum(inp * r.router[...].reshape(1, D), axis=-1, keepdims=True))
        for load in loads[4:]:
            load.wait()
        for copy in swaps:
            copy.wait()

        sel = nn(r.oht[...], r.chg[...].reshape(R, D))
        r.sel[...] = sel.astype(BF)
        ro = inp + gate * sel
        r.ro[...] = ro
        r.ro_o[...] = ro.astype(BF)
        normed = rms(ro, r.gains[1, 0:1]).astype(BF)
        r.nd[...] = normed
        r.kva[s, :, 0:W] = nn(normed, r.wq[1, 1]).astype(BF)
        r.kva[s, :, W : 2 * W] = nn(normed, r.wq[1, 2]).astype(BF)
        keys_all = gather(r.kva, r.kv_s, r.kv_r, True)
        keys_all.start()
        r.qa[s] = (nn(normed, r.wq[1, 0]).astype(BF) * SCALE).astype(BF)
        query_all = gather(r.qa, r.q_s, r.q_r, False)
        query_all.start()
        keys_all.level()
        query_all.level()

        def level_rows(ref, first=0):
            def get(ci, h):
                return ref[pl.ds(ci * LEVEL, LEVEL), :, head(first + h)].reshape(CH, HD)

            return get

        def level_line(ref, line):
            return lambda ci: jnp.concatenate([ref[ci * LEVEL + j][line : line + 1] for j in range(LEVEL)], axis=1)

        own_pos = lax.broadcasted_iota(jnp.int32, (T, CH), 0) + s * T
        far_pos = lax.broadcasted_iota(jnp.int32, (T, CH), 1)
        seg_line = level_line(r.sega, 0)

        def dense_mask(ci):
            return (seg_line(ci).astype(F32) == r.segc[...]) & (far_pos + ci * CH <= own_pos)

        def dense_mask_back(ci):
            return (seg_line(ci).astype(F32) == r.segc[...]) & (own_pos <= far_pos + ci * CH)

        attend_start(r.md, r.ld, r.ad)
        walk(
            [keys_all],
            lambda dz: attend(
                z - dz,
                lambda h: r.qa[s, :, head(h)],
                level_rows(r.kva),
                level_rows(r.kva, H),
                dense_mask,
                r.md,
                r.ld,
                r.ad,
            ),
        )
        finish(r.md, r.ld, r.ad, r.right_proj.at[lev])
        mlp_start("d", 0, nn(r.right_proj[lev], r.wp[1]))
        loop(1, query_all.last + 1, query_all.z_step)
        sum_left("qkv", r.nd)
        for x, w in chunks(F):
            r.dact[:, x : x + w] = nt(r.cot[...], r.wd[1, x : x + w, :])
        attn = mlp_total("d", 0)
        hid = r.ro[...] + attn
        r.hid[...] = hid
        normed = rms(hid, r.gains[1, 1:2]).astype(BF)
        r.n2d[...] = normed
        for x, w in chunks(F):
            active, slope = gelu_pair(nn(normed, r.wu[1, :, x : x + w]))
            r.right_down[lev, :, x : x + w] = active.astype(BF)
            r.right_up[lev, :, x : x + w] = (r.dact[:, x : x + w] * slope).astype(BF)
        sum_right("down")
        mlp_start("d", 1, nt(r.right_up[lev], r.wu[1]))
        mlp_start("d", 2, nn(r.right_down[lev], r.wd[1]))

        sum_left("up", r.n2d)
        loop(1, query_all.last + 1, query_all.y_step)
        dn, dg = rms_back(mlp_total("d", 1), r.hid[...], r.gains[1, 1:2])
        r.small[1:2] = dg
        dhid = r.cot[...].astype(F32) + dn
        r.dro[...] = dhid
        r.dattn[...] = dhid.astype(BF)
        r.da[s] = nt(r.dattn[...], r.wp[1]).astype(BF)
        r.sta[s] = row_stats(lambda h: r.da[s, :, head(h)], r.md, r.ld, r.ad)
        grad_all = gather(r.da, r.da_s, r.da_r, False)
        stat_all = gather(r.sta, r.st_s, r.st_r, False)
        for item in (grad_all, stat_all):
            item.start()
        for item in (grad_all, stat_all):
            item.level()
        sum_right("up")
        query_all.level_end()
        loop(1, query_all.last + 1, query_all.sib_step)
        dq_d[...] = jnp.zeros((H, T, HD), F32)
        dk_d[...] = jnp.zeros((H, T, HD), F32)
        dv_d[...] = jnp.zeros((H, T, HD), F32)
        loop(
            0,
            z + 1,
            lambda dz: back_query(
                z - dz,
                lambda h: r.qa[s, :, head(h)],
                lambda h: r.da[s, :, head(h)],
                level_rows(r.kva),
                level_rows(r.kva, H),
                dense_mask,
                r.md,
                r.ld,
                dq_d,
            ),
        )
        walk(
            [grad_all, stat_all],
            lambda dz: back_keys(
                z + dz,
                lambda h: r.kva[s, :, head(h)],
                lambda h: r.kva[s, :, head(H + h)],
                level_rows(r.qa),
                level_rows(r.da),
                dense_mask_back,
                lambda ci, line: level_line(r.sta, line)(ci),
                dk_d,
                dv_d,
            ),
        )
        sum_far("down")
        sum_far("up")
        sum_z("down")
        pack_grads(dq_d, dk_d, dv_d, r.right_qkv.at[lev])
        mlp_start("d", 3, front_back(r.right_qkv.at[lev], 1))
        sum_left("proj", r.dattn)
        sum_right("qkv")
        sum_right("proj")
        dn, dg = rms_back(mlp_total("d", 3), r.ro[...], r.gains[1, 0:1])
        r.small[0:1] = dg
        dro = r.dro[...] + dn
        r.dro[...] = dro

        sel = r.sel[...].astype(F32)
        inp = r.inp[...].astype(F32)
        gate = jax.nn.sigmoid(jnp.sum(inp * r.router[...].reshape(1, D), axis=-1, keepdims=True))
        dlogit = jnp.sum(dro * sel, axis=-1, keepdims=True) * gate * (1.0 - gate)
        scatter_rows((gate * dro).astype(BF))
        spread_start()
        spread_end(lambda: None)
        r.small[2:3] = jnp.sum(inp * dlogit, axis=0, keepdims=True)
        r.small[3:8] = jnp.zeros((5, D), F32)
        r.sblk[...] = jnp.zeros((S, 8, 128), F32)
        for p in range(S):
            r.sblk[p, :, 0:DR] = r.small[:, p * DR : (p + 1) * DR]

        def send_small(i, carry):
            p = lax.rem(s + i, S)
            remote(r.sblk.at[p], r.srec.at[s], r.sm_s.at[0], r.sm_s.at[1], p, m).start()
            return carry

        lax.fori_loop(1, S, send_small, 0)
        r.srec[s] = r.sblk[s]
        sum_z("up")
        sum_far("qkv")
        sum_far("proj")

        dmlp = r.rows[half, :]
        r.attr[...] = r.attr[...] + r.chh[...].astype(F32)
        for x, w in chunks(F):
            grad_active = nt(dmlp, r.wd[0, x : x + w, :])
            r.dprer[:, x : x + w] = (grad_active * gelu_pair(r.prer[:, x : x + w])[1]).astype(BF)
        mlp_start("r", 2, nt(r.dprer[...], r.wu[0]))
        routed_start("down", dmlp, r.actr[...])
        routed_start("up", r.n2r[...], r.dprer[...])
        dn, dg2 = rms_back(mlp_total("r", 2), r.attr[...], r.gains[0, 1:2])
        r.attr[...] = dn
        r.dattr[...] = (dmlp.astype(F32) + dn).astype(BF)
        r.dor[gi] = nt(r.dattr[...], r.wp[0]).astype(BF)
        r.str[gi] = row_stats(lambda h: r.dor[gi, :, head(h)], r.mr, r.lr, r.ar)
        swaps = share(1, r.dor, r.str)
        for copy in swaps:
            copy.start()
        routed_start("proj", r.dattr[...], r.mixr[...])
        sum_z("qkv")
        sum_z("proj")
        dq_r[...] = jnp.zeros((H, RH, HD), F32)
        dk_r[...] = jnp.zeros((H, RH, HD), F32)
        dv_r[...] = jnp.zeros((H, RH, HD), F32)
        routed_loop(
            lambda ci: back_query(
                ci,
                half_rows(r.qr),
                lambda h: r.dor[gi, :, head(h)],
                part_rows(r.kr),
                part_rows(r.vr),
                routed_mask,
                r.mr,
                r.lr,
                dq_r,
            )
        )
        for copy in swaps:
            copy.wait()
        routed_loop(
            lambda ci: back_keys(
                ci,
                half_rows(r.kr),
                half_rows(r.vr),
                part_rows(r.qr),
                lambda ci, h: r.dor[pl.ds(ci * 2, 2), :, head(h)].reshape(2 * RH, HD),
                routed_mask_back,
                lambda ci, line: jnp.concatenate([r.str[ci * 2 + j][line : line + 1] for j in range(2)], axis=1),
                dk_r,
                dv_r,
            )
        )
        pack_grads(dq_r, dk_r, dv_r, r.g3r)
        mlp_start("r", 3, front_back(r.g3r, 0))
        routed_start("qkv", r.nr[...], r.g3r[...])
        sum_end("down")
        sum_end("up")
        dn, dg1 = rms_back(mlp_total("r", 3), r.chh[...].astype(F32), r.gains[0, 0:1])
        r.chg[gi] = (r.attr[...] + dn).astype(BF)
        r.gr[gi] = jnp.concatenate([dg1, dg2, jnp.zeros((6, D), F32)], axis=0)
        swaps = share(3, r.chg, r.gr)
        for copy in swaps:
            copy.start()
        for copy in swaps:
            copy.wait()
        r.rg_o[...] = jnp.sum(r.gr[...], axis=0)[0:2]
        back = nn(r.oht[...], r.chg[...].reshape(R, D))
        inp = r.inp[...].astype(F32)
        gate = jax.nn.sigmoid(jnp.sum(inp * r.router[...].reshape(1, D), axis=-1, keepdims=True))
        dlogit = jnp.sum(r.dro[...] * r.sel[...].astype(F32), axis=-1, keepdims=True) * gate * (1.0 - gate)
        r.gi_o[...] = r.dro[...] + back + dlogit * r.router[...].reshape(1, D)

        r.do_o[...] = (r.hid[...] + mlp_total("d", 2)).astype(BF)
        some = pl.ds(0, S - 1)
        remote(r.sblk.at[some], r.srec.at[some], r.sm_s.at[0], r.sm_s.at[1], s, m).wait()
        r.sm_o[...] = jnp.sum(r.srec[...], axis=0)
        for k in KINDS:
            routed_end(k)
        sum_end("qkv")
        sum_end("proj")
        for item in (keys_all, query_all, grad_all, stat_all):
            item.end()
        for k in KINDS:
            sum_sent(k)

    def layout(*refs):
        moved = [refs[i] for i in (0, 1, 2, 5, 6, 7, 8)]
        sm, rg = refs[3:5]
        moved_o = [refs[9 + i] for i in (0, 1, 2, 5, 6, 7, 8)]
        gains_o, router_o = refs[12:14]
        held, sems = refs[18:25], refs[25]
        ways = [
            (pltpu.make_async_copy(a, v, sems.at[0, i]), pltpu.make_async_copy(v, b, sems.at[1, i]))
            for i, (a, v, b) in enumerate(zip(moved, held, moved_o))
        ]
        for into, _ in ways:
            into.start()
        s = lax.axis_index("seq")
        routed = rg[:, 0:DR]
        for p in range(1, S):
            routed = jnp.where(s == p, rg[:, p * DR : (p + 1) * DR], routed)
        gains_o[0] = routed
        gains_o[1] = sm[0:2, 0:DR]
        router_o[...] = sm[2:3, 0:DR]
        for into, out in ways:
            into.wait()
            out.start()
        for _, out in ways:
            out.wait()

    def run(inp, segments, picks, gains, router, qkv, proj, up, down, cot):
        args = (
            inp,
            segments.reshape(1, T),
            picks,
            gains,
            router,
            cot,
            jnp.asarray(target),
            qkv,
            proj,
            up,
            down,
        )
        vmem = pl.BlockSpec(memory_space=pltpu.VMEM)
        hbm = pl.BlockSpec(memory_space=pl.ANY)
        res = pl.pallas_call(
            kernel,
            out_shape=[jax.ShapeDtypeStruct(sh, dt) for sh, dt in outs.values()],
            in_specs=[vmem] * 7 + [hbm] * 4,
            out_specs=[vmem] * len(outs),
            scratch_shapes=[pltpu.VMEM(sh, dt) for sh, dt in vm.values()] + [DMA(sh) for sh in sems.values()],
            compiler_params=pltpu.CompilerParams(
                collective_id=0, has_side_effects=True, vmem_limit_bytes=62 * 1024 * 1024
            ),
            name="train_step",
        )(*args)
        shapes = [
            ((T, D), BF),
            ((T, D), BF),
            ((T, D), F32),
            ((2, 2, DR), F32),
            ((1, DR), F32),
            ((2, 3, DR, W), F32),
            ((2, DR, W), F32),
            ((2, DR, F), F32),
            ((2, DR, F), F32),
        ]
        last = pl.pallas_call(
            layout,
            out_shape=[jax.ShapeDtypeStruct(sh, dt) for sh, dt in shapes],
            in_specs=[hbm] * 3 + [vmem] * 2 + [hbm] * 4,
            out_specs=[hbm] * 3 + [vmem] * 2 + [hbm] * 4,
            scratch_shapes=[pltpu.VMEM(*shapes[i]) for i in (0, 1, 2, 5, 6, 7, 8)] + [DMA((2, 7))],
            compiler_params=pltpu.CompilerParams(vmem_limit_bytes=62 * 1024 * 1024),
            name="layout",
        )(*res)
        ro, do, gi, gains_grad, router_grad, gq, gp, gu, gd = last
        gp, gd = jnp.swapaxes(gp, 1, 2), jnp.swapaxes(gd, 1, 2)
        return (ro, do, gi, gains_grad, router_grad.reshape(DR), gq, gp, gu, gd)

    return run


def solution(mesh):
    S, n = mesh.shape["seq"], mesh.shape["mlp"]

    def body(inp, segments, picks, gains, router, qkv, proj, up, down, cot):
        run = build(
            S, n, inp.shape[0], inp.shape[1], qkv.shape[-1], up.shape[-1], picks.size, picks.shape[0]
        )
        return run(inp, segments, picks, gains, router, qkv, proj, up, down, cot)

    return jax.shard_map(
        body,
        mesh=mesh,
        in_specs=(
            P("seq", None),
            P("seq"),
            P(),
            P(),
            P(),
            P(None, None, None, "mlp"),
            P(None, "mlp", None),
            P(None, None, "mlp"),
            P(None, "mlp", None),
            P("seq", None),
        ),
        out_specs=(
            P("seq", None),
            P("seq", None),
            P("seq", None),
            P(None, None, "seq"),
            P("seq"),
            P(None, None, "seq", "mlp"),
            P(None, "mlp", "seq"),
            P(None, "seq", "mlp"),
            P(None, "mlp", "seq"),
        ),
        check_vma=False,
    )
```

```python
from types import SimpleNamespace

import jax
import jax.numpy as jnp
import numpy as np
from jax import lax
from jax.experimental import pallas as pl
from jax.experimental.pallas import tpu as pltpu
from jax.sharding import PartitionSpec as P

HD = 64
G = 2048
EPS = 1e-05
NEG = -1e30
SCALE = HD**-0.5
BF = jnp.bfloat16
F32 = jnp.float32
MESH = pl.DeviceIdType.MESH
DMA = pltpu.SemaphoreType.DMA
GELU_A = 0.044715
GELU_B = float(np.sqrt(2.0 / np.pi))
WIDE = 1536
KV_CHAIN = True
DO_CHAIN = False
KINDS = ("down", "up", "proj", "qkv")


def dot(left, right, dims):
    return lax.dot_general(left, right, (dims, ((), ())), preferred_element_type=F32)


def nn(left, right):
    return dot(left, right, ((1,), (0,)))


def nt(left, right):
    return dot(left, right, ((1,), (1,)))


def tn(left, right):
    return dot(left, right, ((0,), (0,)))


def inverse_rms(x):
    return lax.rsqrt(jnp.mean(x * x, axis=-1, keepdims=True) + EPS)


def rms(x, gain):
    return x * inverse_rms(x) * gain


def rms_back(dy, x, gain):
    r = inverse_rms(x)
    gy = gain * dy
    dx = r * gy - x * (r * r * r) * jnp.mean(gy * x, axis=-1, keepdims=True)
    return dx, jnp.sum(dy * x * r, axis=0, keepdims=True)


def gelu_pair(x):
    t = jnp.tanh(GELU_B * (x + GELU_A * x * x * x))
    half = 0.5 * (1.0 + t)
    slope = half + 0.5 * x * (1.0 - t * t) * (GELU_B * (1.0 + 3.0 * GELU_A * x * x))
    return x * half, slope


def column(row):
    wide = jnp.broadcast_to(row.astype(F32), (128, row.shape[1]))
    return jnp.transpose(wide)[:, 0:1]


def chunks(extent):
    width = 384 if extent % 384 == 0 else extent
    return [(at, width) for at in range(0, extent, width)]


def build(S, n, T, D, W, F, R, groups):
    rest = S // 2
    Y = 2 ** ((rest.bit_length() - 1) // 2)
    Z = rest // Y
    ZY = Z * Y
    H = W // HD
    LEVEL = 2 * Y
    CH = LEVEL * T
    GN = R // T
    RH = R // GN
    RB = R // S
    DM = D // n
    DR = D // S
    DRP = -(-DR // 16) * 16
    ZD = Z * DRP
    QY = 2 * ZD
    FOLDED = KINDS if Z == 4 else ()
    XW = {"down": F, "up": F, "proj": W, "qkv": 3 * W}

    target = np.full((Y, 1, QY), -1, np.int32)
    for yy in range(Y):
        for core in range(2):
            for zz in range(Z):
                for j in range(DR):
                    target[yy, 0, (core * Z + zz) * DRP + j] = ((zz * Y + yy) * 2 + core) * DR + j

    ins = ["inp", "segr", "picks", "gains", "router", "cot", "target", "qkv_h", "proj_h", "up_h", "down_h"]
    outs = {
        "ro_o": ((T, D), BF),
        "do_o": ((T, D), BF),
        "gi_o": ((T, D), F32),
        "sm_o": ((8, 128), F32),
        "rg_o": ((2, D), F32),
        "qkv_o": ((2, 3, DR, W), F32),
        "proj_o": ((2, DR, W), F32),
        "up_o": ((2, DR, F), F32),
        "down_o": ((2, DR, F), F32),
    }
    vm = {
        "wq": ((2, 3, D, W), BF),
        "wp": ((2, W, D), BF),
        "wu": ((2, D, F), BF),
        "wd": ((2, F, D), BF),
        "sega": ((S, 8, T), jnp.int32),
        "segc": ((T, 1), F32),
        "oht": ((T, R), BF),
        "oh": ((R, T), BF),
        "posr": ((GN // 2, 8, 2 * RH), F32),
        "posc": ((RH, 1), F32),
        "sgr": ((GN // 2, 8, 2 * RH), F32),
        "sgc": ((RH, 1), F32),
        "part": ((S, RB, DM), BF),
        "r1": ((S, RB, DM), BF),
        "full": ((2, n * ZY, RB, DM), BF),
        "rows": ((R, D), BF),
        "nr": ((RH, D), BF),
        "chh": ((RH, D), BF),
        "qr": ((R, W), BF),
        "kr": ((R, W), BF),
        "vr": ((R, W), BF),
        "mr": ((H, RH, 1), F32),
        "lr": ((H, RH, 1), F32),
        "ar": ((H, RH, HD), F32),
        "mixr": ((RH, W), BF),
        "attr": ((RH, D), F32),
        "n2r": ((RH, D), BF),
        "prer": ((RH, F), F32),
        "actr": ((RH, F), BF),
        "xr": ((2, n, RH, D), BF),
        "xd": ((3, n, T, D), BF),
        "chg": ((GN, RH, D), BF),
        "sel": ((T, D), BF),
        "ro": ((T, D), F32),
        "nd": ((T, D), BF),
        "kva": ((S, T, 2 * W), BF),
        "qa": ((S, T, W), BF),
        "da": ((S, T, W), BF),
        "sta": ((S, 16, T), F32),
        "md": ((H, T, 1), F32),
        "ld": ((H, T, 1), F32),
        "ad": ((H, T, HD), F32),
        "hid": ((T, D), F32),
        "n2d": ((T, D), BF),
        "dact": ((T, F), F32),
        "dattn": ((T, D), BF),
        "dq": ((H, max(T, RH), HD), F32),
        "dk": ((H, max(T, RH), HD), F32),
        "dv": ((H, max(T, RH), HD), F32),
        "dro": ((T, D), F32),
        "small": ((8, D), F32),
        "sblk": ((S, 8, 128), F32),
        "srec": ((S, 8, 128), F32),
        "dor": ((GN, RH, W), BF),
        "str": ((GN, 16, RH), F32),
        "dprer": ((RH, F), BF),
        "dattr": ((RH, D), BF),
        "g3r": ((RH, 3 * W), BF),
        "gr": ((GN, 8, D), F32),
        "sele": ((Y, D, QY), BF),
    }
    for k in KINDS:
        X = XW[k]
        vm["left_" + k] = ((LEVEL, T, QY), BF)
        vm["away_" + k] = ((Y - 1, T, QY), BF)
        vm["right_" + k] = ((LEVEL, T, X), BF)
        vm["zsend_" + k] = ((Z, DRP, X), BF)
        vm["zown_" + k] = ((DRP, X), F32)
        vm["zrec_" + k] = ((Z, DRP, X), BF)
        vm["zfar_" + k] = ((DRP, X), BF)
        vm["rsend_" + k] = ((GN - 1, DRP, X), BF)
        vm["rkeep_" + k] = ((DRP, X), F32)
        vm["rrec_" + k] = ((GN - 1, DRP, X), BF)
    n_sends = (Z - 1) + (Y - 1) + 1 + (Z - 1) * Y + Z * (Y - 1)
    sems = {
        "w_s": (8,),
        "seg_s": (2,),
        "t_s": (6,),
        "xr_s": (2, n - 1),
        "xr_r": (2, n - 1),
        "xd_s": (3, n - 1),
        "xd_r": (3, n - 1),
        "sw_s": (10, GN - 1),
        "sw_r": (10, GN - 1),
        "kv_s": (n_sends,),
        "kv_r": (S,),
        "q_s": (n_sends,),
        "q_r": (S,),
        "da_s": (n_sends,),
        "da_r": (S,),
        "st_s": (n_sends,),
        "st_r": (S,),
        "sm_s": (2,),
        "gl_s": (4, 2, 2 * Y - 1),
        "gl_r": (4, 2, LEVEL),
        "gz_s": (4, Z - 1),
        "gz_r": (4, Z - 1),
    }
    names = ins + list(outs) + list(vm) + list(sems)

    def kernel(*refs):
        r = SimpleNamespace(**dict(zip(names, refs, strict=True)))
        g = r.__dict__
        s = lax.axis_index("seq")
        m = lax.axis_index("mlp")
        c = lax.rem(s, 2)
        chip = s // 2
        y = lax.rem(chip, Y)
        z = chip // Y
        sib = s + 1 - 2 * c
        gi = lax.rem(s, GN)

        def rank(zz, yy, cc):
            return (zz * Y + yy) * 2 + cc

        def remote(src, dst, send, recv, seq, mlp):
            return pltpu.make_async_remote_copy(
                src_ref=src, dst_ref=dst, send_sem=send, recv_sem=recv, device_id=(seq, mlp), device_id_type=MESH
            )

        bar = pltpu.get_barrier_semaphore()

        def greet(i, carry):
            pl.semaphore_signal(bar, inc=1, device_id=(lax.rem(s + i, S), m), device_id_type=MESH)
            return carry

        lax.fori_loop(1, S, greet, 0)
        for j in range(1, n):

            def greet_other(i, carry, j=j):
                pl.semaphore_signal(bar, inc=1, device_id=(i * 2 + c, lax.rem(m + j, n)), device_id_type=MESH)
                return carry

            lax.fori_loop(0, ZY, greet_other, 0)
        loads = [
            pltpu.make_async_copy(src.at[b], dst.at[b], r.w_s.at[4 * b + i])
            for b in range(2)
            for i, (src, dst) in enumerate(
                ((r.qkv_h, r.wq), (r.proj_h, r.wp), (r.up_h, r.wu), (r.down_h, r.wd))
            )
        ]
        prow = jnp.concatenate([r.picks[i : i + 1, :] + G * i for i in range(groups)], axis=1)
        here = s * T + lax.broadcasted_iota(jnp.int32, (T, R), 0)
        hot = jnp.where(prow == here, 1.0, 0.0)
        r.oht[...] = hot.astype(BF)
        r.oh[...] = jnp.transpose(hot).astype(BF)

        def my_columns(x):
            got = x[:, 0:DM]
            for j in range(1, n):
                got = jnp.where(m == j, x[:, j * DM : (j + 1) * DM], got)
            return got

        def scatter_rows(x):
            r.part[...] = nn(r.oh[...], my_columns(x)).astype(BF).reshape(S, RB, DM)

        scatter_rows(r.inp[...])
        def send_segments(i, carry):
            remote(r.sega.at[s], r.sega.at[s], r.seg_s.at[0], r.seg_s.at[1], lax.rem(s + i, S), m).start()
            return carry

        sem = [r.t_s.at[j] for j in range(6)]

        def spread_start():
            def first(k, carry):
                p = lax.rem(s + k, S)
                remote(r.part.at[p], r.r1.at[s], sem[0], sem[1], p, m).start()
                return carry

            lax.fori_loop(1, S, first, 0)
            r.r1[s] = r.part[s]

        def spread_end(after):
            some = pl.ds(0, S - 1)
            remote(r.part.at[some], r.r1.at[some], sem[0], sem[1], s, m).wait()
            me = m * ZY + chip
            r.full[c, me] = jnp.sum(r.r1[...].astype(F32), axis=0).astype(BF)

            def second(k, carry):
                p = lax.rem(me + k, n * ZY)
                block = r.full.at[c, me]
                remote(block, block, sem[2], sem[3], lax.rem(p, ZY) * 2 + c, p // ZY).start()
                return carry

            lax.fori_loop(1, n * ZY, second, 0)
            after()
            some = r.full.at[c, pl.ds(0, n * ZY - 1)]
            remote(some, some, sem[2], sem[3], s, m).wait()
            swap = remote(r.full.at[c], r.full.at[c], sem[4], sem[5], sib, m)
            swap.start()
            swap.wait()

            def place(k, carry):
                for cc in range(2):
                    rows = pl.ds(pl.multiple_of((k * 2 + cc) * RB, RB), RB)
                    for mm in range(n):
                        r.rows[rows, mm * DM : (mm + 1) * DM] = r.full[cc, mm * ZY + k]
                return carry

            lax.fori_loop(0, ZY, place, 0)

        def mlp_copies(buf, send, recv, i):
            i = i % buf.shape[0]
            return [
                remote(buf.at[i, m], buf.at[i, m], send.at[i, j - 1], recv.at[i, j - 1], s, lax.rem(m + j, n))
                for j in range(1, n)
            ]

        def mlp_start(which, i, value):
            buf = g["x" + which]
            buf[i % buf.shape[0], m] = value.astype(BF)
            for copy in mlp_copies(buf, g["x" + which + "_s"], g["x" + which + "_r"], i):
                copy.start()

        def mlp_total(which, i):
            buf = g["x" + which]
            for copy in mlp_copies(buf, g["x" + which + "_s"], g["x" + which + "_r"], i):
                copy.wait()
            i = i % buf.shape[0]
            total = buf[i, 0].astype(F32)
            for j in range(1, n):
                total = total + buf[i, j].astype(F32)
            return total

        def friend(j):
            return s - gi + lax.rem(gi + j, GN)

        def share(i, *refs):
            return [
                remote(ref.at[gi], ref.at[gi], r.sw_s.at[i + k, j - 1], r.sw_r.at[i + k, j - 1], friend(j), m)
                for k, ref in enumerate(refs)
                for j in range(1, GN)
            ]

        def attend_start(top, total, acc):
            top[...] = jnp.full(top.shape, NEG, F32)
            total[...] = jnp.zeros(total.shape, F32)
            acc[...] = jnp.zeros(acc.shape, F32)

        def head_groups(width):
            step = min(H, max(1, WIDE // width))
            return [range(at, min(at + step, H)) for at in range(0, H, step)]

        def attend(ci, query, key, value, mask, top, total, acc):
            kept = mask(ci)
            for group in head_groups(kept.shape[1]):
                scores = {h: nt(query(h), key(ci, h)) for h in group}
                weights = {}
                for h in group:
                    score = jnp.where(kept, scores[h], NEG)
                    old = top[h]
                    new = jnp.maximum(old, jnp.max(score, axis=-1, keepdims=True))
                    shrink = jnp.exp(old - new)
                    weight = jnp.exp(score - new)
                    total[h] = total[h] * shrink + jnp.sum(weight, axis=-1, keepdims=True)
                    acc[h] = acc[h] * shrink
                    top[h] = new
                    weights[h] = weight.astype(BF)
                for h in group:
                    acc[h] = acc[h] + nn(weights[h], value(ci, h))

        def finish(top, total, acc, mixed):
            for h in range(H):
                out = acc[h] / total[h]
                acc[h] = out
                mixed[:, h * HD : (h + 1) * HD] = out.astype(BF)
                top[h] = top[h] + jnp.log(total[h])

        def row_stats(grad, top, total, acc):
            lane = lax.broadcasted_iota(jnp.int32, (acc.shape[1], 128), 1)
            stats = jnp.zeros((acc.shape[1], 128), F32)
            for h in range(H):
                delta = jnp.sum(grad(h).astype(F32) * acc[h], axis=-1, keepdims=True)
                total[h] = delta
                stats = jnp.where(lane == h, top[h], jnp.where(lane == 8 + h, delta, stats))
            return jnp.transpose(stats)[0:16]

        def back_query(ci, query, grad, key, value, mask, log_total, delta, out):
            kept = mask(ci)
            for group in head_groups(kept.shape[1]):
                scores = {h: nt(query(h), key(ci, h)) for h in group}
                grad_probs = {h: nt(grad(h), value(ci, h)) for h in group}
                grad_scores = {}
                for h in group:
                    probs = jnp.where(kept, jnp.exp(scores[h] - log_total[h]), 0.0)
                    grad_scores[h] = (probs * (grad_probs[h] - delta[h])).astype(BF)
                for h in group:
                    out[h] = out[h] + nn(grad_scores[h], key(ci, h))

        def back_keys(ci, key, value, query, grad, mask, stat, out_key, out_value):
            kept = mask(ci)
            for group in head_groups(kept.shape[1]):
                scores = {h: nt(key(h), query(ci, h)) for h in group}
                grad_probs = {h: nt(value(h), grad(ci, h)) for h in group}
                probs, grad_scores = {}, {}
                for h in group:
                    prob = jnp.where(kept, jnp.exp(scores[h] - stat(ci, h)), 0.0)
                    grad_scores[h] = (prob * (grad_probs[h] - stat(ci, 8 + h))).astype(BF)
                    probs[h] = prob.astype(BF)
                for h in group:
                    out_value[h] = out_value[h] + nn(probs[h], grad(ci, h))
                    out_key[h] = out_key[h] + nn(grad_scores[h], query(ci, h))

        dq_d, dk_d, dv_d = (ref.at[:, 0:T] for ref in (r.dq, r.dk, r.dv))
        dq_r, dk_r, dv_r = (ref.at[:, 0:RH] for ref in (r.dq, r.dk, r.dv))

        def pack_grads(dq, dk, dv, out):
            for h in range(H):
                out[:, h * HD : (h + 1) * HD] = (dq[h] * SCALE).astype(BF)
                out[:, W + h * HD : W + (h + 1) * HD] = dk[h].astype(BF)
                out[:, 2 * W + h * HD : 2 * W + (h + 1) * HD] = dv[h].astype(BF)

        def front_back(grads, b):
            return (
                nt(grads[:, 0:W], r.wq[b, 0])
                + nt(grads[:, W : 2 * W], r.wq[b, 1])
                + nt(grads[:, 2 * W : 3 * W], r.wq[b, 2])
            )

        def loop(low, high, body):
            def step(i, carry):
                body(i)
                return carry

            lax.fori_loop(low, high, step, 0)

        def gather(buf, ss, rs, up, chain):
            sign = -1 if up else 1
            last = z if up else Z - 1 - z
            ahead = Z - 1 - z if up else z
            at_y, at_sib, at_level = Z - 1, Z + Y - 2, Z + Y - 1
            at_z = at_level + Y - 1
            at_far = at_z + (Z - 1) * Y

            def copy(slot, dst, k):
                return remote(buf.at[slot], buf.at[slot], ss.at[k], rs.at[slot], dst, m)

            def recv(slot):
                copy(slot, sib, 0).wait_recv()

            def side(dy):
                return lax.rem(y + dy, Y)

            def copies(each):
                if chain:
                    pl.when(ahead > 0)(lambda: each(copy(s, rank(z - sign, y, c), 0)))
                else:
                    loop(1, ahead + 1, lambda dz: each(copy(s, rank(z - sign * dz, y, c), dz - 1)))
                for dy in range(1, Y):
                    each(copy(s, rank(z, side(dy), c), at_y + dy - 1))
                each(copy(s, sib, at_sib))

            def level_copy(dy):
                return copy(rank(z, side(dy), c), sib, at_level + dy - 1)

            def z_copies(dz):
                slot = rank(z + sign * dz, y, c)
                k = at_z + (dz - 1) * Y
                outs = [copy(slot, rank(z, side(dy), c), k + dy - 1) for dy in range(1, Y)]
                return [*outs, copy(slot, sib, k + Y - 1)]

            def far_copy(dz, dy):
                return copy(rank(z + sign * dz, side(dy), c), sib, at_far + (dz - 1) * (Y - 1) + dy - 1)

            def start():
                copies(lambda one: one.start())

            def level():
                for dy in range(1, Y):
                    recv(rank(z, side(dy), c))
                    level_copy(dy).start()

            def level_end():
                for dy in range(Y):
                    recv(rank(z, side(dy), 1 - c))

            def onward(dz, each):
                if chain:
                    slot = rank(z + sign * dz, y, c)
                    pl.when(ahead > 0)(lambda: each(copy(slot, rank(z - sign, y, c), dz)))

            def z_step(dz):
                recv(rank(z + sign * dz, y, c))
                onward(dz, lambda one: one.start())
                for one in z_copies(dz):
                    one.start()

            def y_step(dz):
                for dy in range(1, Y):
                    recv(rank(z + sign * dz, side(dy), c))
                    far_copy(dz, dy).start()

            def sib_step(dz):
                for dy in range(Y):
                    recv(rank(z + sign * dz, side(dy), 1 - c))

            def end():
                copies(lambda one: one.wait_send())
                for dy in range(1, Y):
                    level_copy(dy).wait_send()

                def sent(dz):
                    onward(dz, lambda one: one.wait_send())
                    for one in z_copies(dz):
                        one.wait_send()
                    for dy in range(1, Y):
                        far_copy(dz, dy).wait_send()

                loop(1, last + 1, sent)

            return SimpleNamespace(
                start=start,
                level=level,
                level_end=level_end,
                z_step=z_step,
                y_step=y_step,
                sib_step=sib_step,
                end=end,
                last=last,
            )

        def walk(items, body):
            last = items[0].last

            def all_of(name, *args):
                for item in items:
                    getattr(item, name)(*args)

            pl.when(last > 0)(lambda: all_of("z_step", 1))
            all_of("level_end")
            body(0)

            def step(dz):
                all_of("y_step", dz)
                pl.when(dz < last)(lambda: all_of("z_step", dz + 1))
                all_of("sib_step", dz)
                body(dz)

            loop(1, last + 1, step)

        lev = lax.rem(s, LEVEL)

        def level_slot(dy, cc):
            return lax.rem(y + dy, Y) * 2 + cc

        def level_copy(k, side, j, src, slot, dst):
            i = KINDS.index(k)
            buf = g[("left_", "right_")[side] + k]
            return remote(src, buf.at[slot], r.gl_s.at[i, side, j], r.gl_r.at[i, side, slot], dst, m)

        def own_copies(k, side):
            mine = g[("left_", "right_")[side] + k].at[lev]
            out = [level_copy(k, side, 0, mine, lev, sib)]
            for dy in range(1, Y):
                src = g["away_" + k].at[dy - 1] if side == 0 else mine
                out.append(level_copy(k, side, dy, src, lev, rank(z, lax.rem(y + dy, Y), c)))
            return out

        def far_copies(k):
            return [
                level_copy(k, side, Y + dy - 1, g[("left_", "right_")[side] + k].at[level_slot(dy, c)], level_slot(dy, c), sib)
                for side in range(2)
                for dy in range(1, Y)
            ]

        def level_wait(k, slot):
            for side in range(2):
                buf = g[("left_", "right_")[side] + k]
                level_copy(k, side, 0, buf.at[slot], slot, sib).wait_recv()

        def sum_left(k, lhs):
            g["left_" + k][lev] = nn(lhs[...], r.sele[y]).astype(BF)
            for dy in range(1, Y):
                g["away_" + k][dy - 1] = nn(lhs[...], r.sele[lax.rem(y + dy, Y)]).astype(BF)
            for copy in own_copies(k, 0):
                copy.start()

        def sum_right(k):
            for copy in own_copies(k, 1):
                copy.start()

        def sum_far(k):
            for dy in range(1, Y):
                level_wait(k, level_slot(dy, c))
            for copy in far_copies(k):
                copy.start()

        def z_copy(k, dz):
            i = KINDS.index(k)
            return remote(
                g["zsend_" + k].at[lax.rem(z + dz, Z)],
                g["zrec_" + k].at[dz - 1],
                r.gz_s.at[i, dz - 1],
                r.gz_r.at[i, dz - 1],
                rank(lax.rem(z + dz, Z), y, c),
                m,
            )

        def sum_z(k):
            for dy in range(Y):
                level_wait(k, level_slot(dy, 1 - c))
            left = g["left_" + k][...].reshape(LEVEL * T, QY)
            left = jnp.where(c == 0, left[:, 0:ZD], left[:, ZD:QY])
            for x, w in chunks(XW[k]):
                total = tn(left, g["right_" + k][:, :, x : x + w].reshape(LEVEL * T, w)).reshape(Z, DRP, w)
                g["zsend_" + k][:, :, x : x + w] = total.astype(BF)
                own = total[0]
                for zz in range(1, Z):
                    own = jnp.where(z == zz, total[zz], own)
                g["zown_" + k][:, x : x + w] = own
            if k in FOLDED:
                fold_first(k, lambda one: one.start())
            else:
                for dz in range(1, Z):
                    z_copy(k, dz).start()

        edge = (z == 0) | (z == Z - 1)
        low_half = z < 2
        near = jnp.where(low_half, jnp.where(z == 0, 1, 0), jnp.where(z == 3, 2, 3))
        three = pl.ds(jnp.where(low_half, 1, 0), 3)

        def fold_first(k, then):
            i = KINDS.index(k)
            one = pl.ds(near, 1)
            for cond, blocks in ((edge, three), (jnp.logical_not(edge), one)):
                pl.when(cond)(
                    lambda blocks=blocks: then(
                        remote(
                            g["zsend_" + k].at[blocks],
                            g["zrec_" + k].at[blocks],
                            r.gz_s.at[i, 0],
                            r.gz_r.at[i, 0],
                            rank(near, y, c),
                            m,
                        )
                    )
                )

        def fold_copies(k):
            i = KINDS.index(k)
            far = (3 - z, jnp.where(low_half, 3, 0))
            return [
                remote(
                    g["zsend_" + k].at[b],
                    g["zfar_" + k],
                    r.gz_s.at[i, 1 + j],
                    r.gz_r.at[i, 1],
                    rank(b, y, c),
                    m,
                )
                for j, b in enumerate(far)
            ]

        def fold_recv(k, blocks):
            i = KINDS.index(k)
            some = g["zrec_" + k].at[blocks]
            remote(some, some, r.gz_s.at[i, 0], r.gz_r.at[i, 0], sib, m).wait_recv()

        def sum_mid(k):
            if k not in FOLDED:
                return

            def work():
                fold_recv(k, three)
                for b, copy in zip((3 - z, jnp.where(low_half, 3, 0)), fold_copies(k)):
                    t = g["zsend_" + k][b].astype(F32) + g["zrec_" + k][b].astype(F32)
                    g["zsend_" + k][b] = t.astype(BF)
                    copy.start()

            pl.when(jnp.logical_not(edge))(work)

        def fold_end(k):
            i = KINDS.index(k)
            pl.when(edge)(lambda: fold_recv(k, pl.ds(z, 1)))
            far = g["zfar_" + k]
            remote(far, far, r.gz_s.at[i, 1], r.gz_r.at[i, 1], sib, m).wait_recv()
            fold_first(k, lambda one: one.wait_send())

            def sent():
                for copy in fold_copies(k):
                    copy.wait_send()

            pl.when(jnp.logical_not(edge))(sent)
            t = g["zown_" + k][...] + g["zrec_" + k][z].astype(F32) + far[...].astype(F32)
            put(1, k, t)

        def put(b, k, value):
            if k == "qkv":
                for j in range(3):
                    r.qkv_o[b, j] = value[0:DR, j * W : (j + 1) * W]
            else:
                g[k + "_o"][b] = value[0:DR]

        def sum_end(k):
            if k in FOLDED:
                return fold_end(k)
            t = g["zown_" + k][...]
            for dz in range(1, Z):
                z_copy(k, dz).wait()
                t = t + g["zrec_" + k][dz - 1].astype(F32)
            put(1, k, t)

        def sum_sent(k):
            for side in range(2):
                for copy in own_copies(k, side):
                    copy.wait_send()
            for copy in far_copies(k):
                copy.wait_send()

        def routed_copy(k, j):
            i = 6 + KINDS.index(k)
            send, recv = r.sw_s.at[i, j - 1], r.sw_r.at[i, j - 1]
            return remote(g["rsend_" + k].at[j - 1], g["rrec_" + k].at[j - 1], send, recv, friend(j), m)

        def routed_start(k, lhs, rhs):
            col = lax.broadcasted_iota(jnp.int32, (D, DRP), 1)
            row = lax.broadcasted_iota(jnp.int32, (D, DRP), 0)

            def block(who):
                hit = (row - who * DR == col) & (col < DR)
                return nn(lhs, jnp.where(hit, 1.0, 0.0).astype(BF)).astype(BF)

            for j in range(1, GN):
                g["rsend_" + k][j - 1] = tn(block(friend(j)), rhs).astype(BF)
                routed_copy(k, j).start()
            g["rkeep_" + k][...] = tn(block(s), rhs)

        def routed_end(k):
            t = g["rkeep_" + k][...]
            for j in range(1, GN):
                routed_copy(k, j).wait()
                t = t + g["rrec_" + k][j - 1].astype(F32)
            put(0, k, t)

        def head(h):
            return slice(h * HD, (h + 1) * HD)

        pl.semaphore_wait(bar, S - 1 + (n - 1) * ZY)
        spread_start()
        r.sega[s] = jnp.broadcast_to(r.segr[...], (8, T))
        for load in loads:
            load.start()
        prow_f = prow.astype(F32)
        for i in range(GN // 2):
            r.posr[i] = jnp.broadcast_to(prow_f[:, i * 2 * RH : (i + 1) * 2 * RH], (8, 2 * RH))
        mine = r.posr[gi // 2][0:1]
        r.posc[...] = column(jnp.where(lax.rem(gi, 2) == 0, mine[:, 0:RH], mine[:, RH : 2 * RH]))
        r.segc[...] = column(r.segr[...])
        for yy in range(Y):
            ids = lax.broadcasted_iota(jnp.int32, (D, QY), 0)
            r.sele[yy] = jnp.where(ids == r.target[yy], 1.0, 0.0).astype(BF)
        spread_end(lambda: lax.fori_loop(1, S, send_segments, 0))
        some = pl.ds(0, S - 1)
        remote(r.sega.at[some], r.sega.at[some], r.seg_s.at[0], r.seg_s.at[1], s, m).wait()
        starts = [
            jnp.sum(
                jnp.sum(jnp.where(r.sega[...] < k, 0.125, 0.0), axis=0), axis=(0, 1), keepdims=True
            )
            for k in range(1, 5)
        ]
        for i in range(GN // 2):
            r.sgr[i] = sum(jnp.where(r.posr[i] >= at, 1.0, 0.0) for at in starts)
        r.sgc[...] = sum(jnp.where(r.posc[...] >= at, 1.0, 0.0) for at in starts)
        half = pl.ds(pl.multiple_of(gi * RH, RH), RH)

        loads[0].wait()
        r.chh[...] = r.rows[half, :]
        r.nr[...] = rms(r.chh[...].astype(F32), r.gains[0, 0:1]).astype(BF)
        for at in range(0, R, 256):
            part = slice(at, at + 256)
            normed = rms(r.rows[part].astype(F32), r.gains[0, 0:1]).astype(BF)
            r.qr[part] = (nn(normed, r.wq[0, 0]).astype(BF) * SCALE).astype(BF)
            r.kr[part] = nn(normed, r.wq[0, 1]).astype(BF)
            r.vr[part] = nn(normed, r.wq[0, 2]).astype(BF)

        def part_rows(ref):
            return lambda ci, h: ref[pl.ds(pl.multiple_of(ci * 2 * RH, RH), 2 * RH), head(h)]

        def half_rows(ref):
            return lambda h: ref[half, head(h)]

        def routed_mask(ci):
            return (r.sgr[ci][0:1] == r.sgc[...]) & (r.posr[ci][0:1] <= r.posc[...])

        def routed_mask_back(ci):
            return (r.sgr[ci][0:1] == r.sgc[...]) & (r.posc[...] <= r.posr[ci][0:1])

        def routed_pick(i):
            return lax.rem(gi // 2 + i, GN // 2)

        def routed_loop(body):
            if GN == 2:
                body(0)
            else:
                loop(0, GN // 2, lambda i: body(routed_pick(i)))

        attend_start(r.mr, r.lr, r.ar)
        routed_loop(
            lambda ci: attend(
                ci, half_rows(r.qr), part_rows(r.kr), part_rows(r.vr), routed_mask, r.mr, r.lr, r.ar
            )
        )
        finish(r.mr, r.lr, r.ar, r.mixr)
        loads[1].wait()
        mlp_start("r", 0, nn(r.mixr[...], r.wp[0]))
        sum_left("down", r.cot)
        loads[2].wait()
        loads[3].wait()
        attn = mlp_total("r", 0)
        r.attr[...] = attn
        normed = rms(r.chh[...].astype(F32) + attn, r.gains[0, 1:2]).astype(BF)
        r.n2r[...] = normed
        for x, w in chunks(F):
            pre = nn(normed, r.wu[0, :, x : x + w])
            r.prer[:, x : x + w] = pre
            r.actr[:, x : x + w] = gelu_pair(pre)[0].astype(BF)
        mlp_start("r", 1, nn(r.actr[...], r.wd[0]))
        mlp = mlp_total("r", 1)
        r.chg[gi] = (r.attr[...] + mlp).astype(BF)
        swaps = share(0, r.chg)
        for copy in swaps:
            copy.start()
        inp = r.inp[...].astype(F32)
        gate = jax.nn.sigmoid(jnp.sum(inp * r.router[...].reshape(1, D), axis=-1, keepdims=True))
        for load in loads[4:]:
            load.wait()
        for copy in swaps:
            copy.wait()

        sel = nn(r.oht[...], r.chg[...].reshape(R, D))
        r.sel[...] = sel.astype(BF)
        ro = inp + gate * sel
        r.ro[...] = ro
        r.ro_o[...] = ro.astype(BF)
        normed = rms(ro, r.gains[1, 0:1]).astype(BF)
        r.nd[...] = normed
        r.kva[s, :, 0:W] = nn(normed, r.wq[1, 1]).astype(BF)
        r.kva[s, :, W : 2 * W] = nn(normed, r.wq[1, 2]).astype(BF)
        keys_all = gather(r.kva, r.kv_s, r.kv_r, True, KV_CHAIN)
        keys_all.start()
        r.qa[s] = (nn(normed, r.wq[1, 0]).astype(BF) * SCALE).astype(BF)
        query_all = gather(r.qa, r.q_s, r.q_r, False, False)
        query_all.start()
        keys_all.level()
        query_all.level()

        def level_rows(ref, first=0):
            def get(ci, h):
                return ref[pl.ds(ci * LEVEL, LEVEL), :, head(first + h)].reshape(CH, HD)

            return get

        def level_line(ref, line):
            return lambda ci: jnp.concatenate([ref[ci * LEVEL + j][line : line + 1] for j in range(LEVEL)], axis=1)

        own_pos = lax.broadcasted_iota(jnp.int32, (T, CH), 0) + s * T
        far_pos = lax.broadcasted_iota(jnp.int32, (T, CH), 1)
        seg_line = level_line(r.sega, 0)

        def dense_mask(ci):
            return (seg_line(ci).astype(F32) == r.segc[...]) & (far_pos + ci * CH <= own_pos)

        def dense_mask_back(ci):
            return (seg_line(ci).astype(F32) == r.segc[...]) & (own_pos <= far_pos + ci * CH)

        attend_start(r.md, r.ld, r.ad)
        walk(
            [keys_all],
            lambda dz: attend(
                z - dz,
                lambda h: r.qa[s, :, head(h)],
                level_rows(r.kva),
                level_rows(r.kva, H),
                dense_mask,
                r.md,
                r.ld,
                r.ad,
            ),
        )
        finish(r.md, r.ld, r.ad, r.right_proj.at[lev])
        mlp_start("d", 0, nn(r.right_proj[lev], r.wp[1]))
        loop(1, query_all.last + 1, query_all.z_step)
        sum_left("qkv", r.nd)
        for x, w in chunks(F):
            r.dact[:, x : x + w] = nt(r.cot[...], r.wd[1, x : x + w, :])
        attn = mlp_total("d", 0)
        hid = r.ro[...] + attn
        r.hid[...] = hid
        normed = rms(hid, r.gains[1, 1:2]).astype(BF)
        r.n2d[...] = normed
        for x, w in chunks(F):
            active, slope = gelu_pair(nn(normed, r.wu[1, :, x : x + w]))
            r.right_down[lev, :, x : x + w] = active.astype(BF)
            r.right_up[lev, :, x : x + w] = (r.dact[:, x : x + w] * slope).astype(BF)
        sum_right("down")
        mlp_start("d", 1, nt(r.right_up[lev], r.wu[1]))
        mlp_start("d", 2, nn(r.right_down[lev], r.wd[1]))

        sum_left("up", r.n2d)
        loop(1, query_all.last + 1, query_all.y_step)
        dn, dg = rms_back(mlp_total("d", 1), r.hid[...], r.gains[1, 1:2])
        r.small[1:2] = dg
        dhid = r.cot[...].astype(F32) + dn
        r.dro[...] = dhid
        r.dattn[...] = dhid.astype(BF)
        r.da[s] = nt(r.dattn[...], r.wp[1]).astype(BF)
        r.sta[s] = row_stats(lambda h: r.da[s, :, head(h)], r.md, r.ld, r.ad)
        grad_all = gather(r.da, r.da_s, r.da_r, False, DO_CHAIN)
        stat_all = gather(r.sta, r.st_s, r.st_r, False, DO_CHAIN)
        for item in (grad_all, stat_all):
            item.start()
        for item in (grad_all, stat_all):
            item.level()
        sum_right("up")
        query_all.level_end()
        loop(1, query_all.last + 1, query_all.sib_step)
        dq_d[...] = jnp.zeros((H, T, HD), F32)
        dk_d[...] = jnp.zeros((H, T, HD), F32)
        dv_d[...] = jnp.zeros((H, T, HD), F32)
        loop(
            0,
            z + 1,
            lambda dz: back_query(
                z - dz,
                lambda h: r.qa[s, :, head(h)],
                lambda h: r.da[s, :, head(h)],
                level_rows(r.kva),
                level_rows(r.kva, H),
                dense_mask,
                r.md,
                r.ld,
                dq_d,
            ),
        )
        walk(
            [grad_all, stat_all],
            lambda dz: back_keys(
                z + dz,
                lambda h: r.kva[s, :, head(h)],
                lambda h: r.kva[s, :, head(H + h)],
                level_rows(r.qa),
                level_rows(r.da),
                dense_mask_back,
                lambda ci, line: level_line(r.sta, line)(ci),
                dk_d,
                dv_d,
            ),
        )
        sum_far("down")
        sum_far("up")
        sum_z("down")
        pack_grads(dq_d, dk_d, dv_d, r.right_qkv.at[lev])
        mlp_start("d", 3, front_back(r.right_qkv.at[lev], 1))
        sum_left("proj", r.dattn)
        sum_right("qkv")
        sum_right("proj")
        dn, dg = rms_back(mlp_total("d", 3), r.ro[...], r.gains[1, 0:1])
        r.small[0:1] = dg
        dro = r.dro[...] + dn
        r.dro[...] = dro

        sel = r.sel[...].astype(F32)
        inp = r.inp[...].astype(F32)
        gate = jax.nn.sigmoid(jnp.sum(inp * r.router[...].reshape(1, D), axis=-1, keepdims=True))
        dlogit = jnp.sum(dro * sel, axis=-1, keepdims=True) * gate * (1.0 - gate)
        scatter_rows((gate * dro).astype(BF))
        spread_start()
        r.small[2:3] = jnp.sum(inp * dlogit, axis=0, keepdims=True)

        def in_wait():
            pass
            sum_mid("down")
            sum_z("up")

        spread_end(in_wait)
        sum_far("qkv")
        sum_far("proj")

        dmlp = r.rows[half, :]
        r.attr[...] = r.attr[...] + r.chh[...].astype(F32)
        for x, w in chunks(F):
            grad_active = nt(dmlp, r.wd[0, x : x + w, :])
            r.dprer[:, x : x + w] = (grad_active * gelu_pair(r.prer[:, x : x + w])[1]).astype(BF)
        mlp_start("r", 2, nt(r.dprer[...], r.wu[0]))
        routed_start("down", dmlp, r.actr[...])
        routed_start("up", r.n2r[...], r.dprer[...])
        r.small[3:8] = jnp.zeros((5, D), F32)
        r.sblk[...] = jnp.zeros((S, 8, 128), F32)
        for p in range(S):
            r.sblk[p, :, 0:DR] = r.small[:, p * DR : (p + 1) * DR]

        def send_small(i, carry):
            p = lax.rem(s + i, S)
            remote(r.sblk.at[p], r.srec.at[s], r.sm_s.at[0], r.sm_s.at[1], p, m).start()
            return carry

        lax.fori_loop(1, S, send_small, 0)
        r.srec[s] = r.sblk[s]
        dn, dg2 = rms_back(mlp_total("r", 2), r.attr[...], r.gains[0, 1:2])
        r.attr[...] = dn
        r.dattr[...] = (dmlp.astype(F32) + dn).astype(BF)
        r.dor[gi] = nt(r.dattr[...], r.wp[0]).astype(BF)
        r.str[gi] = row_stats(lambda h: r.dor[gi, :, head(h)], r.mr, r.lr, r.ar)
        swaps = share(1, r.dor, r.str)
        for copy in swaps:
            copy.start()
        routed_start("proj", r.dattr[...], r.mixr[...])
        sum_mid("up")
        sum_z("qkv")
        sum_z("proj")
        dq_r[...] = jnp.zeros((H, RH, HD), F32)
        dk_r[...] = jnp.zeros((H, RH, HD), F32)
        dv_r[...] = jnp.zeros((H, RH, HD), F32)
        routed_loop(
            lambda ci: back_query(
                ci,
                half_rows(r.qr),
                lambda h: r.dor[gi, :, head(h)],
                part_rows(r.kr),
                part_rows(r.vr),
                routed_mask,
                r.mr,
                r.lr,
                dq_r,
            )
        )
        for copy in swaps:
            copy.wait()
        routed_loop(
            lambda ci: back_keys(
                ci,
                half_rows(r.kr),
                half_rows(r.vr),
                part_rows(r.qr),
                lambda ci, h: r.dor[pl.ds(ci * 2, 2), :, head(h)].reshape(2 * RH, HD),
                routed_mask_back,
                lambda ci, line: jnp.concatenate([r.str[ci * 2 + j][line : line + 1] for j in range(2)], axis=1),
                dk_r,
                dv_r,
            )
        )
        pack_grads(dq_r, dk_r, dv_r, r.g3r)
        mlp_start("r", 3, front_back(r.g3r, 0))
        routed_start("qkv", r.nr[...], r.g3r[...])
        sum_end("down")
        sum_mid("qkv")
        sum_mid("proj")
        dn, dg1 = rms_back(mlp_total("r", 3), r.chh[...].astype(F32), r.gains[0, 0:1])
        r.chg[gi] = (r.attr[...] + dn).astype(BF)
        r.gr[gi] = jnp.concatenate([dg1, dg2, jnp.zeros((6, D), F32)], axis=0)
        swaps = share(3, r.chg, r.gr)
        for copy in swaps:
            copy.start()
        for copy in swaps:
            copy.wait()
        r.rg_o[...] = jnp.sum(r.gr[...], axis=0)[0:2]
        back = nn(r.oht[...], r.chg[...].reshape(R, D))
        inp = r.inp[...].astype(F32)
        gate = jax.nn.sigmoid(jnp.sum(inp * r.router[...].reshape(1, D), axis=-1, keepdims=True))
        dlogit = jnp.sum(r.dro[...] * r.sel[...].astype(F32), axis=-1, keepdims=True) * gate * (1.0 - gate)
        r.gi_o[...] = r.dro[...] + back + dlogit * r.router[...].reshape(1, D)

        r.do_o[...] = (r.hid[...] + mlp_total("d", 2)).astype(BF)
        some = pl.ds(0, S - 1)
        remote(r.sblk.at[some], r.srec.at[some], r.sm_s.at[0], r.sm_s.at[1], s, m).wait()
        r.sm_o[...] = jnp.sum(r.srec[...], axis=0)
        for k in KINDS:
            routed_end(k)
        sum_end("up")
        sum_end("qkv")
        sum_end("proj")
        for item in (keys_all, query_all, grad_all, stat_all):
            item.end()
        for k in KINDS:
            sum_sent(k)

    def layout(*refs):
        moved = [refs[i] for i in (0, 1, 2, 5, 6, 7, 8)]
        sm, rg = refs[3:5]
        moved_o = [refs[9 + i] for i in (0, 1, 2, 5, 6, 7, 8)]
        gains_o, router_o = refs[12:14]
        held, sems = refs[18:25], refs[25]
        ways = [
            (pltpu.make_async_copy(a, v, sems.at[0, i]), pltpu.make_async_copy(v, b, sems.at[1, i]))
            for i, (a, v, b) in enumerate(zip(moved, held, moved_o))
        ]
        for into, _ in ways:
            into.start()
        s = lax.axis_index("seq")
        routed = rg[:, 0:DR]
        for p in range(1, S):
            routed = jnp.where(s == p, rg[:, p * DR : (p + 1) * DR], routed)
        gains_o[0] = routed
        gains_o[1] = sm[0:2, 0:DR]
        router_o[...] = sm[2:3, 0:DR]
        for into, out in ways:
            into.wait()
            out.start()
        for _, out in ways:
            out.wait()

    def run(inp, segments, picks, gains, router, qkv, proj, up, down, cot):
        args = (
            inp,
            segments.reshape(1, T),
            picks,
            gains,
            router,
            cot,
            jnp.asarray(target),
            qkv,
            proj,
            up,
            down,
        )
        vmem = pl.BlockSpec(memory_space=pltpu.VMEM)
        hbm = pl.BlockSpec(memory_space=pl.ANY)
        res = pl.pallas_call(
            kernel,
            out_shape=[jax.ShapeDtypeStruct(sh, dt) for sh, dt in outs.values()],
            in_specs=[vmem] * 7 + [hbm] * 4,
            out_specs=[vmem] * len(outs),
            scratch_shapes=[pltpu.VMEM(sh, dt) for sh, dt in vm.values()] + [DMA(sh) for sh in sems.values()],
            compiler_params=pltpu.CompilerParams(
                collective_id=0, has_side_effects=True, vmem_limit_bytes=62 * 1024 * 1024
            ),
            name="train_step",
        )(*args)
        shapes = [
            ((T, D), BF),
            ((T, D), BF),
            ((T, D), F32),
            ((2, 2, DR), F32),
            ((1, DR), F32),
            ((2, 3, DR, W), F32),
            ((2, DR, W), F32),
            ((2, DR, F), F32),
            ((2, DR, F), F32),
        ]
        last = pl.pallas_call(
            layout,
            out_shape=[jax.ShapeDtypeStruct(sh, dt) for sh, dt in shapes],
            in_specs=[hbm] * 3 + [vmem] * 2 + [hbm] * 4,
            out_specs=[hbm] * 3 + [vmem] * 2 + [hbm] * 4,
            scratch_shapes=[pltpu.VMEM(*shapes[i]) for i in (0, 1, 2, 5, 6, 7, 8)] + [DMA((2, 7))],
            compiler_params=pltpu.CompilerParams(vmem_limit_bytes=62 * 1024 * 1024),
            name="layout",
        )(*res)
        ro, do, gi, gains_grad, router_grad, gq, gp, gu, gd = last
        gp, gd = jnp.swapaxes(gp, 1, 2), jnp.swapaxes(gd, 1, 2)
        return (ro, do, gi, gains_grad, router_grad.reshape(DR), gq, gp, gu, gd)

    return run


def solution(mesh):
    S, n = mesh.shape["seq"], mesh.shape["mlp"]

    def body(inp, segments, picks, gains, router, qkv, proj, up, down, cot):
        run = build(
            S, n, inp.shape[0], inp.shape[1], qkv.shape[-1], up.shape[-1], picks.size, picks.shape[0]
        )
        return run(inp, segments, picks, gains, router, qkv, proj, up, down, cot)

    return jax.shard_map(
        body,
        mesh=mesh,
        in_specs=(
            P("seq", None),
            P("seq"),
            P(),
            P(),
            P(),
            P(None, None, None, "mlp"),
            P(None, "mlp", None),
            P(None, None, "mlp"),
            P(None, "mlp", None),
            P("seq", None),
        ),
        out_specs=(
            P("seq", None),
            P("seq", None),
            P("seq", None),
            P(None, None, "seq"),
            P("seq"),
            P(None, None, "seq", "mlp"),
            P(None, "mlp", "seq"),
            P(None, "seq", "mlp"),
            P(None, "mlp", "seq"),
        ),
        check_vma=False,
    )
```

```python
from types import SimpleNamespace

import jax
import jax.numpy as jnp
import numpy as np
from jax import lax
from jax.experimental import pallas as pl
from jax.experimental.pallas import tpu as pltpu
from jax.sharding import PartitionSpec as P

HD = 64
G = 2048
EPS = 1e-05
NEG = -1e30
SCALE = HD**-0.5
BF = jnp.bfloat16
F32 = jnp.float32
MESH = pl.DeviceIdType.MESH
DMA = pltpu.SemaphoreType.DMA
GELU_A = 0.044715
GELU_B = float(np.sqrt(2.0 / np.pi))
WIDE = 1536
KV_CHAIN = True
DO_CHAIN = False
REDONE = ("down", "up")
KINDS = ("down", "up", "proj", "qkv")


def dot(left, right, dims):
    return lax.dot_general(left, right, (dims, ((), ())), preferred_element_type=F32)


def nn(left, right):
    return dot(left, right, ((1,), (0,)))


def nt(left, right):
    return dot(left, right, ((1,), (1,)))


def tn(left, right):
    return dot(left, right, ((0,), (0,)))


def inverse_rms(x):
    return lax.rsqrt(jnp.mean(x * x, axis=-1, keepdims=True) + EPS)


def rms(x, gain):
    return x * inverse_rms(x) * gain


def rms_back(dy, x, gain):
    r = inverse_rms(x)
    gy = gain * dy
    dx = r * gy - x * (r * r * r) * jnp.mean(gy * x, axis=-1, keepdims=True)
    return dx, jnp.sum(dy * x * r, axis=0, keepdims=True)


def gelu_pair(x):
    t = jnp.tanh(GELU_B * (x + GELU_A * x * x * x))
    half = 0.5 * (1.0 + t)
    slope = half + 0.5 * x * (1.0 - t * t) * (GELU_B * (1.0 + 3.0 * GELU_A * x * x))
    return x * half, slope


def column(row):
    wide = jnp.broadcast_to(row.astype(F32), (128, row.shape[1]))
    return jnp.transpose(wide)[:, 0:1]


def chunks(extent):
    width = 384 if extent % 384 == 0 else extent
    return [(at, width) for at in range(0, extent, width)]


def build(S, n, T, D, W, F, R, groups):
    rest = S // 2
    Y = 2 ** ((rest.bit_length() - 1) // 2)
    Z = rest // Y
    ZY = Z * Y
    H = W // HD
    LEVEL = 2 * Y
    CH = LEVEL * T
    GN = R // T
    RH = R // GN
    RB = R // S
    DM = D // n
    DR = D // S
    DRP = -(-DR // 16) * 16
    ZD = Z * DRP
    QY = 2 * ZD
    FOLDED = KINDS if Z == 4 else ()
    XW = {"down": F, "up": F, "proj": W, "qkv": 3 * W}

    target = np.full((Y, 1, QY), -1, np.int32)
    for yy in range(Y):
        for core in range(2):
            for zz in range(Z):
                for j in range(DR):
                    target[yy, 0, (core * Z + zz) * DRP + j] = ((zz * Y + yy) * 2 + core) * DR + j

    ins = ["inp", "segr", "picks", "gains", "router", "cot", "target", "qkv_h", "proj_h", "up_h", "down_h"]
    outs = {
        "ro_o": ((T, D), BF),
        "do_o": ((T, D), BF),
        "gi_o": ((T, D), F32),
        "sm_o": ((8, 128), F32),
        "rg_o": ((2, D), F32),
        "qkv_o": ((2, 3, DR, W), F32),
        "proj_o": ((2, DR, W), F32),
        "up_o": ((2, DR, F), F32),
        "down_o": ((2, DR, F), F32),
    }
    vm = {
        "wq": ((2, 3, D, W), BF),
        "wp": ((2, W, D), BF),
        "wu": ((2, D, F), BF),
        "wd": ((2, F, D), BF),
        "sega": ((S, 8, T), jnp.int32),
        "segc": ((T, 1), F32),
        "oht": ((T, R), BF),
        "oh": ((R, T), BF),
        "posr": ((GN // 2, 8, 2 * RH), F32),
        "posc": ((RH, 1), F32),
        "sgr": ((GN // 2, 8, 2 * RH), F32),
        "sgc": ((RH, 1), F32),
        "part": ((S, RB, DM), BF),
        "r1": ((S, RB, DM), BF),
        "full": ((2, n * ZY, RB, DM), BF),
        "rows": ((R, D), BF),
        "nr": ((RH, D), BF),
        "chh": ((RH, D), BF),
        "qr": ((R, W), BF),
        "kr": ((R, W), BF),
        "vr": ((R, W), BF),
        "mr": ((H, RH, 1), F32),
        "lr": ((H, RH, 1), F32),
        "ar": ((H, RH, HD), F32),
        "mixr": ((RH, W), BF),
        "attr": ((RH, D), F32),
        "n2r": ((RH, D), BF),
        "prer": ((RH, F), F32),
        "actr": ((RH, F), BF),
        "xr": ((2, n, RH, D), BF),
        "xd": ((3, n, T, D), BF),
        "chg": ((GN, RH, D), BF),
        "sel": ((T, D), BF),
        "ro": ((T, D), F32),
        "nd": ((T, D), BF),
        "kall": ((S, T, W), BF),
        "vall": ((S, T, W), BF),
        "qa": ((S, T, W), BF),
        "da": ((S, T, W), BF),
        "sta": ((S, 16, T), F32),
        "md": ((H, T, 1), F32),
        "ld": ((H, T, 1), F32),
        "ad": ((H, T, HD), F32),
        "hid": ((T, D), F32),
        "n2d": ((T, D), BF),
        "dact": ((T, F), F32),
        "nbr": ((2, Y - 1, T, D), BF),
        "dactn": ((Y - 1, T, F), F32),
        "dattn": ((T, D), BF),
        "dq": ((H, max(T, RH), HD), F32),
        "dk": ((H, max(T, RH), HD), F32),
        "dv": ((H, max(T, RH), HD), F32),
        "dro": ((T, D), F32),
        "small": ((8, D), F32),
        "sblk": ((S, 8, 128), F32),
        "srec": ((S, 8, 128), F32),
        "dor": ((GN, RH, W), BF),
        "str": ((GN, 16, RH), F32),
        "dprer": ((RH, F), BF),
        "dattr": ((RH, D), BF),
        "g3r": ((RH, 3 * W), BF),
        "gr": ((GN, 8, D), F32),
        "sele": ((Y, D, QY), BF),
    }
    for k in KINDS:
        X = XW[k]
        vm["left_" + k] = ((LEVEL, T, QY), BF)
        if k not in REDONE:
            vm["away_" + k] = ((Y - 1, T, QY), BF)
        vm["right_" + k] = ((LEVEL, T, X), BF)
        vm["zsend_" + k] = ((Z, DRP, X), BF)
        vm["zown_" + k] = ((DRP, X), F32)
        vm["zrec_" + k] = ((Z, DRP, X), BF)
        vm["zfar_" + k] = ((DRP, X), BF)
        vm["rsend_" + k] = ((GN - 1, DRP, X), BF)
        vm["rkeep_" + k] = ((DRP, X), F32)
        vm["rrec_" + k] = ((GN - 1, DRP, X), BF)
    n_sends = (Z - 1) + (Y - 1) + 1 + (Z - 1) * Y + Z * (Y - 1)
    sems = {
        "w_s": (8,),
        "seg_s": (2,),
        "t_s": (6,),
        "xr_s": (2, n - 1),
        "xr_r": (2, n - 1),
        "xd_s": (3, n - 1),
        "xd_r": (3, n - 1),
        "sw_s": (10, GN - 1),
        "sw_r": (10, GN - 1),
        "k_s": (n_sends,),
        "k_r": (S,),
        "v_s": (n_sends,),
        "v_r": (S,),
        "q_s": (n_sends,),
        "q_r": (S,),
        "da_s": (n_sends,),
        "da_r": (S,),
        "st_s": (n_sends,),
        "st_r": (S,),
        "sm_s": (2,),
        "gn_s": (2, Y - 1),
        "gn_r": (2, Y - 1),
        "gl_s": (4, 2, 2 * Y - 1),
        "gl_r": (4, 2, LEVEL),
        "gz_s": (4, Z - 1),
        "gz_r": (4, Z - 1),
    }
    names = ins + list(outs) + list(vm) + list(sems)

    def kernel(*refs):
        r = SimpleNamespace(**dict(zip(names, refs, strict=True)))
        g = r.__dict__
        s = lax.axis_index("seq")
        m = lax.axis_index("mlp")
        c = lax.rem(s, 2)
        chip = s // 2
        y = lax.rem(chip, Y)
        z = chip // Y
        sib = s + 1 - 2 * c
        gi = lax.rem(s, GN)

        def rank(zz, yy, cc):
            return (zz * Y + yy) * 2 + cc

        def remote(src, dst, send, recv, seq, mlp):
            return pltpu.make_async_remote_copy(
                src_ref=src, dst_ref=dst, send_sem=send, recv_sem=recv, device_id=(seq, mlp), device_id_type=MESH
            )

        bar = pltpu.get_barrier_semaphore()

        def greet(i, carry):
            pl.semaphore_signal(bar, inc=1, device_id=(lax.rem(s + i, S), m), device_id_type=MESH)
            return carry

        lax.fori_loop(1, S, greet, 0)
        for j in range(1, n):

            def greet_other(i, carry, j=j):
                pl.semaphore_signal(bar, inc=1, device_id=(i * 2 + c, lax.rem(m + j, n)), device_id_type=MESH)
                return carry

            lax.fori_loop(0, ZY, greet_other, 0)
        loads = [
            pltpu.make_async_copy(src.at[b], dst.at[b], r.w_s.at[4 * b + i])
            for b in range(2)
            for i, (src, dst) in enumerate(
                ((r.qkv_h, r.wq), (r.proj_h, r.wp), (r.up_h, r.wu), (r.down_h, r.wd))
            )
        ]
        prow = jnp.concatenate([r.picks[i : i + 1, :] + G * i for i in range(groups)], axis=1)
        here = s * T + lax.broadcasted_iota(jnp.int32, (T, R), 0)
        hot = jnp.where(prow == here, 1.0, 0.0)
        r.oht[...] = hot.astype(BF)
        r.oh[...] = jnp.transpose(hot).astype(BF)

        def my_columns(x):
            got = x[:, 0:DM]
            for j in range(1, n):
                got = jnp.where(m == j, x[:, j * DM : (j + 1) * DM], got)
            return got

        def scatter_rows(x):
            r.part[...] = nn(r.oh[...], my_columns(x)).astype(BF).reshape(S, RB, DM)

        scatter_rows(r.inp[...])
        def send_segments(i, carry):
            remote(r.sega.at[s], r.sega.at[s], r.seg_s.at[0], r.seg_s.at[1], lax.rem(s + i, S), m).start()
            return carry

        sem = [r.t_s.at[j] for j in range(6)]

        def spread_start():
            def first(k, carry):
                p = lax.rem(s + k, S)
                remote(r.part.at[p], r.r1.at[s], sem[0], sem[1], p, m).start()
                return carry

            lax.fori_loop(1, S, first, 0)
            r.r1[s] = r.part[s]

        def spread_end(after):
            some = pl.ds(0, S - 1)
            remote(r.part.at[some], r.r1.at[some], sem[0], sem[1], s, m).wait()
            me = m * ZY + chip
            r.full[c, me] = jnp.sum(r.r1[...].astype(F32), axis=0).astype(BF)

            def second(k, carry):
                p = lax.rem(me + k, n * ZY)
                block = r.full.at[c, me]
                remote(block, block, sem[2], sem[3], lax.rem(p, ZY) * 2 + c, p // ZY).start()
                return carry

            lax.fori_loop(1, n * ZY, second, 0)
            after()
            some = r.full.at[c, pl.ds(0, n * ZY - 1)]
            remote(some, some, sem[2], sem[3], s, m).wait()
            swap = remote(r.full.at[c], r.full.at[c], sem[4], sem[5], sib, m)
            swap.start()
            swap.wait()

            def place(k, carry):
                for cc in range(2):
                    rows = pl.ds(pl.multiple_of((k * 2 + cc) * RB, RB), RB)
                    for mm in range(n):
                        r.rows[rows, mm * DM : (mm + 1) * DM] = r.full[cc, mm * ZY + k]
                return carry

            lax.fori_loop(0, ZY, place, 0)

        def mlp_copies(buf, send, recv, i):
            i = i % buf.shape[0]
            return [
                remote(buf.at[i, m], buf.at[i, m], send.at[i, j - 1], recv.at[i, j - 1], s, lax.rem(m + j, n))
                for j in range(1, n)
            ]

        def mlp_start(which, i, value):
            buf = g["x" + which]
            buf[i % buf.shape[0], m] = value.astype(BF)
            for copy in mlp_copies(buf, g["x" + which + "_s"], g["x" + which + "_r"], i):
                copy.start()

        def mlp_total(which, i):
            buf = g["x" + which]
            for copy in mlp_copies(buf, g["x" + which + "_s"], g["x" + which + "_r"], i):
                copy.wait()
            i = i % buf.shape[0]
            total = buf[i, 0].astype(F32)
            for j in range(1, n):
                total = total + buf[i, j].astype(F32)
            return total

        def friend(j):
            return s - gi + lax.rem(gi + j, GN)

        def share(i, *refs):
            return [
                remote(ref.at[gi], ref.at[gi], r.sw_s.at[i + k, j - 1], r.sw_r.at[i + k, j - 1], friend(j), m)
                for k, ref in enumerate(refs)
                for j in range(1, GN)
            ]

        def attend_start(top, total, acc):
            top[...] = jnp.full(top.shape, NEG, F32)
            total[...] = jnp.zeros(total.shape, F32)
            acc[...] = jnp.zeros(acc.shape, F32)

        def head_groups(width):
            step = min(H, max(1, WIDE // width))
            return [range(at, min(at + step, H)) for at in range(0, H, step)]

        def attend(ci, query, key, value, mask, top, total, acc):
            kept = mask(ci)
            for group in head_groups(kept.shape[1]):
                scores = {h: nt(query(h), key(ci, h)) for h in group}
                weights = {}
                for h in group:
                    score = jnp.where(kept, scores[h], NEG)
                    old = top[h]
                    new = jnp.maximum(old, jnp.max(score, axis=-1, keepdims=True))
                    shrink = jnp.exp(old - new)
                    weight = jnp.exp(score - new)
                    total[h] = total[h] * shrink + jnp.sum(weight, axis=-1, keepdims=True)
                    acc[h] = acc[h] * shrink
                    top[h] = new
                    weights[h] = weight.astype(BF)
                for h in group:
                    acc[h] = acc[h] + nn(weights[h], value(ci, h))

        def finish(top, total, acc, mixed):
            for h in range(H):
                out = acc[h] / total[h]
                acc[h] = out
                mixed[:, h * HD : (h + 1) * HD] = out.astype(BF)
                top[h] = top[h] + jnp.log(total[h])

        def row_stats(grad, top, total, acc):
            lane = lax.broadcasted_iota(jnp.int32, (acc.shape[1], 128), 1)
            stats = jnp.zeros((acc.shape[1], 128), F32)
            for h in range(H):
                delta = jnp.sum(grad(h).astype(F32) * acc[h], axis=-1, keepdims=True)
                total[h] = delta
                stats = jnp.where(lane == h, top[h], jnp.where(lane == 8 + h, delta, stats))
            return jnp.transpose(stats)[0:16]

        def back_query(ci, query, grad, key, value, mask, log_total, delta, out):
            kept = mask(ci)
            for group in head_groups(kept.shape[1]):
                scores = {h: nt(query(h), key(ci, h)) for h in group}
                grad_probs = {h: nt(grad(h), value(ci, h)) for h in group}
                grad_scores = {}
                for h in group:
                    probs = jnp.where(kept, jnp.exp(scores[h] - log_total[h]), 0.0)
                    grad_scores[h] = (probs * (grad_probs[h] - delta[h])).astype(BF)
                for h in group:
                    out[h] = out[h] + nn(grad_scores[h], key(ci, h))

        def back_keys(ci, key, value, query, grad, mask, stat, out_key, out_value):
            kept = mask(ci)
            for group in head_groups(kept.shape[1]):
                scores = {h: nt(key(h), query(ci, h)) for h in group}
                grad_probs = {h: nt(value(h), grad(ci, h)) for h in group}
                probs, grad_scores = {}, {}
                for h in group:
                    prob = jnp.where(kept, jnp.exp(scores[h] - stat(ci, h)), 0.0)
                    grad_scores[h] = (prob * (grad_probs[h] - stat(ci, 8 + h))).astype(BF)
                    probs[h] = prob.astype(BF)
                for h in group:
                    out_value[h] = out_value[h] + nn(probs[h], grad(ci, h))
                    out_key[h] = out_key[h] + nn(grad_scores[h], query(ci, h))

        dq_d, dk_d, dv_d = (ref.at[:, 0:T] for ref in (r.dq, r.dk, r.dv))
        dq_r, dk_r, dv_r = (ref.at[:, 0:RH] for ref in (r.dq, r.dk, r.dv))

        def pack_grads(dq, dk, dv, out):
            for h in range(H):
                out[:, h * HD : (h + 1) * HD] = (dq[h] * SCALE).astype(BF)
                out[:, W + h * HD : W + (h + 1) * HD] = dk[h].astype(BF)
                out[:, 2 * W + h * HD : 2 * W + (h + 1) * HD] = dv[h].astype(BF)

        def front_back(grads, b):
            return (
                nt(grads[:, 0:W], r.wq[b, 0])
                + nt(grads[:, W : 2 * W], r.wq[b, 1])
                + nt(grads[:, 2 * W : 3 * W], r.wq[b, 2])
            )

        def loop(low, high, body):
            def step(i, carry):
                body(i)
                return carry

            lax.fori_loop(low, high, step, 0)

        def gather(buf, ss, rs, up, chain):
            sign = -1 if up else 1
            last = z if up else Z - 1 - z
            ahead = Z - 1 - z if up else z
            at_y, at_sib, at_level = Z - 1, Z + Y - 2, Z + Y - 1
            at_z = at_level + Y - 1
            at_far = at_z + (Z - 1) * Y

            def copy(slot, dst, k):
                return remote(buf.at[slot], buf.at[slot], ss.at[k], rs.at[slot], dst, m)

            def recv(slot):
                copy(slot, sib, 0).wait_recv()

            def side(dy):
                return lax.rem(y + dy, Y)

            def copies(each):
                if chain:
                    pl.when(ahead > 0)(lambda: each(copy(s, rank(z - sign, y, c), 0)))
                else:
                    loop(1, ahead + 1, lambda dz: each(copy(s, rank(z - sign * dz, y, c), dz - 1)))
                for dy in range(1, Y):
                    each(copy(s, rank(z, side(dy), c), at_y + dy - 1))
                each(copy(s, sib, at_sib))

            def level_copy(dy):
                return copy(rank(z, side(dy), c), sib, at_level + dy - 1)

            def z_copies(dz):
                slot = rank(z + sign * dz, y, c)
                k = at_z + (dz - 1) * Y
                outs = [copy(slot, rank(z, side(dy), c), k + dy - 1) for dy in range(1, Y)]
                return [*outs, copy(slot, sib, k + Y - 1)]

            def far_copy(dz, dy):
                return copy(rank(z + sign * dz, side(dy), c), sib, at_far + (dz - 1) * (Y - 1) + dy - 1)

            def start():
                copies(lambda one: one.start())

            def level():
                for dy in range(1, Y):
                    recv(rank(z, side(dy), c))
                    level_copy(dy).start()

            def level_end():
                for dy in range(Y):
                    recv(rank(z, side(dy), 1 - c))

            def onward(dz, each):
                if chain:
                    slot = rank(z + sign * dz, y, c)
                    pl.when(ahead > 0)(lambda: each(copy(slot, rank(z - sign, y, c), dz)))

            def z_step(dz):
                recv(rank(z + sign * dz, y, c))
                onward(dz, lambda one: one.start())
                for one in z_copies(dz):
                    one.start()

            def y_step(dz):
                for dy in range(1, Y):
                    recv(rank(z + sign * dz, side(dy), c))
                    far_copy(dz, dy).start()

            def sib_step(dz):
                for dy in range(Y):
                    recv(rank(z + sign * dz, side(dy), 1 - c))

            def end():
                copies(lambda one: one.wait_send())
                for dy in range(1, Y):
                    level_copy(dy).wait_send()

                def sent(dz):
                    onward(dz, lambda one: one.wait_send())
                    for one in z_copies(dz):
                        one.wait_send()
                    for dy in range(1, Y):
                        far_copy(dz, dy).wait_send()

                loop(1, last + 1, sent)

            return SimpleNamespace(
                start=start,
                level=level,
                level_end=level_end,
                z_step=z_step,
                y_step=y_step,
                sib_step=sib_step,
                end=end,
                last=last,
            )

        def walk(items, body):
            last = items[0].last

            def all_of(name, *args):
                for item in items:
                    getattr(item, name)(*args)

            pl.when(last > 0)(lambda: all_of("z_step", 1))
            all_of("level_end")
            body(0)

            def step(dz):
                all_of("y_step", dz)
                pl.when(dz < last)(lambda: all_of("z_step", dz + 1))
                all_of("sib_step", dz)
                body(dz)

            loop(1, last + 1, step)

        lev = lax.rem(s, LEVEL)

        def level_slot(dy, cc):
            return lax.rem(y + dy, Y) * 2 + cc

        def level_copy(k, side, j, src, slot, dst):
            i = KINDS.index(k)
            buf = g[("left_", "right_")[side] + k]
            return remote(src, buf.at[slot], r.gl_s.at[i, side, j], r.gl_r.at[i, side, slot], dst, m)

        def own_copies(k, side):
            mine = g[("left_", "right_")[side] + k].at[lev]
            out = [level_copy(k, side, 0, mine, lev, sib)]
            for dy in range(1, 1 if k in REDONE else Y):
                src = g["away_" + k].at[dy - 1] if side == 0 else mine
                out.append(level_copy(k, side, dy, src, lev, rank(z, lax.rem(y + dy, Y), c)))
            return out

        def far_copies(k):
            return [
                level_copy(k, side, Y + dy - 1, g[("left_", "right_")[side] + k].at[level_slot(dy, c)], level_slot(dy, c), sib)
                for side in range(2)
                for dy in range(1, Y)
            ]

        def level_wait(k, slot):
            for side in range(2):
                buf = g[("left_", "right_")[side] + k]
                level_copy(k, side, 0, buf.at[slot], slot, sib).wait_recv()

        def sum_left(k, lhs):
            g["left_" + k][lev] = nn(lhs[...], r.sele[y]).astype(BF)
            for dy in range(1, 1 if k in REDONE else Y):
                g["away_" + k][dy - 1] = nn(lhs[...], r.sele[lax.rem(y + dy, Y)]).astype(BF)
            for copy in own_copies(k, 0):
                copy.start()

        def sum_right(k):
            for copy in own_copies(k, 1):
                copy.start()

        def give(i, src):
            return [
                remote(
                    src, r.nbr.at[i, dy - 1], r.gn_s.at[i, dy - 1], r.gn_r.at[i, dy - 1], rank(z, lax.rem(y + dy, Y), c), m
                )
                for dy in range(1, Y)
            ]

        def redo_first():
            for dy in range(1, Y):
                give(0, r.cot)[dy - 1].wait_recv()
                for x, w in chunks(F):
                    r.dactn[dy - 1, :, x : x + w] = nt(r.nbr[0, dy - 1], r.wd[1, x : x + w, :])

        def redo():
            for dy in range(1, Y):
                give(1, r.n2d)[dy - 1].wait_recv()
                slot = level_slot(Y - dy, c)
                for x, w in chunks(F):
                    active, slope = gelu_pair(nn(r.nbr[1, dy - 1], r.wu[1, :, x : x + w]))
                    r.right_down[slot, :, x : x + w] = active.astype(BF)
                    r.right_up[slot, :, x : x + w] = (r.dactn[dy - 1, :, x : x + w] * slope).astype(BF)
                r.left_down[slot] = nn(r.nbr[0, dy - 1], r.sele[y]).astype(BF)
                r.left_up[slot] = nn(r.nbr[1, dy - 1], r.sele[y]).astype(BF)
            for k in REDONE:
                for copy in far_copies(k):
                    copy.start()

        def sum_far(k):
            if k in REDONE:
                if k == REDONE[0]:
                    redo()
                return
            for dy in range(1, Y):
                level_wait(k, level_slot(dy, c))
            for copy in far_copies(k):
                copy.start()

        def z_copy(k, dz):
            i = KINDS.index(k)
            return remote(
                g["zsend_" + k].at[lax.rem(z + dz, Z)],
                g["zrec_" + k].at[dz - 1],
                r.gz_s.at[i, dz - 1],
                r.gz_r.at[i, dz - 1],
                rank(lax.rem(z + dz, Z), y, c),
                m,
            )

        def sum_z(k):
            for dy in range(Y):
                level_wait(k, level_slot(dy, 1 - c))
            left = g["left_" + k][...].reshape(LEVEL * T, QY)
            left = jnp.where(c == 0, left[:, 0:ZD], left[:, ZD:QY])
            for x, w in chunks(XW[k]):
                total = tn(left, g["right_" + k][:, :, x : x + w].reshape(LEVEL * T, w)).reshape(Z, DRP, w)
                g["zsend_" + k][:, :, x : x + w] = total.astype(BF)
                own = total[0]
                for zz in range(1, Z):
                    own = jnp.where(z == zz, total[zz], own)
                g["zown_" + k][:, x : x + w] = own
            if k in FOLDED:
                fold_first(k, lambda one: one.start())
            else:
                for dz in range(1, Z):
                    z_copy(k, dz).start()

        edge = (z == 0) | (z == Z - 1)
        low_half = z < 2
        near = jnp.where(low_half, jnp.where(z == 0, 1, 0), jnp.where(z == 3, 2, 3))
        three = pl.ds(jnp.where(low_half, 1, 0), 3)

        def fold_first(k, then):
            i = KINDS.index(k)
            one = pl.ds(near, 1)
            for cond, blocks in ((edge, three), (jnp.logical_not(edge), one)):
                pl.when(cond)(
                    lambda blocks=blocks: then(
                        remote(
                            g["zsend_" + k].at[blocks],
                            g["zrec_" + k].at[blocks],
                            r.gz_s.at[i, 0],
                            r.gz_r.at[i, 0],
                            rank(near, y, c),
                            m,
                        )
                    )
                )

        def fold_copies(k):
            i = KINDS.index(k)
            far = (3 - z, jnp.where(low_half, 3, 0))
            return [
                remote(
                    g["zsend_" + k].at[b],
                    g["zfar_" + k],
                    r.gz_s.at[i, 1 + j],
                    r.gz_r.at[i, 1],
                    rank(b, y, c),
                    m,
                )
                for j, b in enumerate(far)
            ]

        def fold_recv(k, blocks):
            i = KINDS.index(k)
            some = g["zrec_" + k].at[blocks]
            remote(some, some, r.gz_s.at[i, 0], r.gz_r.at[i, 0], sib, m).wait_recv()

        def sum_mid(k):
            if k not in FOLDED:
                return

            def work():
                fold_recv(k, three)
                for b, copy in zip((3 - z, jnp.where(low_half, 3, 0)), fold_copies(k)):
                    t = g["zsend_" + k][b].astype(F32) + g["zrec_" + k][b].astype(F32)
                    g["zsend_" + k][b] = t.astype(BF)
                    copy.start()

            pl.when(jnp.logical_not(edge))(work)

        def fold_end(k):
            i = KINDS.index(k)
            pl.when(edge)(lambda: fold_recv(k, pl.ds(z, 1)))
            far = g["zfar_" + k]
            remote(far, far, r.gz_s.at[i, 1], r.gz_r.at[i, 1], sib, m).wait_recv()
            fold_first(k, lambda one: one.wait_send())

            def sent():
                for copy in fold_copies(k):
                    copy.wait_send()

            pl.when(jnp.logical_not(edge))(sent)
            t = g["zown_" + k][...] + g["zrec_" + k][z].astype(F32) + far[...].astype(F32)
            put(1, k, t)

        def put(b, k, value):
            if k == "qkv":
                for j in range(3):
                    r.qkv_o[b, j] = value[0:DR, j * W : (j + 1) * W]
            else:
                g[k + "_o"][b] = value[0:DR]

        def sum_end(k):
            if k in FOLDED:
                return fold_end(k)
            t = g["zown_" + k][...]
            for dz in range(1, Z):
                z_copy(k, dz).wait()
                t = t + g["zrec_" + k][dz - 1].astype(F32)
            put(1, k, t)

        def sum_sent(k):
            for side in range(2):
                for copy in own_copies(k, side):
                    copy.wait_send()
            for copy in far_copies(k):
                copy.wait_send()

        def routed_copy(k, j):
            i = 6 + KINDS.index(k)
            send, recv = r.sw_s.at[i, j - 1], r.sw_r.at[i, j - 1]
            return remote(g["rsend_" + k].at[j - 1], g["rrec_" + k].at[j - 1], send, recv, friend(j), m)

        def routed_start(k, lhs, rhs):
            col = lax.broadcasted_iota(jnp.int32, (D, DRP), 1)
            row = lax.broadcasted_iota(jnp.int32, (D, DRP), 0)

            def block(who):
                hit = (row - who * DR == col) & (col < DR)
                return nn(lhs, jnp.where(hit, 1.0, 0.0).astype(BF)).astype(BF)

            for j in range(1, GN):
                g["rsend_" + k][j - 1] = tn(block(friend(j)), rhs).astype(BF)
                routed_copy(k, j).start()
            g["rkeep_" + k][...] = tn(block(s), rhs)

        def routed_end(k):
            t = g["rkeep_" + k][...]
            for j in range(1, GN):
                routed_copy(k, j).wait()
                t = t + g["rrec_" + k][j - 1].astype(F32)
            put(0, k, t)

        def head(h):
            return slice(h * HD, (h + 1) * HD)

        pl.semaphore_wait(bar, S - 1 + (n - 1) * ZY)
        spread_start()
        r.sega[s] = jnp.broadcast_to(r.segr[...], (8, T))
        for load in loads:
            load.start()
        prow_f = prow.astype(F32)
        for i in range(GN // 2):
            r.posr[i] = jnp.broadcast_to(prow_f[:, i * 2 * RH : (i + 1) * 2 * RH], (8, 2 * RH))
        mine = r.posr[gi // 2][0:1]
        r.posc[...] = column(jnp.where(lax.rem(gi, 2) == 0, mine[:, 0:RH], mine[:, RH : 2 * RH]))
        r.segc[...] = column(r.segr[...])
        for yy in range(Y):
            ids = lax.broadcasted_iota(jnp.int32, (D, QY), 0)
            r.sele[yy] = jnp.where(ids == r.target[yy], 1.0, 0.0).astype(BF)
        spread_end(lambda: lax.fori_loop(1, S, send_segments, 0))
        some = pl.ds(0, S - 1)
        remote(r.sega.at[some], r.sega.at[some], r.seg_s.at[0], r.seg_s.at[1], s, m).wait()
        starts = [
            jnp.sum(
                jnp.sum(jnp.where(r.sega[...] < k, 0.125, 0.0), axis=0), axis=(0, 1), keepdims=True
            )
            for k in range(1, 5)
        ]
        for i in range(GN // 2):
            r.sgr[i] = sum(jnp.where(r.posr[i] >= at, 1.0, 0.0) for at in starts)
        r.sgc[...] = sum(jnp.where(r.posc[...] >= at, 1.0, 0.0) for at in starts)
        half = pl.ds(pl.multiple_of(gi * RH, RH), RH)

        loads[0].wait()
        r.chh[...] = r.rows[half, :]
        r.nr[...] = rms(r.chh[...].astype(F32), r.gains[0, 0:1]).astype(BF)
        for at in range(0, R, 256):
            part = slice(at, at + 256)
            normed = rms(r.rows[part].astype(F32), r.gains[0, 0:1]).astype(BF)
            r.qr[part] = (nn(normed, r.wq[0, 0]).astype(BF) * SCALE).astype(BF)
            r.kr[part] = nn(normed, r.wq[0, 1]).astype(BF)
            r.vr[part] = nn(normed, r.wq[0, 2]).astype(BF)

        def part_rows(ref):
            return lambda ci, h: ref[pl.ds(pl.multiple_of(ci * 2 * RH, RH), 2 * RH), head(h)]

        def half_rows(ref):
            return lambda h: ref[half, head(h)]

        def routed_mask(ci):
            return (r.sgr[ci][0:1] == r.sgc[...]) & (r.posr[ci][0:1] <= r.posc[...])

        def routed_mask_back(ci):
            return (r.sgr[ci][0:1] == r.sgc[...]) & (r.posc[...] <= r.posr[ci][0:1])

        def routed_pick(i):
            return lax.rem(gi // 2 + i, GN // 2)

        def routed_loop(body):
            if GN == 2:
                body(0)
            else:
                loop(0, GN // 2, lambda i: body(routed_pick(i)))

        attend_start(r.mr, r.lr, r.ar)
        routed_loop(
            lambda ci: attend(
                ci, half_rows(r.qr), part_rows(r.kr), part_rows(r.vr), routed_mask, r.mr, r.lr, r.ar
            )
        )
        finish(r.mr, r.lr, r.ar, r.mixr)
        loads[1].wait()
        mlp_start("r", 0, nn(r.mixr[...], r.wp[0]))
        for copy in give(0, r.cot):
            copy.start()
        sum_left("down", r.cot)
        loads[2].wait()
        loads[3].wait()
        attn = mlp_total("r", 0)
        r.attr[...] = attn
        normed = rms(r.chh[...].astype(F32) + attn, r.gains[0, 1:2]).astype(BF)
        r.n2r[...] = normed
        for x, w in chunks(F):
            pre = nn(normed, r.wu[0, :, x : x + w])
            r.prer[:, x : x + w] = pre
            r.actr[:, x : x + w] = gelu_pair(pre)[0].astype(BF)
        mlp_start("r", 1, nn(r.actr[...], r.wd[0]))
        for load in loads[4:]:
            load.wait()
        for x, w in chunks(F):
            r.dact[:, x : x + w] = nt(r.cot[...], r.wd[1, x : x + w, :])
        mlp = mlp_total("r", 1)
        r.chg[gi] = (r.attr[...] + mlp).astype(BF)
        swaps = share(0, r.chg)
        for copy in swaps:
            copy.start()
        inp = r.inp[...].astype(F32)
        gate = jax.nn.sigmoid(jnp.sum(inp * r.router[...].reshape(1, D), axis=-1, keepdims=True))
        for copy in swaps:
            copy.wait()

        sel = nn(r.oht[...], r.chg[...].reshape(R, D))
        r.sel[...] = sel.astype(BF)
        ro = inp + gate * sel
        r.ro[...] = ro
        r.ro_o[...] = ro.astype(BF)
        normed = rms(ro, r.gains[1, 0:1]).astype(BF)
        r.nd[...] = normed
        r.kall[s] = nn(normed, r.wq[1, 1]).astype(BF)
        r.vall[s] = nn(normed, r.wq[1, 2]).astype(BF)
        keys_all = gather(r.kall, r.k_s, r.k_r, True, KV_CHAIN)
        values_all = gather(r.vall, r.v_s, r.v_r, True, KV_CHAIN)
        keys_all.start()
        values_all.start()
        r.qa[s] = (nn(normed, r.wq[1, 0]).astype(BF) * SCALE).astype(BF)
        query_all = gather(r.qa, r.q_s, r.q_r, False, False)
        query_all.start()
        keys_all.level()
        values_all.level()
        query_all.level()

        def level_rows(ref, first=0):
            def get(ci, h):
                return ref[pl.ds(ci * LEVEL, LEVEL), :, head(first + h)].reshape(CH, HD)

            return get

        def level_line(ref, line):
            return lambda ci: jnp.concatenate([ref[ci * LEVEL + j][line : line + 1] for j in range(LEVEL)], axis=1)

        own_pos = lax.broadcasted_iota(jnp.int32, (T, CH), 0) + s * T
        far_pos = lax.broadcasted_iota(jnp.int32, (T, CH), 1)
        seg_line = level_line(r.sega, 0)

        def dense_mask(ci):
            return (seg_line(ci).astype(F32) == r.segc[...]) & (far_pos + ci * CH <= own_pos)

        def dense_mask_back(ci):
            return (seg_line(ci).astype(F32) == r.segc[...]) & (own_pos <= far_pos + ci * CH)

        attend_start(r.md, r.ld, r.ad)
        walk(
            [keys_all, values_all],
            lambda dz: attend(
                z - dz,
                lambda h: r.qa[s, :, head(h)],
                level_rows(r.kall),
                level_rows(r.vall),
                dense_mask,
                r.md,
                r.ld,
                r.ad,
            ),
        )
        finish(r.md, r.ld, r.ad, r.right_proj.at[lev])
        mlp_start("d", 0, nn(r.right_proj[lev], r.wp[1]))
        loop(1, query_all.last + 1, query_all.z_step)
        sum_left("qkv", r.nd)
        redo_first()
        attn = mlp_total("d", 0)
        hid = r.ro[...] + attn
        r.hid[...] = hid
        normed = rms(hid, r.gains[1, 1:2]).astype(BF)
        r.n2d[...] = normed
        for copy in give(1, r.n2d):
            copy.start()
        for x, w in chunks(F):
            active, slope = gelu_pair(nn(normed, r.wu[1, :, x : x + w]))
            r.right_down[lev, :, x : x + w] = active.astype(BF)
            r.right_up[lev, :, x : x + w] = (r.dact[:, x : x + w] * slope).astype(BF)
        sum_right("down")
        mlp_start("d", 1, nt(r.right_up[lev], r.wu[1]))
        mlp_start("d", 2, nn(r.right_down[lev], r.wd[1]))

        sum_left("up", r.n2d)
        loop(1, query_all.last + 1, query_all.y_step)
        dn, dg = rms_back(mlp_total("d", 1), r.hid[...], r.gains[1, 1:2])
        r.small[1:2] = dg
        dhid = r.cot[...].astype(F32) + dn
        r.dro[...] = dhid
        r.dattn[...] = dhid.astype(BF)
        r.da[s] = nt(r.dattn[...], r.wp[1]).astype(BF)
        r.sta[s] = row_stats(lambda h: r.da[s, :, head(h)], r.md, r.ld, r.ad)
        grad_all = gather(r.da, r.da_s, r.da_r, False, DO_CHAIN)
        stat_all = gather(r.sta, r.st_s, r.st_r, False, DO_CHAIN)
        for item in (grad_all, stat_all):
            item.start()
        for item in (grad_all, stat_all):
            item.level()
        sum_right("up")
        query_all.level_end()
        loop(1, query_all.last + 1, query_all.sib_step)
        dq_d[...] = jnp.zeros((H, T, HD), F32)
        dk_d[...] = jnp.zeros((H, T, HD), F32)
        dv_d[...] = jnp.zeros((H, T, HD), F32)
        loop(
            0,
            z + 1,
            lambda dz: back_query(
                z - dz,
                lambda h: r.qa[s, :, head(h)],
                lambda h: r.da[s, :, head(h)],
                level_rows(r.kall),
                level_rows(r.vall),
                dense_mask,
                r.md,
                r.ld,
                dq_d,
            ),
        )
        sum_far("down")
        sum_far("up")
        walk(
            [grad_all, stat_all],
            lambda dz: back_keys(
                z + dz,
                lambda h: r.kall[s, :, head(h)],
                lambda h: r.vall[s, :, head(h)],
                level_rows(r.qa),
                level_rows(r.da),
                dense_mask_back,
                lambda ci, line: level_line(r.sta, line)(ci),
                dk_d,
                dv_d,
            ),
        )
        sum_z("down")
        pack_grads(dq_d, dk_d, dv_d, r.right_qkv.at[lev])
        mlp_start("d", 3, front_back(r.right_qkv.at[lev], 1))
        sum_left("proj", r.dattn)
        sum_right("qkv")
        sum_right("proj")
        dn, dg = rms_back(mlp_total("d", 3), r.ro[...], r.gains[1, 0:1])
        r.small[0:1] = dg
        dro = r.dro[...] + dn
        r.dro[...] = dro

        sel = r.sel[...].astype(F32)
        inp = r.inp[...].astype(F32)
        gate = jax.nn.sigmoid(jnp.sum(inp * r.router[...].reshape(1, D), axis=-1, keepdims=True))
        dlogit = jnp.sum(dro * sel, axis=-1, keepdims=True) * gate * (1.0 - gate)
        scatter_rows((gate * dro).astype(BF))
        spread_start()
        r.small[2:3] = jnp.sum(inp * dlogit, axis=0, keepdims=True)

        def in_wait():
            pass
            sum_mid("down")
            sum_z("up")

        spread_end(in_wait)
        sum_far("qkv")
        sum_far("proj")

        dmlp = r.rows[half, :]
        r.attr[...] = r.attr[...] + r.chh[...].astype(F32)
        for x, w in chunks(F):
            grad_active = nt(dmlp, r.wd[0, x : x + w, :])
            r.dprer[:, x : x + w] = (grad_active * gelu_pair(r.prer[:, x : x + w])[1]).astype(BF)
        mlp_start("r", 2, nt(r.dprer[...], r.wu[0]))
        routed_start("down", dmlp, r.actr[...])
        routed_start("up", r.n2r[...], r.dprer[...])
        r.small[3:8] = jnp.zeros((5, D), F32)
        r.sblk[...] = jnp.zeros((S, 8, 128), F32)
        for p in range(S):
            r.sblk[p, :, 0:DR] = r.small[:, p * DR : (p + 1) * DR]

        def send_small(i, carry):
            p = lax.rem(s + i, S)
            remote(r.sblk.at[p], r.srec.at[s], r.sm_s.at[0], r.sm_s.at[1], p, m).start()
            return carry

        lax.fori_loop(1, S, send_small, 0)
        r.srec[s] = r.sblk[s]
        dn, dg2 = rms_back(mlp_total("r", 2), r.attr[...], r.gains[0, 1:2])
        r.attr[...] = dn
        r.dattr[...] = (dmlp.astype(F32) + dn).astype(BF)
        r.dor[gi] = nt(r.dattr[...], r.wp[0]).astype(BF)
        r.str[gi] = row_stats(lambda h: r.dor[gi, :, head(h)], r.mr, r.lr, r.ar)
        swaps = share(1, r.dor, r.str)
        for copy in swaps:
            copy.start()
        routed_start("proj", r.dattr[...], r.mixr[...])
        sum_mid("up")
        sum_z("qkv")
        sum_z("proj")
        dq_r[...] = jnp.zeros((H, RH, HD), F32)
        dk_r[...] = jnp.zeros((H, RH, HD), F32)
        dv_r[...] = jnp.zeros((H, RH, HD), F32)
        routed_loop(
            lambda ci: back_query(
                ci,
                half_rows(r.qr),
                lambda h: r.dor[gi, :, head(h)],
                part_rows(r.kr),
                part_rows(r.vr),
                routed_mask,
                r.mr,
                r.lr,
                dq_r,
            )
        )
        for copy in swaps:
            copy.wait()
        routed_loop(
            lambda ci: back_keys(
                ci,
                half_rows(r.kr),
                half_rows(r.vr),
                part_rows(r.qr),
                lambda ci, h: r.dor[pl.ds(ci * 2, 2), :, head(h)].reshape(2 * RH, HD),
                routed_mask_back,
                lambda ci, line: jnp.concatenate([r.str[ci * 2 + j][line : line + 1] for j in range(2)], axis=1),
                dk_r,
                dv_r,
            )
        )
        pack_grads(dq_r, dk_r, dv_r, r.g3r)
        mlp_start("r", 3, front_back(r.g3r, 0))
        routed_start("qkv", r.nr[...], r.g3r[...])
        sum_end("down")
        sum_mid("qkv")
        sum_mid("proj")
        dn, dg1 = rms_back(mlp_total("r", 3), r.chh[...].astype(F32), r.gains[0, 0:1])
        r.chg[gi] = (r.attr[...] + dn).astype(BF)
        r.gr[gi] = jnp.concatenate([dg1, dg2, jnp.zeros((6, D), F32)], axis=0)
        swaps = share(3, r.chg, r.gr)
        for copy in swaps:
            copy.start()
        for copy in swaps:
            copy.wait()
        r.rg_o[...] = jnp.sum(r.gr[...], axis=0)[0:2]
        back = nn(r.oht[...], r.chg[...].reshape(R, D))
        inp = r.inp[...].astype(F32)
        gate = jax.nn.sigmoid(jnp.sum(inp * r.router[...].reshape(1, D), axis=-1, keepdims=True))
        dlogit = jnp.sum(r.dro[...] * r.sel[...].astype(F32), axis=-1, keepdims=True) * gate * (1.0 - gate)
        r.gi_o[...] = r.dro[...] + back + dlogit * r.router[...].reshape(1, D)

        r.do_o[...] = (r.hid[...] + mlp_total("d", 2)).astype(BF)
        some = pl.ds(0, S - 1)
        remote(r.sblk.at[some], r.srec.at[some], r.sm_s.at[0], r.sm_s.at[1], s, m).wait()
        r.sm_o[...] = jnp.sum(r.srec[...], axis=0)
        for k in KINDS:
            routed_end(k)
        sum_end("up")
        sum_end("qkv")
        sum_end("proj")
        for item in (keys_all, values_all, query_all, grad_all, stat_all):
            item.end()
        for k in KINDS:
            sum_sent(k)
        for i, src in enumerate((r.cot, r.n2d)):
            for copy in give(i, src):
                copy.wait_send()

    def layout(*refs):
        into, out, held, made, sems = refs[:9], refs[9:18], refs[18:27], refs[27:29], refs[29]
        order = (3, 4, 0, 1, 2, 5, 6, 7, 8)
        reads = {i: pltpu.make_async_copy(into[i], held[i], sems.at[0, i]) for i in order}
        for i in order:
            reads[i].start()
        made = {3: made[0], 4: made[1]}
        writes = {i: pltpu.make_async_copy(made.get(i, held[i]), out[i], sems.at[1, i]) for i in order}
        s = lax.axis_index("seq")
        reads[3].wait()
        reads[4].wait()
        sm, rg = held[3], held[4]
        for i in order[2:]:
            reads[i].wait()
            writes[i].start()
        routed = rg[:, 0:DR]
        for p in range(1, S):
            routed = jnp.where(s == p, rg[:, p * DR : (p + 1) * DR], routed)
        made[3][0] = routed
        made[3][1] = sm[0:2, 0:DR]
        made[4][...] = sm[2:3, 0:DR]
        writes[3].start()
        writes[4].start()
        for i in order:
            writes[i].wait()

    def run(inp, segments, picks, gains, router, qkv, proj, up, down, cot):
        args = (
            inp,
            segments.reshape(1, T),
            picks,
            gains,
            router,
            cot,
            jnp.asarray(target),
            qkv,
            proj,
            up,
            down,
        )
        vmem = pl.BlockSpec(memory_space=pltpu.VMEM)
        hbm = pl.BlockSpec(memory_space=pl.ANY)
        res = pl.pallas_call(
            kernel,
            out_shape=[jax.ShapeDtypeStruct(sh, dt) for sh, dt in outs.values()],
            in_specs=[vmem] * 7 + [hbm] * 4,
            out_specs=[vmem] * len(outs),
            scratch_shapes=[pltpu.VMEM(sh, dt) for sh, dt in vm.values()] + [DMA(sh) for sh in sems.values()],
            compiler_params=pltpu.CompilerParams(
                collective_id=0, has_side_effects=True, vmem_limit_bytes=62 * 1024 * 1024
            ),
            name="train_step",
        )(*args)
        shapes = [
            ((T, D), BF),
            ((T, D), BF),
            ((T, D), F32),
            ((2, 2, DR), F32),
            ((1, DR), F32),
            ((2, 3, DR, W), F32),
            ((2, DR, W), F32),
            ((2, DR, F), F32),
            ((2, DR, F), F32),
        ]
        last = pl.pallas_call(
            layout,
            out_shape=[jax.ShapeDtypeStruct(sh, dt) for sh, dt in shapes],
            in_specs=[hbm] * 9,
            out_specs=[hbm] * 9,
            scratch_shapes=[pltpu.VMEM(x.shape, x.dtype) for x in res]
            + [pltpu.VMEM(*shapes[i]) for i in (3, 4)]
            + [DMA((2, 9))],
            compiler_params=pltpu.CompilerParams(vmem_limit_bytes=62 * 1024 * 1024),
            name="layout",
        )(*res)
        ro, do, gi, gains_grad, router_grad, gq, gp, gu, gd = last
        gp, gd = jnp.swapaxes(gp, 1, 2), jnp.swapaxes(gd, 1, 2)
        return (ro, do, gi, gains_grad, router_grad.reshape(DR), gq, gp, gu, gd)

    return run


def solution(mesh):
    S, n = mesh.shape["seq"], mesh.shape["mlp"]

    def body(inp, segments, picks, gains, router, qkv, proj, up, down, cot):
        run = build(
            S, n, inp.shape[0], inp.shape[1], qkv.shape[-1], up.shape[-1], picks.size, picks.shape[0]
        )
        return run(inp, segments, picks, gains, router, qkv, proj, up, down, cot)

    return jax.shard_map(
        body,
        mesh=mesh,
        in_specs=(
            P("seq", None),
            P("seq"),
            P(),
            P(),
            P(),
            P(None, None, None, "mlp"),
            P(None, "mlp", None),
            P(None, None, "mlp"),
            P(None, "mlp", None),
            P("seq", None),
        ),
        out_specs=(
            P("seq", None),
            P("seq", None),
            P("seq", None),
            P(None, None, "seq"),
            P("seq"),
            P(None, None, "seq", "mlp"),
            P(None, "mlp", "seq"),
            P(None, "seq", "mlp"),
            P(None, "mlp", "seq"),
        ),
        check_vma=False,
    )
```

```python
from types import SimpleNamespace

import jax
import jax.numpy as jnp
import numpy as np
from jax import lax
from jax.experimental import pallas as pl
from jax.experimental.pallas import tpu as pltpu
from jax.sharding import PartitionSpec as P

HD = 64
G = 2048
EPS = 1e-05
NEG = -1e30
SCALE = HD**-0.5
BF = jnp.bfloat16
F32 = jnp.float32
MESH = pl.DeviceIdType.MESH
DMA = pltpu.SemaphoreType.DMA
GELU_A = 0.044715
GELU_B = float(np.sqrt(2.0 / np.pi))
WIDE = 1536
KV_CHAIN = True
DO_CHAIN = False
REDONE = ("down", "up")
KINDS = ("down", "up", "proj", "qkv")


def dot(left, right, dims):
    return lax.dot_general(left, right, (dims, ((), ())), preferred_element_type=F32)


def nn(left, right):
    return dot(left, right, ((1,), (0,)))


def nt(left, right):
    return dot(left, right, ((1,), (1,)))


def tn(left, right):
    return dot(left, right, ((0,), (0,)))


def inverse_rms(x):
    return lax.rsqrt(jnp.mean(x * x, axis=-1, keepdims=True) + EPS)


def rms(x, gain):
    return x * inverse_rms(x) * gain


def rms_back(dy, x, gain):
    r = inverse_rms(x)
    gy = gain * dy
    dx = r * gy - x * (r * r * r) * jnp.mean(gy * x, axis=-1, keepdims=True)
    return dx, jnp.sum(dy * x * r, axis=0, keepdims=True)


def gelu_pair(x):
    t = jnp.tanh(GELU_B * (x + GELU_A * x * x * x))
    half = 0.5 * (1.0 + t)
    slope = half + 0.5 * x * (1.0 - t * t) * (GELU_B * (1.0 + 3.0 * GELU_A * x * x))
    return x * half, slope


def column(row):
    wide = jnp.broadcast_to(row.astype(F32), (128, row.shape[1]))
    return jnp.transpose(wide)[:, 0:1]


def chunks(extent):
    width = 768 if extent % 768 == 0 else 384 if extent % 384 == 0 else extent
    return [(at, width) for at in range(0, extent, width)]


def build(S, n, T, D, W, F, R, groups):
    rest = S // 2
    Y = 2 ** ((rest.bit_length() - 1) // 2)
    Z = rest // Y
    ZY = Z * Y
    H = W // HD
    LEVEL = 2 * Y
    CH = LEVEL * T
    GN = R // T
    RH = R // GN
    RB = R // S
    DM = D // n
    DR = D // S
    DRP = -(-DR // 16) * 16
    ZD = Z * DRP
    QY = 2 * ZD
    FOLDED = KINDS if Z == 4 else ()
    XW = {"down": F, "up": F, "proj": W, "qkv": 3 * W}

    target = np.full((Y, 1, QY), -1, np.int32)
    for yy in range(Y):
        for core in range(2):
            for zz in range(Z):
                for j in range(DR):
                    target[yy, 0, (core * Z + zz) * DRP + j] = ((zz * Y + yy) * 2 + core) * DR + j

    ins = ["inp", "segr", "picks", "gains", "router", "cot", "target", "qkv_h", "proj_h", "up_h", "down_h"]
    outs = {
        "ro_o": ((T, D), BF),
        "do_o": ((T, D), BF),
        "gi_o": ((T, D), F32),
        "sm_o": ((8, 128), F32),
        "rg_o": ((2, D), F32),
        "qkv_o": ((2, 3, DR, W), F32),
        "proj_o": ((2, DR, W), F32),
        "up_o": ((2, DR, F), F32),
        "down_o": ((2, DR, F), F32),
    }
    vm = {
        "wq": ((2, 3, D, W), BF),
        "wp": ((2, W, D), BF),
        "wu": ((2, D, F), BF),
        "wd": ((2, F, D), BF),
        "sega": ((S, 8, T), jnp.int32),
        "segc": ((T, 1), F32),
        "oht": ((T, R), BF),
        "oh": ((R, T), BF),
        "posr": ((GN // 2, 8, 2 * RH), F32),
        "posc": ((RH, 1), F32),
        "sgr": ((GN // 2, 8, 2 * RH), F32),
        "sgc": ((RH, 1), F32),
        "part": ((S, RB, DM), BF),
        "r1": ((S, RB, DM), BF),
        "full": ((2, n * ZY, RB, DM), BF),
        "rows": ((R, D), BF),
        "nr": ((RH, D), BF),
        "chh": ((RH, D), BF),
        "qr": ((R, W), BF),
        "kr": ((R, W), BF),
        "vr": ((R, W), BF),
        "mr": ((H, RH, 1), F32),
        "lr": ((H, RH, 1), F32),
        "ar": ((H, RH, HD), F32),
        "mixr": ((RH, W), BF),
        "attr": ((RH, D), F32),
        "n2r": ((RH, D), BF),
        "prer": ((RH, F), F32),
        "actr": ((RH, F), BF),
        "xr": ((2, n, RH, D), BF),
        "xd": ((3, n, T, D), BF),
        "chg": ((GN, RH, D), BF),
        "sel": ((T, D), BF),
        "ro": ((T, D), F32),
        "nd": ((T, D), BF),
        "kall": ((S, T, W), BF),
        "vall": ((S, T, W), BF),
        "qa": ((S, T, W), BF),
        "da": ((S, T, W), BF),
        "sta": ((S, 16, T), F32),
        "md": ((H, T, 1), F32),
        "ld": ((H, T, 1), F32),
        "ad": ((H, T, HD), F32),
        "hid": ((T, D), F32),
        "n2d": ((T, D), BF),
        "dact": ((T, F), F32),
        "nbr": ((2, Y - 1, T, D), BF),
        "dactn": ((Y - 1, T, F), F32),
        "dattn": ((T, D), BF),
        "dq": ((H, max(T, RH), HD), F32),
        "dk": ((H, max(T, RH), HD), F32),
        "dv": ((H, max(T, RH), HD), F32),
        "dro": ((T, D), F32),
        "small": ((8, D), F32),
        "sblk": ((S, 8, 128), F32),
        "srec": ((S, 8, 128), F32),
        "dor": ((GN, RH, W), BF),
        "str": ((GN, 16, RH), F32),
        "dprer": ((RH, F), BF),
        "dattr": ((RH, D), BF),
        "g3r": ((RH, 3 * W), BF),
        "gr": ((GN, 8, D), F32),
        "sele": ((Y, D, QY), BF),
    }
    for k in KINDS:
        X = XW[k]
        vm["left_" + k] = ((LEVEL, T, QY), BF)
        if k not in REDONE:
            vm["away_" + k] = ((Y - 1, T, QY), BF)
        vm["right_" + k] = ((LEVEL, T, X), BF)
        vm["zsend_" + k] = ((Z, DRP, X), BF)
        vm["zown_" + k] = ((DRP, X), F32)
        vm["zrec_" + k] = ((Z, DRP, X), BF)
        vm["zfar_" + k] = ((DRP, X), BF)
        vm["rsend_" + k] = ((GN - 1, DRP, X), BF)
        vm["rkeep_" + k] = ((DRP, X), F32)
        vm["rrec_" + k] = ((GN - 1, DRP, X), BF)
    n_sends = (Z - 1) + (Y - 1) + 1 + (Z - 1) * Y + Z * (Y - 1)
    sems = {
        "w_s": (8,),
        "seg_s": (2,),
        "t_s": (6,),
        "xr_s": (2, n - 1),
        "xr_r": (2, n - 1),
        "xd_s": (3, n - 1),
        "xd_r": (3, n - 1),
        "sw_s": (10, GN - 1),
        "sw_r": (10, GN - 1),
        "k_s": (n_sends,),
        "k_r": (S,),
        "v_s": (n_sends,),
        "v_r": (S,),
        "q_s": (n_sends,),
        "q_r": (S,),
        "da_s": (n_sends,),
        "da_r": (S,),
        "st_s": (n_sends,),
        "st_r": (S,),
        "sm_s": (2,),
        "gn_s": (2, Y - 1),
        "gn_r": (2, Y - 1),
        "gl_s": (4, 2, 2 * Y - 1),
        "gl_r": (4, 2, LEVEL),
        "gz_s": (4, Z - 1),
        "gz_r": (4, Z - 1),
    }
    names = ins + list(outs) + list(vm) + list(sems)

    def kernel(*refs):
        r = SimpleNamespace(**dict(zip(names, refs, strict=True)))
        g = r.__dict__
        s = lax.axis_index("seq")
        m = lax.axis_index("mlp")
        c = lax.rem(s, 2)
        chip = s // 2
        y = lax.rem(chip, Y)
        z = chip // Y
        sib = s + 1 - 2 * c
        gi = lax.rem(s, GN)

        def rank(zz, yy, cc):
            return (zz * Y + yy) * 2 + cc

        def remote(src, dst, send, recv, seq, mlp):
            return pltpu.make_async_remote_copy(
                src_ref=src, dst_ref=dst, send_sem=send, recv_sem=recv, device_id=(seq, mlp), device_id_type=MESH
            )

        bar = pltpu.get_barrier_semaphore()

        def greet(i, carry):
            pl.semaphore_signal(bar, inc=1, device_id=(lax.rem(s + i, S), m), device_id_type=MESH)
            return carry

        lax.fori_loop(1, S, greet, 0)
        for j in range(1, n):

            def greet_other(i, carry, j=j):
                pl.semaphore_signal(bar, inc=1, device_id=(i * 2 + c, lax.rem(m + j, n)), device_id_type=MESH)
                return carry

            lax.fori_loop(0, ZY, greet_other, 0)
        loads = [
            pltpu.make_async_copy(src.at[b], dst.at[b], r.w_s.at[4 * b + i])
            for b in range(2)
            for i, (src, dst) in enumerate(
                ((r.qkv_h, r.wq), (r.proj_h, r.wp), (r.up_h, r.wu), (r.down_h, r.wd))
            )
        ]
        prow = jnp.concatenate([r.picks[i : i + 1, :] + G * i for i in range(groups)], axis=1)
        here = s * T + lax.broadcasted_iota(jnp.int32, (T, R), 0)
        hot = jnp.where(prow == here, 1.0, 0.0)
        r.oht[...] = hot.astype(BF)
        r.oh[...] = jnp.transpose(hot).astype(BF)

        def my_columns(x):
            got = x[:, 0:DM]
            for j in range(1, n):
                got = jnp.where(m == j, x[:, j * DM : (j + 1) * DM], got)
            return got

        def scatter_rows(x):
            r.part[...] = nn(r.oh[...], my_columns(x)).astype(BF).reshape(S, RB, DM)

        scatter_rows(r.inp[...])
        def send_segments(i, carry):
            remote(r.sega.at[s], r.sega.at[s], r.seg_s.at[0], r.seg_s.at[1], lax.rem(s + i, S), m).start()
            return carry

        sem = [r.t_s.at[j] for j in range(6)]

        def spread_start():
            def first(k, carry):
                p = lax.rem(s + k, S)
                remote(r.part.at[p], r.r1.at[s], sem[0], sem[1], p, m).start()
                return carry

            lax.fori_loop(1, S, first, 0)
            r.r1[s] = r.part[s]

        def spread_end(after):
            some = pl.ds(0, S - 1)
            remote(r.part.at[some], r.r1.at[some], sem[0], sem[1], s, m).wait()
            me = m * ZY + chip
            r.full[c, me] = jnp.sum(r.r1[...].astype(F32), axis=0).astype(BF)

            def second(k, carry):
                p = lax.rem(me + k, n * ZY)
                block = r.full.at[c, me]
                remote(block, block, sem[2], sem[3], lax.rem(p, ZY) * 2 + c, p // ZY).start()
                return carry

            lax.fori_loop(1, n * ZY, second, 0)
            after()
            some = r.full.at[c, pl.ds(0, n * ZY - 1)]
            remote(some, some, sem[2], sem[3], s, m).wait()
            swap = remote(r.full.at[c], r.full.at[c], sem[4], sem[5], sib, m)
            swap.start()
            swap.wait()

            def place(k, carry):
                for cc in range(2):
                    rows = pl.ds(pl.multiple_of((k * 2 + cc) * RB, RB), RB)
                    for mm in range(n):
                        r.rows[rows, mm * DM : (mm + 1) * DM] = r.full[cc, mm * ZY + k]
                return carry

            lax.fori_loop(0, ZY, place, 0)

        def mlp_copies(buf, send, recv, i):
            i = i % buf.shape[0]
            return [
                remote(buf.at[i, m], buf.at[i, m], send.at[i, j - 1], recv.at[i, j - 1], s, lax.rem(m + j, n))
                for j in range(1, n)
            ]

        def mlp_start(which, i, value):
            buf = g["x" + which]
            buf[i % buf.shape[0], m] = value.astype(BF)
            for copy in mlp_copies(buf, g["x" + which + "_s"], g["x" + which + "_r"], i):
                copy.start()

        def mlp_total(which, i):
            buf = g["x" + which]
            for copy in mlp_copies(buf, g["x" + which + "_s"], g["x" + which + "_r"], i):
                copy.wait()
            i = i % buf.shape[0]
            total = buf[i, 0].astype(F32)
            for j in range(1, n):
                total = total + buf[i, j].astype(F32)
            return total

        def friend(j):
            return s - gi + lax.rem(gi + j, GN)

        def share(i, *refs):
            return [
                remote(ref.at[gi], ref.at[gi], r.sw_s.at[i + k, j - 1], r.sw_r.at[i + k, j - 1], friend(j), m)
                for k, ref in enumerate(refs)
                for j in range(1, GN)
            ]

        def attend_start(top, total, acc):
            top[...] = jnp.full(top.shape, NEG, F32)
            total[...] = jnp.zeros(total.shape, F32)
            acc[...] = jnp.zeros(acc.shape, F32)

        def head_groups(width):
            step = min(H, max(1, (2 * WIDE if CH <= 512 else WIDE) // width))
            return [range(at, min(at + step, H)) for at in range(0, H, step)]

        def attend(ci, query, key, value, mask, top, total, acc):
            kept = mask(ci)
            for group in head_groups(kept.shape[1]):
                scores = {h: nt(query(h), key(ci, h)) for h in group}
                weights = {}
                for h in group:
                    score = jnp.where(kept, scores[h], NEG)
                    old = top[h]
                    new = jnp.maximum(old, jnp.max(score, axis=-1, keepdims=True))
                    shrink = jnp.exp(old - new)
                    weight = jnp.exp(score - new)
                    total[h] = total[h] * shrink + jnp.sum(weight, axis=-1, keepdims=True)
                    acc[h] = acc[h] * shrink
                    top[h] = new
                    weights[h] = weight.astype(BF)
                for h in group:
                    acc[h] = acc[h] + nn(weights[h], value(ci, h))

        def finish(top, total, acc, mixed):
            for h in range(H):
                out = acc[h] / total[h]
                acc[h] = out
                mixed[:, h * HD : (h + 1) * HD] = out.astype(BF)
                top[h] = top[h] + jnp.log(total[h])

        def row_stats(grad, top, total, acc):
            lane = lax.broadcasted_iota(jnp.int32, (acc.shape[1], 128), 1)
            stats = jnp.zeros((acc.shape[1], 128), F32)
            for h in range(H):
                delta = jnp.sum(grad(h).astype(F32) * acc[h], axis=-1, keepdims=True)
                total[h] = delta
                stats = jnp.where(lane == h, top[h], jnp.where(lane == 8 + h, delta, stats))
            return jnp.transpose(stats)[0:16]

        def back_query(ci, query, grad, key, value, mask, log_total, delta, out):
            kept = mask(ci)
            for group in head_groups(kept.shape[1]):
                scores = {h: nt(query(h), key(ci, h)) for h in group}
                grad_probs = {h: nt(grad(h), value(ci, h)) for h in group}
                grad_scores = {}
                for h in group:
                    probs = jnp.where(kept, jnp.exp(scores[h] - log_total[h]), 0.0)
                    grad_scores[h] = (probs * (grad_probs[h] - delta[h])).astype(BF)
                for h in group:
                    out[h] = out[h] + nn(grad_scores[h], key(ci, h))

        def back_keys(ci, key, value, query, grad, mask, stat, out_key, out_value):
            kept = mask(ci)
            for group in head_groups(kept.shape[1]):
                scores = {h: nt(key(h), query(ci, h)) for h in group}
                grad_probs = {h: nt(value(h), grad(ci, h)) for h in group}
                probs, grad_scores = {}, {}
                for h in group:
                    prob = jnp.where(kept, jnp.exp(scores[h] - stat(ci, h)), 0.0)
                    grad_scores[h] = (prob * (grad_probs[h] - stat(ci, 8 + h))).astype(BF)
                    probs[h] = prob.astype(BF)
                for h in group:
                    out_value[h] = out_value[h] + nn(probs[h], grad(ci, h))
                    out_key[h] = out_key[h] + nn(grad_scores[h], query(ci, h))

        dq_d, dk_d, dv_d = (ref.at[:, 0:T] for ref in (r.dq, r.dk, r.dv))
        dq_r, dk_r, dv_r = (ref.at[:, 0:RH] for ref in (r.dq, r.dk, r.dv))

        def pack_grads(dq, dk, dv, out):
            for h in range(H):
                out[:, h * HD : (h + 1) * HD] = (dq[h] * SCALE).astype(BF)
                out[:, W + h * HD : W + (h + 1) * HD] = dk[h].astype(BF)
                out[:, 2 * W + h * HD : 2 * W + (h + 1) * HD] = dv[h].astype(BF)

        def front_back(grads, b):
            return (
                nt(grads[:, 0:W], r.wq[b, 0])
                + nt(grads[:, W : 2 * W], r.wq[b, 1])
                + nt(grads[:, 2 * W : 3 * W], r.wq[b, 2])
            )

        def loop(low, high, body):
            def step(i, carry):
                body(i)
                return carry

            lax.fori_loop(low, high, step, 0)

        def gather(buf, ss, rs, up, chain):
            sign = -1 if up else 1
            last = z if up else Z - 1 - z
            ahead = Z - 1 - z if up else z
            at_y, at_sib, at_level = Z - 1, Z + Y - 2, Z + Y - 1
            at_z = at_level + Y - 1
            at_far = at_z + (Z - 1) * Y

            def copy(slot, dst, k):
                return remote(buf.at[slot], buf.at[slot], ss.at[k], rs.at[slot], dst, m)

            def recv(slot):
                copy(slot, sib, 0).wait_recv()

            def side(dy):
                return lax.rem(y + dy, Y)

            def copies(each):
                if chain:
                    pl.when(ahead > 0)(lambda: each(copy(s, rank(z - sign, y, c), 0)))
                else:
                    loop(1, ahead + 1, lambda dz: each(copy(s, rank(z - sign * dz, y, c), dz - 1)))
                for dy in range(1, Y):
                    each(copy(s, rank(z, side(dy), c), at_y + dy - 1))
                each(copy(s, sib, at_sib))

            def level_copy(dy):
                return copy(rank(z, side(dy), c), sib, at_level + dy - 1)

            def z_copies(dz):
                slot = rank(z + sign * dz, y, c)
                k = at_z + (dz - 1) * Y
                outs = [copy(slot, rank(z, side(dy), c), k + dy - 1) for dy in range(1, Y)]
                return [*outs, copy(slot, sib, k + Y - 1)]

            def far_copy(dz, dy):
                return copy(rank(z + sign * dz, side(dy), c), sib, at_far + (dz - 1) * (Y - 1) + dy - 1)

            def start():
                copies(lambda one: one.start())

            def level():
                for dy in range(1, Y):
                    recv(rank(z, side(dy), c))
                    level_copy(dy).start()

            def level_end():
                for dy in range(Y):
                    recv(rank(z, side(dy), 1 - c))

            def onward(dz, each):
                if chain:
                    slot = rank(z + sign * dz, y, c)
                    pl.when(ahead > 0)(lambda: each(copy(slot, rank(z - sign, y, c), dz)))

            def z_step(dz):
                recv(rank(z + sign * dz, y, c))
                onward(dz, lambda one: one.start())
                for one in z_copies(dz):
                    one.start()

            def y_step(dz):
                for dy in range(1, Y):
                    recv(rank(z + sign * dz, side(dy), c))
                    far_copy(dz, dy).start()

            def sib_step(dz):
                for dy in range(Y):
                    recv(rank(z + sign * dz, side(dy), 1 - c))

            def end():
                copies(lambda one: one.wait_send())
                for dy in range(1, Y):
                    level_copy(dy).wait_send()

                def sent(dz):
                    onward(dz, lambda one: one.wait_send())
                    for one in z_copies(dz):
                        one.wait_send()
                    for dy in range(1, Y):
                        far_copy(dz, dy).wait_send()

                loop(1, last + 1, sent)

            return SimpleNamespace(
                start=start,
                level=level,
                level_end=level_end,
                z_step=z_step,
                y_step=y_step,
                sib_step=sib_step,
                end=end,
                last=last,
            )

        def walk(items, body):
            last = items[0].last

            def all_of(name, *args):
                for item in items:
                    getattr(item, name)(*args)

            pl.when(last > 0)(lambda: all_of("z_step", 1))
            all_of("level_end")
            body(0)

            def step(dz):
                all_of("y_step", dz)
                pl.when(dz < last)(lambda: all_of("z_step", dz + 1))
                all_of("sib_step", dz)
                body(dz)

            loop(1, last + 1, step)

        lev = lax.rem(s, LEVEL)

        def level_slot(dy, cc):
            return lax.rem(y + dy, Y) * 2 + cc

        def level_copy(k, side, j, src, slot, dst):
            i = KINDS.index(k)
            buf = g[("left_", "right_")[side] + k]
            return remote(src, buf.at[slot], r.gl_s.at[i, side, j], r.gl_r.at[i, side, slot], dst, m)

        def own_copies(k, side):
            mine = g[("left_", "right_")[side] + k].at[lev]
            out = [level_copy(k, side, 0, mine, lev, sib)]
            for dy in range(1, 1 if k in REDONE else Y):
                src = g["away_" + k].at[dy - 1] if side == 0 else mine
                out.append(level_copy(k, side, dy, src, lev, rank(z, lax.rem(y + dy, Y), c)))
            return out

        def far_copies(k):
            return [
                level_copy(k, side, Y + dy - 1, g[("left_", "right_")[side] + k].at[level_slot(dy, c)], level_slot(dy, c), sib)
                for side in range(2)
                for dy in range(1, Y)
            ]

        def level_wait(k, slot):
            for side in range(2):
                buf = g[("left_", "right_")[side] + k]
                level_copy(k, side, 0, buf.at[slot], slot, sib).wait_recv()

        def sum_left(k, lhs):
            g["left_" + k][lev] = nn(lhs[...], r.sele[y]).astype(BF)
            for dy in range(1, 1 if k in REDONE else Y):
                g["away_" + k][dy - 1] = nn(lhs[...], r.sele[lax.rem(y + dy, Y)]).astype(BF)
            for copy in own_copies(k, 0):
                copy.start()

        def sum_right(k):
            for copy in own_copies(k, 1):
                copy.start()

        def give(i, src):
            return [
                remote(
                    src, r.nbr.at[i, dy - 1], r.gn_s.at[i, dy - 1], r.gn_r.at[i, dy - 1], rank(z, lax.rem(y + dy, Y), c), m
                )
                for dy in range(1, Y)
            ]

        def redo_first():
            for dy in range(1, Y):
                give(0, r.cot)[dy - 1].wait_recv()
                for x, w in chunks(F):
                    r.dactn[dy - 1, :, x : x + w] = nt(r.nbr[0, dy - 1], r.wd[1, x : x + w, :])

        def redo():
            for dy in range(1, Y):
                give(1, r.n2d)[dy - 1].wait_recv()
                slot = level_slot(Y - dy, c)
                for x, w in chunks(F):
                    active, slope = gelu_pair(nn(r.nbr[1, dy - 1], r.wu[1, :, x : x + w]))
                    r.right_down[slot, :, x : x + w] = active.astype(BF)
                    r.right_up[slot, :, x : x + w] = (r.dactn[dy - 1, :, x : x + w] * slope).astype(BF)
                r.left_down[slot] = nn(r.nbr[0, dy - 1], r.sele[y]).astype(BF)
                r.left_up[slot] = nn(r.nbr[1, dy - 1], r.sele[y]).astype(BF)
            for k in REDONE:
                for copy in far_copies(k):
                    copy.start()

        def sum_far(k):
            if k in REDONE:
                if k == REDONE[0]:
                    redo()
                return
            for dy in range(1, Y):
                level_wait(k, level_slot(dy, c))
            for copy in far_copies(k):
                copy.start()

        def z_copy(k, dz):
            i = KINDS.index(k)
            return remote(
                g["zsend_" + k].at[lax.rem(z + dz, Z)],
                g["zrec_" + k].at[dz - 1],
                r.gz_s.at[i, dz - 1],
                r.gz_r.at[i, dz - 1],
                rank(lax.rem(z + dz, Z), y, c),
                m,
            )

        def sum_z(k):
            for dy in range(Y):
                level_wait(k, level_slot(dy, 1 - c))
            left = g["left_" + k][...].reshape(LEVEL * T, QY)
            left = jnp.where(c == 0, left[:, 0:ZD], left[:, ZD:QY])
            for x, w in chunks(XW[k]):
                total = tn(left, g["right_" + k][:, :, x : x + w].reshape(LEVEL * T, w)).reshape(Z, DRP, w)
                g["zsend_" + k][:, :, x : x + w] = total.astype(BF)
                own = total[0]
                for zz in range(1, Z):
                    own = jnp.where(z == zz, total[zz], own)
                g["zown_" + k][:, x : x + w] = own
            if k in FOLDED:
                fold_first(k, lambda one: one.start())
            else:
                for dz in range(1, Z):
                    z_copy(k, dz).start()

        edge = (z == 0) | (z == Z - 1)
        low_half = z < 2
        near = jnp.where(low_half, jnp.where(z == 0, 1, 0), jnp.where(z == 3, 2, 3))
        three = pl.ds(jnp.where(low_half, 1, 0), 3)

        def fold_first(k, then):
            i = KINDS.index(k)
            one = pl.ds(near, 1)
            for cond, blocks in ((edge, three), (jnp.logical_not(edge), one)):
                pl.when(cond)(
                    lambda blocks=blocks: then(
                        remote(
                            g["zsend_" + k].at[blocks],
                            g["zrec_" + k].at[blocks],
                            r.gz_s.at[i, 0],
                            r.gz_r.at[i, 0],
                            rank(near, y, c),
                            m,
                        )
                    )
                )

        def fold_copies(k):
            i = KINDS.index(k)
            far = (3 - z, jnp.where(low_half, 3, 0))
            return [
                remote(
                    g["zsend_" + k].at[b],
                    g["zfar_" + k],
                    r.gz_s.at[i, 1 + j],
                    r.gz_r.at[i, 1],
                    rank(b, y, c),
                    m,
                )
                for j, b in enumerate(far)
            ]

        def fold_recv(k, blocks):
            i = KINDS.index(k)
            some = g["zrec_" + k].at[blocks]
            remote(some, some, r.gz_s.at[i, 0], r.gz_r.at[i, 0], sib, m).wait_recv()

        def sum_mid(k):
            if k not in FOLDED:
                return

            def work():
                fold_recv(k, three)
                for b, copy in zip((3 - z, jnp.where(low_half, 3, 0)), fold_copies(k)):
                    t = g["zsend_" + k][b].astype(F32) + g["zrec_" + k][b].astype(F32)
                    g["zsend_" + k][b] = t.astype(BF)
                    copy.start()

            pl.when(jnp.logical_not(edge))(work)

        def fold_end(k):
            i = KINDS.index(k)
            pl.when(edge)(lambda: fold_recv(k, pl.ds(z, 1)))
            far = g["zfar_" + k]
            remote(far, far, r.gz_s.at[i, 1], r.gz_r.at[i, 1], sib, m).wait_recv()
            fold_first(k, lambda one: one.wait_send())

            def sent():
                for copy in fold_copies(k):
                    copy.wait_send()

            pl.when(jnp.logical_not(edge))(sent)
            t = g["zown_" + k][...] + g["zrec_" + k][z].astype(F32) + far[...].astype(F32)
            put(1, k, t)

        def put(b, k, value):
            if k == "qkv":
                for j in range(3):
                    r.qkv_o[b, j] = value[0:DR, j * W : (j + 1) * W]
            else:
                g[k + "_o"][b] = value[0:DR]

        def sum_end(k):
            if k in FOLDED:
                return fold_end(k)
            t = g["zown_" + k][...]
            for dz in range(1, Z):
                z_copy(k, dz).wait()
                t = t + g["zrec_" + k][dz - 1].astype(F32)
            put(1, k, t)

        def sum_sent(k):
            for side in range(2):
                for copy in own_copies(k, side):
                    copy.wait_send()
            for copy in far_copies(k):
                copy.wait_send()

        def routed_copy(k, j):
            i = 6 + KINDS.index(k)
            send, recv = r.sw_s.at[i, j - 1], r.sw_r.at[i, j - 1]
            return remote(g["rsend_" + k].at[j - 1], g["rrec_" + k].at[j - 1], send, recv, friend(j), m)

        def routed_start(k, lhs, rhs):
            col = lax.broadcasted_iota(jnp.int32, (D, DRP), 1)
            row = lax.broadcasted_iota(jnp.int32, (D, DRP), 0)

            def block(who):
                hit = (row - who * DR == col) & (col < DR)
                return nn(lhs, jnp.where(hit, 1.0, 0.0).astype(BF)).astype(BF)

            for j in range(1, GN):
                g["rsend_" + k][j - 1] = tn(block(friend(j)), rhs).astype(BF)
                routed_copy(k, j).start()
            g["rkeep_" + k][...] = tn(block(s), rhs)

        def routed_end(k):
            t = g["rkeep_" + k][...]
            for j in range(1, GN):
                routed_copy(k, j).wait()
                t = t + g["rrec_" + k][j - 1].astype(F32)
            put(0, k, t)

        def head(h):
            return slice(h * HD, (h + 1) * HD)

        pl.semaphore_wait(bar, S - 1 + (n - 1) * ZY)
        spread_start()
        r.sega[s] = jnp.broadcast_to(r.segr[...], (8, T))
        for load in loads:
            load.start()
        prow_f = prow.astype(F32)
        for i in range(GN // 2):
            r.posr[i] = jnp.broadcast_to(prow_f[:, i * 2 * RH : (i + 1) * 2 * RH], (8, 2 * RH))
        mine = r.posr[gi // 2][0:1]
        r.posc[...] = column(jnp.where(lax.rem(gi, 2) == 0, mine[:, 0:RH], mine[:, RH : 2 * RH]))
        r.segc[...] = column(r.segr[...])
        for yy in range(Y):
            ids = lax.broadcasted_iota(jnp.int32, (D, QY), 0)
            r.sele[yy] = jnp.where(ids == r.target[yy], 1.0, 0.0).astype(BF)
        spread_end(lambda: lax.fori_loop(1, S, send_segments, 0))
        some = pl.ds(0, S - 1)
        remote(r.sega.at[some], r.sega.at[some], r.seg_s.at[0], r.seg_s.at[1], s, m).wait()
        starts = [
            jnp.sum(
                jnp.sum(jnp.where(r.sega[...] < k, 0.125, 0.0), axis=0), axis=(0, 1), keepdims=True
            )
            for k in range(1, 5)
        ]
        for i in range(GN // 2):
            r.sgr[i] = sum(jnp.where(r.posr[i] >= at, 1.0, 0.0) for at in starts)
        r.sgc[...] = sum(jnp.where(r.posc[...] >= at, 1.0, 0.0) for at in starts)
        half = pl.ds(pl.multiple_of(gi * RH, RH), RH)

        loads[0].wait()
        r.chh[...] = r.rows[half, :]
        r.nr[...] = rms(r.chh[...].astype(F32), r.gains[0, 0:1]).astype(BF)
        for at in range(0, R, 256):
            part = slice(at, at + 256)
            normed = rms(r.rows[part].astype(F32), r.gains[0, 0:1]).astype(BF)
            r.qr[part] = (nn(normed, r.wq[0, 0]).astype(BF) * SCALE).astype(BF)
            r.kr[part] = nn(normed, r.wq[0, 1]).astype(BF)
            r.vr[part] = nn(normed, r.wq[0, 2]).astype(BF)

        def part_rows(ref):
            return lambda ci, h: ref[pl.ds(pl.multiple_of(ci * 2 * RH, RH), 2 * RH), head(h)]

        def half_rows(ref):
            return lambda h: ref[half, head(h)]

        def routed_mask(ci):
            return (r.sgr[ci][0:1] == r.sgc[...]) & (r.posr[ci][0:1] <= r.posc[...])

        def routed_mask_back(ci):
            return (r.sgr[ci][0:1] == r.sgc[...]) & (r.posc[...] <= r.posr[ci][0:1])

        def routed_pick(i):
            return lax.rem(gi // 2 + i, GN // 2)

        def routed_loop(body):
            if GN == 2:
                body(0)
            else:
                loop(0, GN // 2, lambda i: body(routed_pick(i)))

        attend_start(r.mr, r.lr, r.ar)
        routed_loop(
            lambda ci: attend(
                ci, half_rows(r.qr), part_rows(r.kr), part_rows(r.vr), routed_mask, r.mr, r.lr, r.ar
            )
        )
        finish(r.mr, r.lr, r.ar, r.mixr)
        loads[1].wait()
        mlp_start("r", 0, nn(r.mixr[...], r.wp[0]))
        for copy in give(0, r.cot):
            copy.start()
        sum_left("down", r.cot)
        loads[2].wait()
        loads[3].wait()
        attn = mlp_total("r", 0)
        r.attr[...] = attn
        normed = rms(r.chh[...].astype(F32) + attn, r.gains[0, 1:2]).astype(BF)
        r.n2r[...] = normed
        for x, w in chunks(F):
            pre = nn(normed, r.wu[0, :, x : x + w])
            r.prer[:, x : x + w] = pre
            r.actr[:, x : x + w] = gelu_pair(pre)[0].astype(BF)
        mlp_start("r", 1, nn(r.actr[...], r.wd[0]))
        for load in loads[4:]:
            load.wait()
        for x, w in chunks(F):
            r.dact[:, x : x + w] = nt(r.cot[...], r.wd[1, x : x + w, :])
        mlp = mlp_total("r", 1)
        r.chg[gi] = (r.attr[...] + mlp).astype(BF)
        swaps = share(0, r.chg)
        for copy in swaps:
            copy.start()
        inp = r.inp[...].astype(F32)
        gate = jax.nn.sigmoid(jnp.sum(inp * r.router[...].reshape(1, D), axis=-1, keepdims=True))
        for copy in swaps:
            copy.wait()

        sel = nn(r.oht[...], r.chg[...].reshape(R, D))
        r.sel[...] = sel.astype(BF)
        ro = inp + gate * sel
        r.ro[...] = ro
        r.ro_o[...] = ro.astype(BF)
        normed = rms(ro, r.gains[1, 0:1]).astype(BF)
        r.nd[...] = normed
        r.kall[s] = nn(normed, r.wq[1, 1]).astype(BF)
        r.vall[s] = nn(normed, r.wq[1, 2]).astype(BF)
        keys_all = gather(r.kall, r.k_s, r.k_r, True, KV_CHAIN)
        values_all = gather(r.vall, r.v_s, r.v_r, True, KV_CHAIN)
        keys_all.start()
        values_all.start()
        r.qa[s] = (nn(normed, r.wq[1, 0]).astype(BF) * SCALE).astype(BF)
        query_all = gather(r.qa, r.q_s, r.q_r, False, False)
        query_all.start()
        keys_all.level()
        values_all.level()
        query_all.level()

        def level_rows(ref, first=0):
            def get(ci, h):
                return ref[pl.ds(ci * LEVEL, LEVEL), :, head(first + h)].reshape(CH, HD)

            return get

        def level_line(ref, line):
            return lambda ci: jnp.concatenate([ref[ci * LEVEL + j][line : line + 1] for j in range(LEVEL)], axis=1)

        own_pos = lax.broadcasted_iota(jnp.int32, (T, CH), 0) + s * T
        far_pos = lax.broadcasted_iota(jnp.int32, (T, CH), 1)
        seg_line = level_line(r.sega, 0)

        def dense_mask(ci):
            return (seg_line(ci).astype(F32) == r.segc[...]) & (far_pos + ci * CH <= own_pos)

        def dense_mask_back(ci):
            return (seg_line(ci).astype(F32) == r.segc[...]) & (own_pos <= far_pos + ci * CH)

        attend_start(r.md, r.ld, r.ad)
        walk(
            [keys_all, values_all],
            lambda dz: attend(
                z - dz,
                lambda h: r.qa[s, :, head(h)],
                level_rows(r.kall),
                level_rows(r.vall),
                dense_mask,
                r.md,
                r.ld,
                r.ad,
            ),
        )
        finish(r.md, r.ld, r.ad, r.right_proj.at[lev])
        mlp_start("d", 0, nn(r.right_proj[lev], r.wp[1]))
        loop(1, query_all.last + 1, query_all.z_step)
        sum_left("qkv", r.nd)
        redo_first()
        attn = mlp_total("d", 0)
        hid = r.ro[...] + attn
        r.hid[...] = hid
        normed = rms(hid, r.gains[1, 1:2]).astype(BF)
        r.n2d[...] = normed
        for copy in give(1, r.n2d):
            copy.start()
        for x, w in chunks(F):
            active, slope = gelu_pair(nn(normed, r.wu[1, :, x : x + w]))
            r.right_down[lev, :, x : x + w] = active.astype(BF)
            r.right_up[lev, :, x : x + w] = (r.dact[:, x : x + w] * slope).astype(BF)
        sum_right("down")
        mlp_start("d", 1, nt(r.right_up[lev], r.wu[1]))
        mlp_start("d", 2, nn(r.right_down[lev], r.wd[1]))

        sum_left("up", r.n2d)
        loop(1, query_all.last + 1, query_all.y_step)
        dn, dg = rms_back(mlp_total("d", 1), r.hid[...], r.gains[1, 1:2])
        r.small[1:2] = dg
        dhid = r.cot[...].astype(F32) + dn
        r.dro[...] = dhid
        r.dattn[...] = dhid.astype(BF)
        r.da[s] = nt(r.dattn[...], r.wp[1]).astype(BF)
        r.sta[s] = row_stats(lambda h: r.da[s, :, head(h)], r.md, r.ld, r.ad)
        grad_all = gather(r.da, r.da_s, r.da_r, False, DO_CHAIN)
        stat_all = gather(r.sta, r.st_s, r.st_r, False, DO_CHAIN)
        for item in (grad_all, stat_all):
            item.start()
        for item in (grad_all, stat_all):
            item.level()
        sum_right("up")
        query_all.level_end()
        loop(1, query_all.last + 1, query_all.sib_step)
        dq_d[...] = jnp.zeros((H, T, HD), F32)
        dk_d[...] = jnp.zeros((H, T, HD), F32)
        dv_d[...] = jnp.zeros((H, T, HD), F32)
        loop(
            0,
            z + 1,
            lambda dz: back_query(
                z - dz,
                lambda h: r.qa[s, :, head(h)],
                lambda h: r.da[s, :, head(h)],
                level_rows(r.kall),
                level_rows(r.vall),
                dense_mask,
                r.md,
                r.ld,
                dq_d,
            ),
        )
        sum_far("down")
        sum_far("up")
        walk(
            [grad_all, stat_all],
            lambda dz: back_keys(
                z + dz,
                lambda h: r.kall[s, :, head(h)],
                lambda h: r.vall[s, :, head(h)],
                level_rows(r.qa),
                level_rows(r.da),
                dense_mask_back,
                lambda ci, line: level_line(r.sta, line)(ci),
                dk_d,
                dv_d,
            ),
        )
        sum_z("down")
        pack_grads(dq_d, dk_d, dv_d, r.right_qkv.at[lev])
        mlp_start("d", 3, front_back(r.right_qkv.at[lev], 1))
        sum_left("proj", r.dattn)
        sum_right("qkv")
        sum_right("proj")
        dn, dg = rms_back(mlp_total("d", 3), r.ro[...], r.gains[1, 0:1])
        r.small[0:1] = dg
        dro = r.dro[...] + dn
        r.dro[...] = dro

        sel = r.sel[...].astype(F32)
        inp = r.inp[...].astype(F32)
        gate = jax.nn.sigmoid(jnp.sum(inp * r.router[...].reshape(1, D), axis=-1, keepdims=True))
        dlogit = jnp.sum(dro * sel, axis=-1, keepdims=True) * gate * (1.0 - gate)
        scatter_rows((gate * dro).astype(BF))
        spread_start()
        r.small[2:3] = jnp.sum(inp * dlogit, axis=0, keepdims=True)

        def in_wait():
            pass
            sum_mid("down")
            sum_z("up")

        spread_end(in_wait)
        sum_far("qkv")
        sum_far("proj")

        dmlp = r.rows[half, :]
        r.attr[...] = r.attr[...] + r.chh[...].astype(F32)
        for x, w in chunks(F):
            grad_active = nt(dmlp, r.wd[0, x : x + w, :])
            r.dprer[:, x : x + w] = (grad_active * gelu_pair(r.prer[:, x : x + w])[1]).astype(BF)
        mlp_start("r", 2, nt(r.dprer[...], r.wu[0]))
        routed_start("down", dmlp, r.actr[...])
        routed_start("up", r.n2r[...], r.dprer[...])
        r.small[3:8] = jnp.zeros((5, D), F32)
        r.sblk[...] = jnp.zeros((S, 8, 128), F32)
        for p in range(S):
            r.sblk[p, :, 0:DR] = r.small[:, p * DR : (p + 1) * DR]

        def send_small(i, carry):
            p = lax.rem(s + i, S)
            remote(r.sblk.at[p], r.srec.at[s], r.sm_s.at[0], r.sm_s.at[1], p, m).start()
            return carry

        lax.fori_loop(1, S, send_small, 0)
        r.srec[s] = r.sblk[s]
        dn, dg2 = rms_back(mlp_total("r", 2), r.attr[...], r.gains[0, 1:2])
        r.attr[...] = dn
        r.dattr[...] = (dmlp.astype(F32) + dn).astype(BF)
        r.dor[gi] = nt(r.dattr[...], r.wp[0]).astype(BF)
        r.str[gi] = row_stats(lambda h: r.dor[gi, :, head(h)], r.mr, r.lr, r.ar)
        swaps = share(1, r.dor, r.str)
        for copy in swaps:
            copy.start()
        routed_start("proj", r.dattr[...], r.mixr[...])
        sum_mid("up")
        sum_z("qkv")
        sum_z("proj")
        dq_r[...] = jnp.zeros((H, RH, HD), F32)
        dk_r[...] = jnp.zeros((H, RH, HD), F32)
        dv_r[...] = jnp.zeros((H, RH, HD), F32)
        routed_loop(
            lambda ci: back_query(
                ci,
                half_rows(r.qr),
                lambda h: r.dor[gi, :, head(h)],
                part_rows(r.kr),
                part_rows(r.vr),
                routed_mask,
                r.mr,
                r.lr,
                dq_r,
            )
        )
        for copy in swaps:
            copy.wait()
        routed_loop(
            lambda ci: back_keys(
                ci,
                half_rows(r.kr),
                half_rows(r.vr),
                part_rows(r.qr),
                lambda ci, h: r.dor[pl.ds(ci * 2, 2), :, head(h)].reshape(2 * RH, HD),
                routed_mask_back,
                lambda ci, line: jnp.concatenate([r.str[ci * 2 + j][line : line + 1] for j in range(2)], axis=1),
                dk_r,
                dv_r,
            )
        )
        pack_grads(dq_r, dk_r, dv_r, r.g3r)
        mlp_start("r", 3, front_back(r.g3r, 0))
        routed_start("qkv", r.nr[...], r.g3r[...])
        sum_end("down")
        sum_mid("qkv")
        sum_mid("proj")
        dn, dg1 = rms_back(mlp_total("r", 3), r.chh[...].astype(F32), r.gains[0, 0:1])
        r.chg[gi] = (r.attr[...] + dn).astype(BF)
        r.gr[gi] = jnp.concatenate([dg1, dg2, jnp.zeros((6, D), F32)], axis=0)
        swaps = share(3, r.chg, r.gr)
        for copy in swaps:
            copy.start()
        for copy in swaps:
            copy.wait()
        r.rg_o[...] = jnp.sum(r.gr[...], axis=0)[0:2]
        back = nn(r.oht[...], r.chg[...].reshape(R, D))
        inp = r.inp[...].astype(F32)
        gate = jax.nn.sigmoid(jnp.sum(inp * r.router[...].reshape(1, D), axis=-1, keepdims=True))
        dlogit = jnp.sum(r.dro[...] * r.sel[...].astype(F32), axis=-1, keepdims=True) * gate * (1.0 - gate)
        r.gi_o[...] = r.dro[...] + back + dlogit * r.router[...].reshape(1, D)

        r.do_o[...] = (r.hid[...] + mlp_total("d", 2)).astype(BF)
        some = pl.ds(0, S - 1)
        remote(r.sblk.at[some], r.srec.at[some], r.sm_s.at[0], r.sm_s.at[1], s, m).wait()
        r.sm_o[...] = jnp.sum(r.srec[...], axis=0)
        for k in KINDS:
            routed_end(k)
        sum_end("up")
        sum_end("qkv")
        sum_end("proj")
        for item in (keys_all, values_all, query_all, grad_all, stat_all):
            item.end()
        for k in KINDS:
            sum_sent(k)
        for i, src in enumerate((r.cot, r.n2d)):
            for copy in give(i, src):
                copy.wait_send()

    def layout(*refs):
        into, out, held, made, sems = refs[:9], refs[9:18], refs[18:27], refs[27:29], refs[29]
        order = (3, 4, 0, 1, 2, 5, 6, 7, 8)
        reads = {i: pltpu.make_async_copy(into[i], held[i], sems.at[0, i]) for i in order}
        for i in order:
            reads[i].start()
        made = {3: made[0], 4: made[1]}
        writes = {i: pltpu.make_async_copy(made.get(i, held[i]), out[i], sems.at[1, i]) for i in order}
        s = lax.axis_index("seq")
        reads[3].wait()
        reads[4].wait()
        sm, rg = held[3], held[4]
        for i in order[2:]:
            reads[i].wait()
            writes[i].start()
        routed = rg[:, 0:DR]
        for p in range(1, S):
            routed = jnp.where(s == p, rg[:, p * DR : (p + 1) * DR], routed)
        made[3][0] = routed
        made[3][1] = sm[0:2, 0:DR]
        made[4][...] = sm[2:3, 0:DR]
        writes[3].start()
        writes[4].start()
        for i in order:
            writes[i].wait()

    def run(inp, segments, picks, gains, router, qkv, proj, up, down, cot):
        args = (
            inp,
            segments.reshape(1, T),
            picks,
            gains,
            router,
            cot,
            jnp.asarray(target),
            qkv,
            proj,
            up,
            down,
        )
        vmem = pl.BlockSpec(memory_space=pltpu.VMEM)
        hbm = pl.BlockSpec(memory_space=pl.ANY)
        res = pl.pallas_call(
            kernel,
            out_shape=[jax.ShapeDtypeStruct(sh, dt) for sh, dt in outs.values()],
            in_specs=[vmem] * 7 + [hbm] * 4,
            out_specs=[vmem] * len(outs),
            scratch_shapes=[pltpu.VMEM(sh, dt) for sh, dt in vm.values()] + [DMA(sh) for sh in sems.values()],
            compiler_params=pltpu.CompilerParams(
                collective_id=0, has_side_effects=True, vmem_limit_bytes=62 * 1024 * 1024
            ),
            name="train_step",
        )(*args)
        shapes = [
            ((T, D), BF),
            ((T, D), BF),
            ((T, D), F32),
            ((2, 2, DR), F32),
            ((1, DR), F32),
            ((2, 3, DR, W), F32),
            ((2, DR, W), F32),
            ((2, DR, F), F32),
            ((2, DR, F), F32),
        ]
        last = pl.pallas_call(
            layout,
            out_shape=[jax.ShapeDtypeStruct(sh, dt) for sh, dt in shapes],
            in_specs=[hbm] * 9,
            out_specs=[hbm] * 9,
            scratch_shapes=[pltpu.VMEM(x.shape, x.dtype) for x in res]
            + [pltpu.VMEM(*shapes[i]) for i in (3, 4)]
            + [DMA((2, 9))],
            compiler_params=pltpu.CompilerParams(vmem_limit_bytes=62 * 1024 * 1024),
            name="layout",
        )(*res)
        ro, do, gi, gains_grad, router_grad, gq, gp, gu, gd = last
        gp, gd = jnp.swapaxes(gp, 1, 2), jnp.swapaxes(gd, 1, 2)
        return (ro, do, gi, gains_grad, router_grad.reshape(DR), gq, gp, gu, gd)

    return run


def solution(mesh):
    S, n = mesh.shape["seq"], mesh.shape["mlp"]

    def body(inp, segments, picks, gains, router, qkv, proj, up, down, cot):
        run = build(
            S, n, inp.shape[0], inp.shape[1], qkv.shape[-1], up.shape[-1], picks.size, picks.shape[0]
        )
        return run(inp, segments, picks, gains, router, qkv, proj, up, down, cot)

    return jax.shard_map(
        body,
        mesh=mesh,
        in_specs=(
            P("seq", None),
            P("seq"),
            P(),
            P(),
            P(),
            P(None, None, None, "mlp"),
            P(None, "mlp", None),
            P(None, None, "mlp"),
            P(None, "mlp", None),
            P("seq", None),
        ),
        out_specs=(
            P("seq", None),
            P("seq", None),
            P("seq", None),
            P(None, None, "seq"),
            P("seq"),
            P(None, None, "seq", "mlp"),
            P(None, "mlp", "seq"),
            P(None, "seq", "mlp"),
            P(None, "mlp", "seq"),
        ),
        check_vma=False,
    )
```
